32 devices in a mesh: seq: 8 (over y, x, core), tp: 4 (over z).
Axes of the slice: x: 2, y: 2, z: 4, core: 2. Of those that a mesh axis runs over, the one named last changes fastest.
Arguments:
- tokens: bfloat16 [4096, 5376], P(('seq', 'tp')), may hold values from -180 to 180
- in_gain: float32 [5376], replicated, may hold values from 0.5 to 1.5
- raw_queries: bfloat16 [4096, 2048], P('seq', 'tp'), may hold values from -6 to 6
- w_key: bfloat16 [5376, 1024], P(None, 'tp'), may hold values from -0.078125 to 0.078125
- w_value: bfloat16 [5376, 1024], P(None, 'tp'), may hold values from -0.078125 to 0.078125
- q_gain: float32 [128], replicated, may hold values from 0.5 to 1.5
- k_gain: float32 [128], replicated, may hold values from 0.5 to 1.5
- doc_lengths: int32 [4], replicated, may hold values from 1 to 2048, as said below
- out_grad: bfloat16 [4096, 2048], P('seq', 'tp'), may hold values from -60 to 60
Outputs:
- grad_x: bfloat16 [4096, 5376], P(('seq', 'tp'))
- grad_queries: bfloat16 [4096, 2048], P('seq', 'tp')
- grad_wk: float32 [5376, 1024], P('seq', 'tp')
- grad_wv: float32 [5376, 1024], P('seq', 'tp')
The draws below stay inside these ranges and needn't reach their ends.
Inputs may be any that keep to these rules, and one draw needn't show every extreme that they name: `doc_lengths`: the 4 lengths sum to 4096; the last rollout is the longest, exactly 2048 tokens.
All inputs are finite; a program needn't handle non-finite values.
Results may differ from the reference program's by a relative error of at most 0.014.
Values may be sent and summed in bfloat16 or wider, within the bound.
No kernel may reach another device: no remote copies, remote signals or barrier semaphores. Data moves between devices by JAX's collectives and lax.ppermute only.
A program may use at most 128 MiB of HBM per device.

```python
import math
import jax
import jax.numpy as jnp
from jax import lax

D = 5376
HD = 128
QH = 16
KVH = 8
WINDOW = 1024
TOK_DEV = 512
TOKENS = 4096
NDOCS = 4
MAXDOC = 2048
N_TP = 4


def draw_tokens(key, part):
    key_base, key_rows, key_cols = jax.random.split(key, 3)
    row_scale = jnp.exp(jax.random.uniform(key_rows, (TOKENS, 1), jnp.float32, 0.0, math.log(10.0)))
    col_scale = jnp.exp(jax.random.uniform(key_cols, (1, D), jnp.float32, math.log(0.3), math.log(3.0)))
    base = jnp.clip(jax.random.normal(key_base, (TOKENS, D), jnp.float32), -6.0, 6.0)
    return (base * row_scale * col_scale).astype(jnp.bfloat16)


def draw_doc_lengths(key, part):
    other_count = NDOCS - 1
    remaining = TOKENS - MAXDOC
    even_length = remaining // other_count
    leftover = remaining % other_count
    key_moves, key_order = jax.random.split(jax.random.fold_in(key, 7), 2)
    order_index = jnp.arange(other_count, dtype=jnp.int32)
    lengths = even_length + (order_index < leftover).astype(jnp.int32)
    moves = jax.random.randint(key_moves, (other_count,), 0, even_length, jnp.int32)
    pair_moves = jnp.take(moves, order_index // 2)
    paired = order_index // 2 * 2 + 1 < other_count
    signs = jnp.where(order_index % 2 == 0, 1, -1).astype(jnp.int32)
    lengths = lengths + jnp.where(paired, signs * pair_moves, jnp.zeros_like(pair_moves))
    shuffled = jax.random.permutation(key_order, other_count)
    lengths = jnp.take(lengths, shuffled)
    return jnp.concatenate([lengths, jnp.full((1,), MAXDOC, jnp.int32)]).astype(jnp.int32)


def steps_of(rng, shape, cuts, low, top_value):
    factor_of = 1.0
    for dim, shards_of in cuts:
        heights = jax.random.uniform(jax.random.fold_in(jax.random.fold_in(rng, 6), dim), (shards_of,), jnp.float32, low / len(cuts), top_value / len(cuts))
        factor_of = factor_of * jnp.repeat(jnp.exp(heights), shape[dim] // shards_of).reshape((-1,) + (1,) * (len(shape) - 1 - dim))
    return factor_of


def gaussian(own_key, dims, deviation, most, pieces=(), held_as=jnp.bfloat16):
    loudness = steps_of(own_key, dims, pieces, -0.22, 0.18) if pieces else 1.0
    result = jax.random.normal(own_key, dims, jnp.float32) * deviation * loudness
    return jnp.minimum(jnp.maximum(result, -most), most).astype(held_as)


def setup_inputs(seed: int = 0) -> dict:
    arg_keys = jax.random.split(jax.random.key(seed), 10)
    tokens = draw_tokens(jax.random.fold_in(arg_keys[9], 71), 0)
    in_gain = jnp.clip(1.0 + 0.1 * jax.random.normal(arg_keys[1], (D,), jnp.float32), 0.5, 1.5)
    raw_queries = gaussian(arg_keys[2], (TOKENS, QH * HD), 1.0, 6.0, ((0, 8), (1, 4)))
    w_key = gaussian(arg_keys[3], (D, KVH * HD), D ** -0.5, 0.078125, ((1, 4),))
    w_value = gaussian(arg_keys[4], (D, KVH * HD), D ** -0.5, 0.078125, ((1, 4),))
    q_gain = jnp.clip(1.0 + 0.1 * jax.random.normal(arg_keys[5], (HD,), jnp.float32), 0.5, 1.5)
    k_gain = jnp.clip(1.0 + 0.1 * jax.random.normal(arg_keys[6], (HD,), jnp.float32), 0.5, 1.5)
    doc_lengths = draw_doc_lengths(jax.random.fold_in(arg_keys[9], 71), 0)
    out_grad = gaussian(arg_keys[8], (TOKENS, QH * HD), 10.0, 60.0, ((0, 8), (1, 4)))
    return {"tokens": tokens, "in_gain": in_gain, "raw_queries": raw_queries, "w_key": w_key, "w_value": w_value, "q_gain": q_gain, "k_gain": k_gain, "doc_lengths": doc_lengths, "out_grad": out_grad}


EPSILON = 1e-06
QUERY_SCALE = 168.0 ** (-0.5)
ROPE_BASE = 10000.0

def doc_begin(doc_lengths, positions):
    endings = jnp.cumsum(doc_lengths, dtype=jnp.int32)
    starts = endings - doc_lengths
    inside = starts[None, :] <= positions[:, None]
    return lax.optimization_barrier(jnp.max(jnp.where(inside, starts[None, :], jnp.zeros_like(starts)[None, :]), axis=1))

def input_norm(values, gain):
    return values * lax.rsqrt(lax.optimization_barrier(jnp.mean(values * values, axis=1, keepdims=True)) + EPSILON) * gain

def head_norm(values, gain):
    return values * lax.rsqrt(lax.optimization_barrier(jnp.mean(values * values, axis=-1, keepdims=True)) + EPSILON) * gain

def rotate(values, positions):
    half_size = values.shape[-1] // 2
    powers = jnp.arange(half_size, dtype=jnp.float32) * (2.0 / values.shape[-1])
    frequency = ROPE_BASE ** (-powers)
    angles = positions.astype(jnp.float32)[:, None] * frequency[None, :]
    cosine = jnp.cos(angles)[:, None, :]
    sine = jnp.sin(angles)[:, None, :]
    first = values[..., :half_size]
    second = values[..., half_size:]
    return jnp.concatenate([first * cosine - second * sine, second * cosine + first * sine], axis=-1)

def contract_last(left, right):
    return lax.dot_general(left, right, (((1,), (1,)), ((), ())), preferred_element_type=jnp.float32)

def contract_first(left, right):
    return lax.dot_general(left, right, (((0,), (0,)), ((), ())), preferred_element_type=jnp.float32)

def attend(queries, key_rows, value_rows, grads, lowest, positions, key_positions):
    query_float = queries.astype(jnp.float32)
    key_float = key_rows.astype(jnp.float32)
    value_float = value_rows.astype(jnp.float32)
    grad_float = grads.astype(jnp.float32)
    scores = jnp.einsum('qkgd,skd->kgqs', query_float, key_float)
    allowed = (key_positions[None, :] >= lowest[:, None]) & (key_positions[None, :] <= positions[:, None])
    exps = jnp.where(allowed[None, None], jnp.exp(scores), jnp.zeros_like(scores))
    totals = lax.optimization_barrier(jnp.sum(exps, axis=-1, keepdims=True))
    probs = exps / totals
    rounded = lax.optimization_barrier(probs.astype(jnp.bfloat16)).astype(jnp.float32)
    outputs = jnp.einsum('kgqs,skd->qkgd', rounded, value_float)
    deltas = lax.optimization_barrier(jnp.sum(grad_float * outputs, axis=-1))
    along = jnp.einsum('qkgd,skd->kgqs', grad_float, value_float)
    slopes = probs * (along - jnp.transpose(deltas, (1, 2, 0))[..., None])
    slopes = lax.optimization_barrier(slopes.astype(jnp.bfloat16)).astype(jnp.float32)
    query_grad = jnp.einsum('kgqs,skd->qkgd', slopes, key_float)
    key_grad = jnp.einsum('kgqs,qkgd->skd', slopes, query_float)
    value_grad = jnp.einsum('kgqs,qkgd->skd', rounded, grad_float)
    return (query_grad, key_grad, value_grad)

def reference(tokens, in_gain, raw_queries, w_key, w_value, q_gain, k_gain, doc_lengths, out_grad):
    head_size = q_gain.shape[0]
    kv_heads = w_key.shape[1] // head_size
    group_size = raw_queries.shape[1] // w_key.shape[1]
    total_rows = tokens.shape[0]
    reach_count = (WINDOW - 2) // TOK_DEV + 1
    x_float = tokens.astype(jnp.float32)
    normed_rows = input_norm(x_float, in_gain).astype(jnp.bfloat16)
    positions = jnp.arange(total_rows, dtype=jnp.int32)
    begins = doc_begin(doc_lengths, positions)
    offsets = positions - begins
    lowest = jnp.maximum(begins, positions - (WINDOW - 1))
    queries = raw_queries.astype(jnp.float32).reshape(total_rows, -1, head_size)
    keys_raw = jnp.dot(normed_rows, w_key, preferred_element_type=jnp.float32).reshape(total_rows, -1, head_size)
    values_raw = jnp.dot(normed_rows, w_value, preferred_element_type=jnp.float32).reshape(total_rows, -1, head_size)

    def query_map(values):
        return rotate(head_norm(values, q_gain), offsets) * QUERY_SCALE

    def key_map(values):
        return rotate(head_norm(values, k_gain), offsets)
    query_rot, query_back = jax.vjp(query_map, queries)
    key_rot, key_back = jax.vjp(key_map, keys_raw)
    query_rows = query_rot.astype(jnp.bfloat16).reshape(total_rows, kv_heads, group_size, head_size)
    key_rows = key_rot.astype(jnp.bfloat16)
    value_rows = values_raw.astype(jnp.bfloat16)
    grad_rows = out_grad.reshape(total_rows, kv_heads, group_size, head_size)
    margin = reach_count * TOK_DEV
    window_rows = margin + TOK_DEV
    key_padded = jnp.concatenate([jnp.zeros((margin, kv_heads, head_size), jnp.bfloat16), key_rows], axis=0)
    value_padded = jnp.concatenate([jnp.zeros((margin, kv_heads, head_size), jnp.bfloat16), value_rows], axis=0)

    def block_step(carry, block_index):
        key_accum, value_accum = carry
        start = (block_index * TOK_DEV).astype(jnp.int32)
        query_block = lax.dynamic_slice_in_dim(query_rows, start, TOK_DEV, 0)
        grad_block = lax.dynamic_slice_in_dim(grad_rows, start, TOK_DEV, 0)
        key_block = lax.dynamic_slice_in_dim(key_padded, start, window_rows, 0)
        value_block = lax.dynamic_slice_in_dim(value_padded, start, window_rows, 0)
        block_positions = lax.dynamic_slice_in_dim(positions, start, TOK_DEV, 0)
        block_lowest = lax.dynamic_slice_in_dim(lowest, start, TOK_DEV, 0)
        key_positions = start - margin + jnp.arange(window_rows, dtype=jnp.int32)
        query_grad, key_grad, value_grad = attend(query_block, key_block, value_block, grad_block, block_lowest, block_positions, key_positions)
        key_accum = lax.dynamic_update_slice_in_dim(key_accum, lax.dynamic_slice_in_dim(key_accum, start, window_rows, 0) + key_grad, start, 0)
        value_accum = lax.dynamic_update_slice_in_dim(value_accum, lax.dynamic_slice_in_dim(value_accum, start, window_rows, 0) + value_grad, start, 0)
        return ((key_accum, value_accum), query_grad)
    empty = jnp.zeros((total_rows + margin, kv_heads, head_size), jnp.float32)
    (key_accum, value_accum), query_grads = lax.scan(block_step, (empty, empty), jnp.arange(total_rows // TOK_DEV, dtype=jnp.int32))
    query_grad = query_grads.reshape(total_rows, kv_heads * group_size, head_size)
    key_grad = key_accum[margin:]
    value_grad = value_accum[margin:]
    grad_queries = query_back(query_grad)[0].reshape(total_rows, -1).astype(jnp.bfloat16)
    grad_k = key_back(key_grad)[0].reshape(total_rows, -1).astype(jnp.bfloat16)
    grad_v = value_grad.reshape(total_rows, -1).astype(jnp.bfloat16)
    kv_cols = w_key.shape[1] // N_TP
    summed = jnp.zeros(tokens.shape, jnp.float32)
    for member in range(N_TP):
        k_lo = member * kv_cols
        partial_sum = contract_last(grad_k[:, k_lo:k_lo + kv_cols], w_key[:, k_lo:k_lo + kv_cols])
        partial_sum = partial_sum + contract_last(grad_v[:, k_lo:k_lo + kv_cols], w_value[:, k_lo:k_lo + kv_cols])
        summed = summed + lax.optimization_barrier(partial_sum.astype(jnp.bfloat16)).astype(jnp.float32)

    def norm_map(values):
        return input_norm(values, in_gain)
    unused_rows, norm_back = jax.vjp(norm_map, x_float)
    grad_x = norm_back(summed)[0].astype(jnp.bfloat16)
    grad_wk = contract_first(normed_rows, grad_k)
    grad_wv = contract_first(normed_rows, grad_v)
    return (grad_x, grad_queries, grad_wk, grad_wv)
```

```python
import functools
import math

import jax
import jax.numpy as jnp
from jax import lax
from jax.experimental import pallas as pl
from jax.experimental.pallas import tpu as pltpu
from jax.sharding import PartitionSpec as P

WINDOW = 1024
EPSILON = 1e-06
QUERY_SCALE = 168.0 ** (-0.5)
ROPE_BASE = 10000.0
VMEM_BYTES = 56 * 1024 * 1024
SMEM = pltpu.SMEM


def doc_begin(doc_lengths, positions):
    endings = jnp.cumsum(doc_lengths, dtype=jnp.int32)
    starts = endings - doc_lengths
    inside = starts[None, :] <= positions[:, None]
    return jnp.max(jnp.where(inside, starts[None, :], jnp.zeros_like(starts)[None, :]), axis=1)


def rope_tables(offsets, head_size):
    half_size = head_size // 2
    powers = jnp.arange(half_size, dtype=jnp.float32) * (2.0 / head_size)
    frequency = ROPE_BASE ** (-powers)
    angles = offsets.astype(jnp.float32)[:, None] * frequency[None, :]
    cosine = jnp.cos(angles)
    sine = jnp.sin(angles)
    return jnp.concatenate([cosine, cosine], axis=1), jnp.concatenate([-sine, sine], axis=1)


def half_turn(values):
    return pltpu.roll(values, values.shape[-1] // 2, values.ndim - 1)


def rope(values, cosine, sine):
    return values * cosine + half_turn(values) * sine


def rope_back(grads, cosine, sine):
    return grads * cosine + half_turn(grads * sine)


def inv_rms(values):
    return lax.rsqrt(jnp.mean(values * values, axis=-1, keepdims=True) + EPSILON)


def norm_back(grads, values, scale, gain):
    scaled = grads * gain
    mean = jnp.mean(values * scaled, axis=-1, keepdims=True)
    return scale * scaled - values * (scale * scale * scale * mean)


def dot_last(left, right):
    return lax.dot_general(left, right, (((1,), (1,)), ((), ())), preferred_element_type=jnp.float32)


def dot_first(left, right):
    return lax.dot_general(left, right, (((0,), (0,)), ((), ())), preferred_element_type=jnp.float32)


def full_spec(array):
    return pl.BlockSpec(array.shape, lambda *_: (0,) * array.ndim)


def any_spec():
    return pl.BlockSpec(memory_space=pl.ANY)


def smem_spec():
    return pl.BlockSpec(memory_space=SMEM)


def cost(flops, *arrays):
    size = sum(math.prod(a.shape) * jnp.dtype(a.dtype).itemsize for a in arrays)
    return pl.CostEstimate(flops=flops, bytes_accessed=size, transcendentals=0)


def params():
    return pltpu.CompilerParams(vmem_limit_bytes=VMEM_BYTES)


def project_body(count, info, gain, k_gain, cosine, sine, w_key, w_value, *rest):
    blocks = rest[:count]
    normed, key_value, raw_keys, held, sem = rest[count:]
    rows = held.shape[0]
    head_size = k_gain.shape[1]
    for index in range(count):

        @pl.when(info[0] == index)
        def _():
            copy = pltpu.make_async_copy(blocks[index], held, sem)
            copy.start()
            copy.wait()

    values = held[...].astype(jnp.float32)
    normed[...] = (values * inv_rms(values) * gain[...]).astype(jnp.bfloat16)
    keys = jnp.dot(normed[...], w_key[...], preferred_element_type=jnp.float32)
    raw_keys[...] = keys
    vals = jnp.dot(normed[...], w_value[...], preferred_element_type=jnp.float32)
    place = pl.ds(pl.multiple_of(info[1] * rows, rows), rows)
    cos_rows = cosine[place, :]
    sin_rows = sine[place, :]
    for head in range(w_key.shape[1] // head_size):
        cols = slice(head * head_size, (head + 1) * head_size)
        head_keys = keys[:, cols]
        turned = rope(head_keys * inv_rms(head_keys) * k_gain[...], cos_rows, sin_rows)
        low = 2 * head * head_size
        key_value[:, low : low + head_size] = turned.astype(jnp.bfloat16)
        key_value[:, low + head_size : low + 2 * head_size] = vals[:, cols].astype(jnp.bfloat16)


def project(info, blocks, in_gain, k_gain, cosine, sine, w_key, w_value):
    rows, width = blocks[0].shape
    cols = w_key.shape[1]
    outs = (
        jax.ShapeDtypeStruct((rows, width), jnp.bfloat16),
        jax.ShapeDtypeStruct((rows, 2 * cols), jnp.bfloat16),
        jax.ShapeDtypeStruct((rows, cols), jnp.float32),
    )
    dense = (in_gain, k_gain, cosine, sine, w_key, w_value)
    return pl.pallas_call(
        functools.partial(project_body, len(blocks)),
        name="project_block",
        grid=(1,),
        out_shape=outs,
        in_specs=[smem_spec()] + [full_spec(a) for a in dense] + [any_spec()] * len(blocks),
        out_specs=[full_spec(o) for o in outs],
        scratch_shapes=[pltpu.VMEM((rows, width), jnp.bfloat16), pltpu.SemaphoreType.DMA],
        compiler_params=params(),
        cost_estimate=cost(4 * rows * width * cols, blocks[0], w_key, w_value, *outs),
    )(info, *dense, *blocks)


def attend_body(reach, slots, info, lowest, q_gain, cosine, sine, queries, grads, *rest):
    blocks = rest[: (reach + 1) * slots]
    rest = rest[(reach + 1) * slots :]
    query_grads, own = rest[0], rest[1]
    far = rest[2 : 2 + reach]
    keys, values, key_sum, value_sum = rest[2 + reach :]
    rows = queries.shape[0]
    head_size = q_gain.shape[1]
    group = queries.shape[1] // head_size
    tile = blocks[0].shape[0]
    margin = reach * rows
    for slot in range(slots):
        start = info[slot] * tile
        for section in range(reach + 1):
            place = pl.ds(pl.multiple_of(section * rows + start, tile), tile)
            block = blocks[section * slots + slot]
            keys[place, :] = block[:, :head_size]
            values[place, :] = block[:, head_size:]
    key_sum[...] = jnp.zeros_like(key_sum)
    value_sum[...] = jnp.zeros_like(value_sum)
    for index in range(rows // tile):
        top = index * tile
        low = max(0, (top + margin - WINDOW + 1) // tile * tile)
        high = top + tile + margin
        width = high - low
        cos_rows = cosine[top : top + tile, :]
        sin_rows = sine[top : top + tile, :]
        raw = []
        scales = []
        turned = []
        for head in range(group):
            raw.append(queries[top : top + tile, head * head_size : (head + 1) * head_size].astype(jnp.float32))
            scales.append(inv_rms(raw[head]))
            turned.append(rope(raw[head] * scales[head] * q_gain[...], cos_rows, sin_rows) * QUERY_SCALE)
        query_rows = jnp.concatenate(turned, axis=0).astype(jnp.bfloat16)
        grad_rows = jnp.concatenate(
            [grads[top : top + tile, head * head_size : (head + 1) * head_size] for head in range(group)], axis=0
        )
        key_rows = keys[low:high, :]
        value_rows = values[low:high, :]
        columns = lax.broadcasted_iota(jnp.int32, (tile, width), 1) + low
        last = lax.broadcasted_iota(jnp.int32, (tile, width), 0) + (top + margin)
        allowed = (columns >= lowest[top : top + tile, :]) & (columns <= last)
        scores = dot_last(query_rows, key_rows).reshape(group, tile, width)
        exps = jnp.where(allowed[None], jnp.exp(scores), 0.0)
        probs = exps * (1.0 / jnp.sum(exps, axis=-1, keepdims=True))
        weights = probs.astype(jnp.bfloat16)
        along = dot_last(grad_rows, value_rows).reshape(group, tile, width)
        deltas = jnp.sum(weights.astype(jnp.float32) * along, axis=-1, keepdims=True)
        slopes = (probs * (along - deltas)).astype(jnp.bfloat16).reshape(group * tile, width)
        weights = weights.reshape(group * tile, width)
        key_sum[low:high, :] += dot_first(slopes, query_rows)
        value_sum[low:high, :] += dot_first(weights, grad_rows)
        back = jnp.dot(slopes, key_rows, preferred_element_type=jnp.float32)
        for head in range(group):
            turned_back = rope_back(back[head * tile : (head + 1) * tile] * QUERY_SCALE, cos_rows, sin_rows)
            result = norm_back(turned_back, raw[head], scales[head], q_gain[...])
            query_grads[top : top + tile, head * head_size : (head + 1) * head_size] = result.astype(jnp.bfloat16)
    for section in range(reach):
        span = slice(section * rows, (section + 1) * rows)
        far[section][:, :head_size] = key_sum[span, :].astype(jnp.bfloat16)
        far[section][:, head_size:] = value_sum[span, :].astype(jnp.bfloat16)
    own[:, :head_size] = key_sum[margin:, :]
    own[:, head_size:] = value_sum[margin:, :]


def attend(head, kv_heads, reach, info, lowest, q_gain, cosine, sine, queries, grads, blocks):
    rows = queries.shape[0]
    head_size = q_gain.shape[1]
    slots = len(blocks) // (reach + 1)
    tile = blocks[0].shape[0]
    cols = queries.shape[1] // kv_heads
    pick = lambda *_: (0, head)
    outs = (
        jax.ShapeDtypeStruct((rows, cols), jnp.bfloat16),
        jax.ShapeDtypeStruct((rows, 2 * head_size), jnp.float32),
    ) + (jax.ShapeDtypeStruct((rows, 2 * head_size), jnp.bfloat16),) * reach
    dense = (lowest, q_gain, cosine, sine)
    window = (reach + 1) * rows
    return pl.pallas_call(
        functools.partial(attend_body, reach, slots),
        name="attend_head",
        grid=(1,),
        out_shape=outs,
        in_specs=[smem_spec()]
        + [full_spec(a) for a in dense]
        + [pl.BlockSpec((rows, cols), pick)] * 2
        + [pl.BlockSpec((tile, 2 * head_size), pick)] * len(blocks),
        out_specs=[full_spec(o) for o in outs],
        scratch_shapes=[pltpu.VMEM((window, head_size), jnp.bfloat16)] * 2
        + [pltpu.VMEM((window, head_size), jnp.float32)] * 2,
        compiler_params=params(),
        cost_estimate=cost(10 * rows * window * cols, queries, grads, *blocks, *outs),
    )(info, *dense, queries, grads, *blocks)


def finish_body(reach, slots, info, k_gain, cosine, sine, own, *rest):
    arrived = rest[:reach]
    raw_keys = rest[reach : reach + slots]
    result = rest[reach + slots]
    head_size = k_gain.shape[1]
    rows = raw_keys[0].shape[0]
    for slot in range(slots):
        place = pl.ds(pl.multiple_of(info[slot] * rows, rows), rows)
        total = own[place, :]
        for part in arrived:
            total = total + part[place, :].astype(jnp.float32)
        values = raw_keys[slot][...]
        turned = rope_back(total[:, :head_size], cosine[place, :], sine[place, :])
        keys = norm_back(turned, values, inv_rms(values), k_gain[...])
        result[place, :head_size] = keys.astype(jnp.bfloat16)
        result[place, head_size:] = total[:, head_size:].astype(jnp.bfloat16)


def finish(head, info, k_gain, cosine, sine, own, arrived, raw_keys):
    head_size = k_gain.shape[1]
    out = jax.ShapeDtypeStruct(own.shape, jnp.bfloat16)
    dense = (k_gain, cosine, sine, own, *arrived)
    return pl.pallas_call(
        functools.partial(finish_body, len(arrived), len(raw_keys)),
        name="finish_kv",
        grid=(1,),
        out_shape=out,
        in_specs=[smem_spec()]
        + [full_spec(a) for a in dense]
        + [pl.BlockSpec((raw_keys[0].shape[0], head_size), lambda *_: (0, head))] * len(raw_keys),
        out_specs=full_spec(out),
        compiler_params=params(),
        cost_estimate=cost(0, own, *arrived, out),
    )(info, *dense, *raw_keys)


def weight_body(slots, info, grads, *rest):
    blocks = rest[:slots]
    send, keep, held = rest[slots:]
    rows = blocks[0].shape[0]
    chunk = send.shape[1]
    own = info[slots]
    left = jnp.concatenate([block[...] for block in blocks], axis=0)
    right = jnp.concatenate(
        [grads[pl.ds(pl.multiple_of(info[slot] * rows, rows), rows), :] for slot in range(slots)], axis=0
    )
    held[...] = dot_first(left, right)
    for pair in range(send.shape[0]):
        other = pl.ds(pl.multiple_of((2 * pair + 1 - own) * chunk, 8), chunk)
        mine = pl.ds(pl.multiple_of((2 * pair + own) * chunk, 8), chunk)
        send[pair] = held[other, :].astype(jnp.bfloat16)
        keep[pair] = held[mine, :].astype(jnp.bfloat16)


def weight_terms(info, grads, blocks, chunk):
    rows, width = blocks[0].shape
    cols = grads.shape[1]
    tile = math.lcm(2 * chunk, 128)
    pairs = tile // (2 * chunk)
    out = jax.ShapeDtypeStruct((width // (2 * chunk), chunk, cols), jnp.bfloat16)
    out_spec = pl.BlockSpec((pairs, chunk, cols), lambda step: (step, 0, 0))
    return pl.pallas_call(
        functools.partial(weight_body, len(blocks)),
        name="weight_terms",
        grid=(width // tile,),
        out_shape=(out, out),
        in_specs=[smem_spec(), full_spec(grads)]
        + [pl.BlockSpec((rows, tile), lambda step: (0, step))] * len(blocks),
        out_specs=(out_spec, out_spec),
        scratch_shapes=[pltpu.VMEM((tile, cols), jnp.float32)],
        compiler_params=params(),
        cost_estimate=cost(2 * len(blocks) * rows * width * cols, grads, *blocks, out, out),
    )(info, grads, *blocks)


def add(left, right):
    return left.astype(jnp.float32) + right.astype(jnp.float32)


def split_body(halves, info, *rest):
    keeps, arrivals, outs = rest[: len(halves)], rest[len(halves) : 2 * len(halves)], rest[2 * len(halves) :]
    for index, (cols, outer, inner) in enumerate(halves):
        own = info[index]
        for high in range(outer):
            for low in range(inner):
                for side, target in ((1 - own, outs[2 * index]), (own, outs[2 * index + 1])):
                    place = (high * 2 + side) * inner + low
                    total = add(keeps[index][place, :, cols], arrivals[index][place, :, cols])
                    target[high * inner + low] = total.astype(jnp.bfloat16)


def split_sum(info, keeps, arrivals, halves):
    outs = []
    for keep, (cols, outer, inner) in zip(keeps, halves):
        outs += [jax.ShapeDtypeStruct((outer * inner, keep.shape[1], cols.stop - cols.start), jnp.bfloat16)] * 2
    return pl.pallas_call(
        functools.partial(split_body, halves),
        name="split_sum",
        grid=(1,),
        out_shape=tuple(outs),
        in_specs=[smem_spec()] + [full_spec(a) for a in (*keeps, *arrivals)],
        out_specs=tuple(full_spec(o) for o in outs),
        compiler_params=params(),
        cost_estimate=cost(0, *keeps, *arrivals, *outs),
    )(info, *keeps, *arrivals)


def swap(array, bit):
    size = lax.axis_size("seq")
    return lax.ppermute(array, "seq", [(i, i ^ (1 << bit)) for i in range(size)])


def scatter_sum(send, keep):
    bits = lax.axis_size("seq").bit_length() - 1
    index = lax.axis_index("seq")
    half = keep.shape[2] // 2
    routes = (list(range(1, bits)), list(range(bits - 1, 0, -1)))
    lefts = [list(range(1, bits)), list(range(1, bits))]
    arrival = swap(send, 0)
    keeps, arrivals = [keep, keep], [arrival, arrival]
    cols = [slice(0, half), slice(half, 2 * half)]
    for step in range(bits - 1):
        turn = [route[step] for route in routes]
        halves = []
        for path in range(2):
            place = lefts[path].index(turn[path])
            halves.append((cols[path], 1 << (len(lefts[path]) - 1 - place), 1 << place))
            lefts[path].remove(turn[path])
        info = jnp.stack([(index >> bit) & 1 for bit in turn]).astype(jnp.int32)
        sent_a, kept_a, sent_b, kept_b = split_sum(info, keeps, arrivals, tuple(halves))
        arrivals = [swap(sent_a, turn[0]), swap(sent_b, turn[1])]
        keeps = [kept_a, kept_b]
        cols = [slice(0, half), slice(0, half)]
    return keeps, arrivals


def gather_body(heads, *rest):
    parts = rest[: 4 * heads]
    outs = rest[4 * heads :]
    size = parts[0].shape[2]
    for head in range(heads):
        for side in range(2):
            keep, arrival = parts[4 * head + side], parts[4 * head + 2 + side]
            outs[side][:, head * size : (head + 1) * size] = add(keep[0], arrival[0])


def gather_heads(parts, heads):
    _, rows, cols = parts[0].shape
    out = jax.ShapeDtypeStruct((rows, cols * heads), jnp.float32)
    return pl.pallas_call(
        functools.partial(gather_body, heads),
        name="gather_heads",
        grid=(1,),
        out_shape=(out, out),
        in_specs=[full_spec(a) for a in parts],
        out_specs=(full_spec(out), full_spec(out)),
        compiler_params=params(),
        cost_estimate=cost(0, *parts, out, out),
    )(*parts)


def arrival_table(count):
    table = []
    for place in range(count):
        arrivals = []
        for step in range(1, count):
            if place - step >= 0:
                arrivals.append((2 * (step - 1), place - step))
            if place + step < count:
                arrivals.append((2 * (step - 1) + 1, place + step))
        table.append(arrivals)
    return table


def shards(tokens, in_gain, raw_queries, w_key, w_value, q_gain, k_gain, doc_lengths, out_grad):
    tp_count = lax.axis_size("tp")
    seq_count = lax.axis_size("seq")
    head_size = q_gain.shape[0]
    kv_heads = w_key.shape[1] // head_size
    rows, width = tokens.shape
    shard_rows = rows * tp_count
    reach = (WINDOW - 2) // shard_rows + 1
    seq_index = lax.axis_index("seq")
    tp_index = lax.axis_index("tp")
    first_row = seq_index * shard_rows
    positions = first_row + jnp.arange(shard_rows, dtype=jnp.int32)
    begins = doc_begin(doc_lengths, positions)
    cosine, sine = rope_tables(positions - begins, head_size)
    lowest = jnp.maximum(begins, positions - (WINDOW - 1)) - (first_row - reach * shard_rows)
    lowest = lowest[:, None]
    gain_row = in_gain[None, :]
    q_row = q_gain[None, :]
    k_row = k_gain[None, :]

    table = arrival_table(tp_count)
    picks = jnp.array(table, dtype=jnp.int32).reshape(tp_count, tp_count - 1, 2)
    picks = lax.dynamic_index_in_dim(picks, tp_index, 0, keepdims=False)
    infos = [jnp.stack([jnp.int32(0), tp_index.astype(jnp.int32)])] + [picks[i] for i in range(tp_count - 1)]
    slot_places = jnp.concatenate([tp_index.astype(jnp.int32)[None], picks[:, 1]])

    normed_blocks, kv_blocks, raw_keys = [], [], []
    halo = [[] for _ in range(reach)]
    arrivals = []
    going_up = going_down = tokens
    for slot in range(tp_count):
        candidates = [tokens] if slot == 0 else list(arrivals)
        if slot < tp_count - 1:
            up_pairs = [(i, i + 1) for i in range(slot, tp_count - 1)]
            down_pairs = [(i + 1, i) for i in range(tp_count - 1 - slot)]
            going_up = lax.ppermute(going_up, "tp", up_pairs)
            going_down = lax.ppermute(going_down, "tp", down_pairs)
            arrivals += [going_up, going_down]
        normed, key_value, keys = project(
            infos[slot], candidates, gain_row, k_row, cosine, sine, w_key, w_value
        )
        normed_blocks.append(normed)
        kv_blocks.append(key_value)
        raw_keys.append(keys)
        for distance in range(1, reach + 1):
            pairs = [(i, i + distance) for i in range(seq_count - distance)]
            halo[distance - 1].append(lax.ppermute(key_value, "seq", pairs))

    blocks = []
    for distance in range(reach, 0, -1):
        blocks += halo[distance - 1]
    blocks += kv_blocks
    query_parts, kv_grads = [], []
    for head in range(kv_heads):
        outs = attend(head, kv_heads, reach, slot_places, lowest, q_row, cosine, sine, raw_queries, out_grad, blocks)
        query_parts.append(outs[0])
        back = []
        for section in range(reach):
            distance = reach - section
            pairs = [(i + distance, i) for i in range(seq_count - distance)]
            back.append(lax.ppermute(outs[2 + section], "seq", pairs))
        kv_grads.append(finish(head, slot_places, k_row, cosine, sine, outs[1], back, raw_keys))
    grad_queries = jnp.concatenate(query_parts, axis=1)

    grad_k = jnp.concatenate([g[:, :head_size] for g in kv_grads], axis=1)
    grad_v = jnp.concatenate([g[:, head_size:] for g in kv_grads], axis=1)
    partial_sum = dot_last(grad_k, w_key) + dot_last(grad_v, w_value)
    normed_grad = lax.psum_scatter(
        partial_sum.astype(jnp.bfloat16), "tp", scatter_dimension=0, tiled=True
    ).astype(jnp.float32)
    x_float = tokens.astype(jnp.float32)
    grad_x = norm_back(normed_grad, x_float, inv_rms(x_float), gain_row).astype(jnp.bfloat16)

    chunk = width // seq_count
    if chunk % 16 == 0 and seq_count & (seq_count - 1) == 0 and seq_count > 1 and width % math.lcm(2 * chunk, 128) == 0:
        info = jnp.concatenate([slot_places, (seq_index & 1).astype(jnp.int32)[None]])
        parts = []
        for head in range(kv_heads):
            send, keep = weight_terms(info, kv_grads[head], normed_blocks, chunk)
            keeps, comings = scatter_sum(send, keep)
            parts += [*keeps, *comings]
        grad_wk, grad_wv = gather_heads(parts, kv_heads)
    else:
        left = jnp.concatenate(normed_blocks, axis=0)
        order = (slot_places[:, None] * rows + jnp.arange(rows, dtype=jnp.int32)[None, :]).reshape(-1)
        right = jnp.take(jnp.concatenate([grad_k, grad_v], axis=1), order, axis=0)
        summed = lax.psum_scatter(dot_first(left, right), "seq", scatter_dimension=0, tiled=True)
        grad_wk = summed[:, : w_key.shape[1]]
        grad_wv = summed[:, w_key.shape[1] :]
    return (grad_x, grad_queries, grad_wk, grad_wv)


def solution(mesh):
    placed = (
        P(("seq", "tp"), None),
        P(),
        P("seq", "tp"),
        P(None, "tp"),
        P(None, "tp"),
        P(),
        P(),
        P(),
        P("seq", "tp"),
    )
    return jax.shard_map(
        shards,
        mesh=mesh,
        in_specs=placed,
        out_specs=(P(("seq", "tp"), None), P("seq", "tp"), P("seq", "tp"), P("seq", "tp")),
        check_vma=False,
    )
```

```python
import functools
import math

import jax
import jax.numpy as jnp
from jax import lax
from jax.experimental import pallas as pl
from jax.experimental.pallas import tpu as pltpu
from jax.sharding import PartitionSpec as P

WINDOW = 1024
EPSILON = 1e-06
QUERY_SCALE = 168.0 ** (-0.5)
ROPE_BASE = 10000.0
SMEM = pltpu.SMEM


def doc_begin(doc_lengths, positions):
    endings = jnp.cumsum(doc_lengths, dtype=jnp.int32)
    starts = endings - doc_lengths
    inside = starts[None, :] <= positions[:, None]
    return jnp.max(jnp.where(inside, starts[None, :], jnp.zeros_like(starts)[None, :]), axis=1)


def rope_tables(offsets, head_size):
    half_size = head_size // 2
    powers = jnp.arange(half_size, dtype=jnp.float32) * (2.0 / head_size)
    frequency = ROPE_BASE ** (-powers)
    angles = offsets.astype(jnp.float32)[:, None] * frequency[None, :]
    cosine = jnp.cos(angles)
    sine = jnp.sin(angles)
    return jnp.concatenate([cosine, cosine], axis=1), jnp.concatenate([-sine, sine], axis=1)


def half_turn(values):
    return pltpu.roll(values, values.shape[-1] // 2, values.ndim - 1)


def rope(values, cosine, sine):
    return values * cosine + half_turn(values) * sine


def rope_back(grads, cosine, sine):
    return grads * cosine + half_turn(grads * sine)


def inv_rms(values):
    return lax.rsqrt(jnp.mean(values * values, axis=-1, keepdims=True) + EPSILON)


def norm_back(grads, values, scale, gain):
    scaled = grads * gain
    mean = jnp.mean(values * scaled, axis=-1, keepdims=True)
    return scale * scaled - values * (scale * scale * scale * mean)


def dot_last(left, right):
    return lax.dot_general(left, right, (((1,), (1,)), ((), ())), preferred_element_type=jnp.float32)


def dot_first(left, right):
    return lax.dot_general(left, right, (((0,), (0,)), ((), ())), preferred_element_type=jnp.float32)


def full_spec(array):
    return pl.BlockSpec(array.shape, lambda *_: (0,) * array.ndim)


def any_spec():
    return pl.BlockSpec(memory_space=pl.ANY)


def smem_spec():
    return pl.BlockSpec(memory_space=SMEM)


def after(value, others):
    return lax.optimization_barrier((value, others))[0]


def cost(flops, *arrays):
    size = sum(math.prod(a.shape) * jnp.dtype(a.dtype).itemsize for a in arrays)
    return pl.CostEstimate(flops=flops, bytes_accessed=size, transcendentals=0)


def params(megabytes=30):
    return pltpu.CompilerParams(vmem_limit_bytes=megabytes * 1024 * 1024)


def start_all(copies):
    for copy in copies:
        copy.start()


def wait_all(copies):
    for copy in copies:
        copy.wait()


def piece_copies(places, seq_index, arrays, target, sems):
    copies = []
    for number, (offset, low) in enumerate(places):
        rows, cols = arrays[number].shape
        start = pl.multiple_of(jnp.bitwise_xor(seq_index, offset) * rows, 16)
        slot = target.at[pl.ds(start, rows), pl.ds(low, cols)]
        copies.append(pltpu.make_async_copy(arrays[number], slot, sems.at[number]))
    return copies


def store_heads(key_value, raw_keys, rows, keys, values, k_gain, cos_rows, sin_rows):
    head_size = k_gain.shape[1]
    raw_keys[rows, :] = keys.astype(raw_keys.dtype)
    for head in range(keys.shape[1] // head_size):
        cols = slice(head * head_size, (head + 1) * head_size)
        low = 2 * head * head_size
        head_keys = keys[:, cols]
        turned = rope(head_keys * inv_rms(head_keys) * k_gain[...], cos_rows, sin_rows)
        key_value[rows, low : low + head_size] = turned.astype(jnp.bfloat16)
        key_value[rows, low + head_size : low + 2 * head_size] = values[:, cols].astype(jnp.bfloat16)


def project_body(count, info, gain, k_gain, cosine, sine, w_key, w_value, *rest):
    blocks = rest[:count]
    key_value, raw_keys, normed, held, key_held, value_held, sems = rest[count:]
    rows = held.shape[0]

    def block_copy(index):
        return pltpu.make_async_copy(blocks[index], held, sems.at[2])

    for index in range(count):
        pl.when(info[0] == index)(lambda index=index: block_copy(index).start())
    own_copies = [
        pltpu.make_async_copy(w_key, key_held, sems.at[0]),
        pltpu.make_async_copy(w_value, value_held, sems.at[1]),
    ]
    start_all(own_copies)
    for index in range(count):
        pl.when(info[0] == index)(lambda index=index: block_copy(index).wait())
    values = held[...].astype(jnp.float32)
    normed[...] = (values * inv_rms(values) * gain[...]).astype(jnp.bfloat16)
    place = pl.ds(pl.multiple_of(info[1] * rows, rows), rows)
    wait_all(own_copies)
    keys = jnp.dot(normed[...], key_held[...], preferred_element_type=jnp.float32)
    vals = jnp.dot(normed[...], value_held[...], preferred_element_type=jnp.float32)
    store_heads(key_value, raw_keys, slice(0, rows), keys, vals, k_gain, cosine[place, :], sine[place, :])


def project(info, blocks, in_gain, k_gain, cosine, sine, w_key, w_value):
    rows, width = blocks[0].shape
    cols = w_key.shape[1]
    outs = [
        jax.ShapeDtypeStruct((rows, 2 * cols), jnp.bfloat16),
        jax.ShapeDtypeStruct((rows, cols), jnp.bfloat16),
        jax.ShapeDtypeStruct((rows, width), jnp.bfloat16),
    ]
    scratch = [
        pltpu.VMEM((rows, width), jnp.bfloat16),
        pltpu.VMEM((width, cols), jnp.bfloat16),
        pltpu.VMEM((width, cols), jnp.bfloat16),
        pltpu.SemaphoreType.DMA((3,)),
    ]
    dense = (in_gain, k_gain, cosine, sine)
    return pl.pallas_call(
        functools.partial(project_body, len(blocks)),
        name="project_block",
        grid=(1,),
        out_shape=tuple(outs),
        in_specs=[smem_spec()] + [full_spec(a) for a in dense] + [any_spec()] * (2 + len(blocks)),
        out_specs=tuple(full_spec(o) for o in outs),
        scratch_shapes=scratch,
        compiler_params=params(56),
        cost_estimate=cost(4 * rows * width * cols, blocks[0], w_key, w_value, *outs),
    )(info, *dense, w_key, w_value, *blocks)


def project_pair_body(places, info, gain, k_gain, cosine, sine, w_key, w_value, ready, block, *rest):
    pieces = rest[: len(places)]
    key_value, raw_keys, normed, far_key_value, far_keys = rest[len(places) : len(places) + 5]
    held, left, key_held, value_held, far_held, sems, far_sems = rest[len(places) + 5 :]
    rows, width = held.shape
    cols = w_key.shape[1]
    block_copy = pltpu.make_async_copy(block, held, sems.at[2])
    block_copy.start()
    ready_copy = pltpu.make_async_copy(ready, left.at[pl.ds(0, rows)], sems.at[3])
    ready_copy.start()
    far_copies = piece_copies(places, info[0], pieces, far_held, far_sems)
    start_all(far_copies)
    own_copies = [
        pltpu.make_async_copy(w_key, key_held, sems.at[0]),
        pltpu.make_async_copy(w_value, value_held, sems.at[1]),
    ]
    start_all(own_copies)
    block_copy.wait()
    values = held[...].astype(jnp.float32)
    normed[...] = (values * inv_rms(values) * gain[...]).astype(jnp.bfloat16)
    ready_copy.wait()
    left[rows:, :] = normed[...]
    wait_all(far_copies)
    both = jnp.dot(left[...], far_held[...], preferred_element_type=jnp.float32)
    for number in range(2):
        place = pl.ds(pl.multiple_of(info[1 + number] * rows, rows), rows)
        span = slice(number * rows, (number + 1) * rows)
        part = both[span]
        store_heads(
            far_key_value, far_keys, span, part[:, :cols], part[:, cols:], k_gain, cosine[place, :], sine[place, :]
        )
    place = pl.ds(pl.multiple_of(info[2] * rows, rows), rows)
    wait_all(own_copies)
    keys = jnp.dot(normed[...], key_held[...], preferred_element_type=jnp.float32)
    vals = jnp.dot(normed[...], value_held[...], preferred_element_type=jnp.float32)
    store_heads(key_value, raw_keys, slice(0, rows), keys, vals, k_gain, cosine[place, :], sine[place, :])


def project_pair(info, ready, block, in_gain, k_gain, cosine, sine, w_key, w_value, pieces):
    rows, width = block.shape
    cols = w_key.shape[1]
    places = [(offset, low) for offset, low, _ in pieces]
    arrays = [piece for _, _, piece in pieces]
    outs = tuple(
        jax.ShapeDtypeStruct(shape, jnp.bfloat16)
        for shape in ((rows, 2 * cols), (rows, cols), (rows, width), (2 * rows, 2 * cols), (2 * rows, cols))
    )
    dense = (in_gain, k_gain, cosine, sine)
    return pl.pallas_call(
        functools.partial(project_pair_body, places),
        name="project_pair",
        grid=(1,),
        out_shape=outs,
        in_specs=[smem_spec()] + [full_spec(a) for a in dense] + [any_spec()] * (4 + len(arrays)),
        out_specs=tuple(full_spec(o) for o in outs),
        scratch_shapes=[
            pltpu.VMEM((rows, width), jnp.bfloat16),
            pltpu.VMEM((2 * rows, width), jnp.bfloat16),
            pltpu.VMEM((width, cols), jnp.bfloat16),
            pltpu.VMEM((width, cols), jnp.bfloat16),
            pltpu.VMEM((width, 2 * cols), jnp.bfloat16),
            pltpu.SemaphoreType.DMA((4,)),
            pltpu.SemaphoreType.DMA((len(arrays),)),
        ],
        compiler_params=params(56),
        cost_estimate=cost(12 * rows * width * cols, block, w_key, w_value, *arrays, *outs),
    )(info, *dense, w_key, w_value, ready, block, *arrays)


def attend_body(reach, slots, info, lowest, q_gain, cosine, sine, queries, grads, *rest):
    blocks = rest[: (reach + 1) * slots]
    rest = rest[(reach + 1) * slots :]
    query_grads, own = rest[0], rest[1]
    far = rest[2 : 2 + reach]
    keys, values, key_sum, value_sum = rest[2 + reach :]
    rows = queries.shape[0]
    head_size = q_gain.shape[1]
    group = queries.shape[1] // head_size
    tile = blocks[0].shape[0]
    margin = reach * rows
    for slot in range(slots):
        start = info[slot] * tile
        for section in range(reach + 1):
            place = pl.ds(pl.multiple_of(section * rows + start, tile), tile)
            block = blocks[section * slots + slot]
            keys[place, :] = block[:, :head_size]
            values[place, :] = block[:, head_size:]
    key_sum[...] = jnp.zeros_like(key_sum)
    value_sum[...] = jnp.zeros_like(value_sum)
    for index in range(rows // tile):
        top = index * tile
        low = max(0, (top + margin - WINDOW + 1) // tile * tile)
        high = top + tile + margin
        width = high - low
        cos_rows = cosine[top : top + tile, :]
        sin_rows = sine[top : top + tile, :]
        raw = []
        scales = []
        turned = []
        for head in range(group):
            raw.append(queries[top : top + tile, head * head_size : (head + 1) * head_size].astype(jnp.float32))
            scales.append(inv_rms(raw[head]))
            turned.append(rope(raw[head] * scales[head] * q_gain[...], cos_rows, sin_rows) * QUERY_SCALE)
        query_rows = jnp.concatenate(turned, axis=0).astype(jnp.bfloat16)
        grad_rows = jnp.concatenate(
            [grads[top : top + tile, head * head_size : (head + 1) * head_size] for head in range(group)], axis=0
        )
        key_rows = keys[low:high, :]
        value_rows = values[low:high, :]
        columns = lax.broadcasted_iota(jnp.int32, (tile, width), 1) + low
        last = lax.broadcasted_iota(jnp.int32, (tile, width), 0) + (top + margin)
        allowed = (columns >= lowest[top : top + tile, :]) & (columns <= last)
        scores = dot_last(query_rows, key_rows).reshape(group, tile, width)
        exps = jnp.where(allowed[None], jnp.exp(scores), 0.0)
        probs = exps * (1.0 / jnp.sum(exps, axis=-1, keepdims=True))
        weights = probs.astype(jnp.bfloat16)
        along = dot_last(grad_rows, value_rows).reshape(group, tile, width)
        deltas = jnp.sum(weights.astype(jnp.float32) * along, axis=-1, keepdims=True)
        slopes = (probs * (along - deltas)).astype(jnp.bfloat16).reshape(group * tile, width)
        weights = weights.reshape(group * tile, width)
        key_sum[low:high, :] += dot_first(slopes, query_rows)
        value_sum[low:high, :] += dot_first(weights, grad_rows)
        back = jnp.dot(slopes, key_rows, preferred_element_type=jnp.float32)
        for head in range(group):
            turned_back = rope_back(back[head * tile : (head + 1) * tile] * QUERY_SCALE, cos_rows, sin_rows)
            result = norm_back(turned_back, raw[head], scales[head], q_gain[...])
            query_grads[top : top + tile, head * head_size : (head + 1) * head_size] = result.astype(jnp.bfloat16)
    for section in range(reach):
        span = slice(section * rows, (section + 1) * rows)
        far[section][:, :head_size] = key_sum[span, :].astype(jnp.bfloat16)
        far[section][:, head_size:] = value_sum[span, :].astype(jnp.bfloat16)
    own[:, :head_size] = key_sum[margin:, :]
    own[:, head_size:] = value_sum[margin:, :]


def attend(head, kv_heads, reach, info, lowest, q_gain, cosine, sine, queries, grads, blocks):
    rows = queries.shape[0]
    head_size = q_gain.shape[1]
    slots = len(blocks) // (reach + 1)
    tile = rows // slots
    cols = queries.shape[1] // kv_heads
    pick = lambda *_: (0, head)
    arrays = [array for array, _ in blocks]
    outs = (
        jax.ShapeDtypeStruct((rows, cols), jnp.bfloat16),
        jax.ShapeDtypeStruct((rows, 2 * head_size), jnp.float32),
    ) + (jax.ShapeDtypeStruct((rows, 2 * head_size), jnp.bfloat16),) * reach
    dense = (lowest, q_gain, cosine, sine)
    window = (reach + 1) * rows
    return pl.pallas_call(
        functools.partial(attend_body, reach, slots),
        name="attend_head",
        grid=(1,),
        out_shape=outs,
        in_specs=[smem_spec()]
        + [full_spec(a) for a in dense]
        + [pl.BlockSpec((rows, cols), pick)] * 2
        + [pl.BlockSpec((tile, 2 * head_size), lambda *_, row=row: (row, head)) for _, row in blocks],
        out_specs=[full_spec(o) for o in outs],
        scratch_shapes=[pltpu.VMEM((window, head_size), jnp.bfloat16)] * 2
        + [pltpu.VMEM((window, head_size), jnp.float32)] * 2,
        compiler_params=params(56),
        cost_estimate=cost(10 * rows * window * cols, queries, grads, *outs),
    )(info, *dense, queries, grads, *arrays)


def finish_body(reach, slots, earlier, info, k_gain, cosine, sine, own, *rest):
    arrived = rest[:reach]
    raw_keys = rest[reach : reach + slots]
    before = rest[reach + slots : reach + slots + earlier]
    outs = rest[reach + slots + earlier :]
    result = outs[0]
    head_size = k_gain.shape[1]
    rows = raw_keys[0].shape[0]
    for slot in range(slots):
        place = pl.ds(pl.multiple_of(info[slot] * rows, rows), rows)
        total = own[place, :]
        for part in arrived:
            total = total + part[place, :].astype(jnp.float32)
        values = raw_keys[slot][...].astype(jnp.float32)
        turned = rope_back(total[:, :head_size], cosine[place, :], sine[place, :])
        keys = norm_back(turned, values, inv_rms(values), k_gain[...])
        result[place, :head_size] = keys.astype(jnp.bfloat16)
        result[place, head_size:] = total[:, head_size:].astype(jnp.bfloat16)
    if len(outs) > 1:
        joined, away = outs[1:]
        for head, part in enumerate((*before, result)):
            joined[:, 2 * head * head_size : 2 * (head + 1) * head_size] = part[...]
        for number, slot in enumerate((1, 3)):
            place = pl.ds(pl.multiple_of(info[slot] * rows, 16), rows)
            away[number * rows : (number + 1) * rows, :] = joined[place, :]


def finish(head, info, k_gain, cosine, sine, own, arrived, raw_keys, before=None):
    rows, cols = own.shape
    head_size = k_gain.shape[1]
    slots = len(raw_keys)
    tile = rows // slots
    arrays = [array for array, _ in raw_keys]
    outs = [jax.ShapeDtypeStruct(own.shape, jnp.bfloat16)]
    if before is not None:
        width = cols * (len(before) + 1)
        outs += [jax.ShapeDtypeStruct((count, width), jnp.bfloat16) for count in (rows, 2 * tile)]
    before = before or []
    dense = (k_gain, cosine, sine, own, *arrived)
    results = pl.pallas_call(
        functools.partial(finish_body, len(arrived), slots, len(before)),
        name="finish_kv",
        grid=(1,),
        out_shape=tuple(outs),
        in_specs=[smem_spec()]
        + [full_spec(a) for a in dense]
        + [pl.BlockSpec((tile, head_size), lambda *_, row=row: (row, head)) for _, row in raw_keys]
        + [full_spec(a) for a in before],
        out_specs=tuple(full_spec(o) for o in outs),
        compiler_params=params(56),
        cost_estimate=cost(0, own, *arrived, *outs),
    )(info, *dense, *arrays, *before)
    return list(results)


def weight_body(slots, info, grads, *rest):
    blocks = rest[:slots]
    send, keep, held = rest[slots:]
    rows = blocks[0].shape[0]
    chunk = send.shape[1]
    own = info[slots]
    left = jnp.concatenate([block[...] for block in blocks], axis=0)
    right = jnp.concatenate(
        [grads[pl.ds(pl.multiple_of(info[slot] * rows, rows), rows), :] for slot in range(slots)], axis=0
    )
    held[...] = dot_first(left, right)
    for pair in range(send.shape[0]):
        other = pl.ds(pl.multiple_of((2 * pair + 1 - own) * chunk, 8), chunk)
        mine = pl.ds(pl.multiple_of((2 * pair + own) * chunk, 8), chunk)
        send[pair] = held[other, :].astype(jnp.bfloat16)
        keep[pair] = held[mine, :].astype(jnp.bfloat16)


def weight_terms(info, grads, blocks, chunk):
    rows, width = blocks[0].shape
    cols = grads.shape[1]
    tile = math.lcm(2 * chunk, 128)
    pairs = tile // (2 * chunk)
    out = jax.ShapeDtypeStruct((width // (2 * chunk), chunk, cols), jnp.bfloat16)
    out_spec = pl.BlockSpec((pairs, chunk, cols), lambda step: (step, 0, 0))
    return pl.pallas_call(
        functools.partial(weight_body, len(blocks)),
        name="weight_terms",
        grid=(width // tile,),
        out_shape=(out, out),
        in_specs=[smem_spec(), full_spec(grads)]
        + [pl.BlockSpec((rows, tile), lambda step: (0, step))] * len(blocks),
        out_specs=(out_spec, out_spec),
        scratch_shapes=[pltpu.VMEM((tile, cols), jnp.float32)],
        compiler_params=params(),
        cost_estimate=cost(2 * len(blocks) * rows * width * cols, grads, *blocks, out, out),
    )(info, grads, *blocks)


def add(left, right):
    return left.astype(jnp.float32) + right.astype(jnp.float32)


def split_body(halves, info, *rest):
    keeps, arrivals, outs = rest[: len(halves)], rest[len(halves) : 2 * len(halves)], rest[2 * len(halves) :]
    for index, (cols, outer, inner) in enumerate(halves):
        own = info[index]
        for high in range(outer):
            for low in range(inner):
                for side, target in ((1 - own, outs[2 * index]), (own, outs[2 * index + 1])):
                    place = (high * 2 + side) * inner + low
                    total = add(keeps[index][place, :, cols], arrivals[index][place, :, cols])
                    target[high * inner + low] = total.astype(jnp.bfloat16)


def row_steps(rows):
    return max(n for n in range(1, 5) if rows % (16 * n) == 0) if rows % 16 == 0 else 1


def split_sum(info, keeps, arrivals, halves):
    outs = []
    for keep, (cols, outer, inner) in zip(keeps, halves):
        outs += [jax.ShapeDtypeStruct((outer * inner, keep.shape[1], cols.stop - cols.start), jnp.bfloat16)] * 2
    rows = keeps[0].shape[1]
    steps = row_steps(rows)

    def spec(array):
        return pl.BlockSpec((array.shape[0], rows // steps, array.shape[2]), lambda step: (0, step, 0))

    return pl.pallas_call(
        functools.partial(split_body, halves),
        name="split_sum",
        grid=(steps,),
        out_shape=tuple(outs),
        in_specs=[smem_spec()] + [spec(a) for a in (*keeps, *arrivals)],
        out_specs=tuple(spec(o) for o in outs),
        compiler_params=params(),
        cost_estimate=cost(0, *keeps, *arrivals, *outs),
    )(info, *keeps, *arrivals)


def swap(array, bit):
    size = lax.axis_size("seq")
    return lax.ppermute(array, "seq", [(i, i ^ (1 << bit)) for i in range(size)])


def scatter_sum(send, keep):
    bits = lax.axis_size("seq").bit_length() - 1
    index = lax.axis_index("seq")
    half = keep.shape[2] // 2
    routes = (list(range(1, bits)), list(range(bits - 1, 0, -1)))
    lefts = [list(range(1, bits)), list(range(1, bits))]
    arrival = swap(send, 0)
    keeps, arrivals = [keep, keep], [arrival, arrival]
    cols = [slice(0, half), slice(half, 2 * half)]
    for step in range(bits - 1):
        turn = [route[step] for route in routes]
        halves = []
        for path in range(2):
            place = lefts[path].index(turn[path])
            halves.append((cols[path], 1 << (len(lefts[path]) - 1 - place), 1 << place))
            lefts[path].remove(turn[path])
        info = jnp.stack([(index >> bit) & 1 for bit in turn]).astype(jnp.int32)
        sent_a, kept_a, sent_b, kept_b = split_sum(info, keeps, arrivals, tuple(halves))
        arrivals = [swap(sent_a, turn[0]), swap(sent_b, turn[1])]
        keeps = [kept_a, kept_b]
        cols = [slice(0, half), slice(0, half)]
    return keeps, arrivals


def gather_body(heads, *rest):
    parts = rest[: 4 * heads]
    outs = rest[4 * heads :]
    size = parts[0].shape[2]
    for head in range(heads):
        for side in range(2):
            keep, arrival = parts[4 * head + side], parts[4 * head + 2 + side]
            outs[side][:, head * size : (head + 1) * size] = add(keep[0], arrival[0])


def gather_heads(parts, heads):
    _, rows, cols = parts[0].shape
    steps = row_steps(rows)
    out = jax.ShapeDtypeStruct((rows, cols * heads), jnp.float32)
    out_spec = pl.BlockSpec((rows // steps, cols * heads), lambda step: (step, 0))
    return pl.pallas_call(
        functools.partial(gather_body, heads),
        name="gather_heads",
        grid=(steps,),
        out_shape=(out, out),
        in_specs=[pl.BlockSpec((1, rows // steps, cols), lambda step: (0, step, 0)) for a in parts],
        out_specs=(out_spec, out_spec),
        compiler_params=params(),
        cost_estimate=cost(0, *parts, out, out),
    )(*parts)


def input_terms_body(heads, w_key, w_value, *rest):
    grads, out = rest[:heads], rest[heads]
    size = grads[0].shape[1] // 2
    left = jnp.concatenate([g[:, :size] for g in grads] + [g[:, size:] for g in grads], axis=1)
    right = jnp.concatenate([w_key[...], w_value[...]], axis=1)
    out[...] = dot_last(left, right).astype(jnp.bfloat16)


def input_terms(kv_grads, w_key, w_value, skip):
    width, cols = w_key.shape
    rows = kv_grads[0].shape[0]
    common = math.gcd(skip, width - skip)
    tile = max(t for t in range(128, 1025, 128) if common % t == 0)
    out = jax.ShapeDtypeStruct((rows, width - skip), jnp.bfloat16)
    weight_spec = pl.BlockSpec((tile, cols), lambda step: (step + skip // tile, 0))
    return pl.pallas_call(
        functools.partial(input_terms_body, len(kv_grads)),
        name="input_terms",
        grid=((width - skip) // tile,),
        out_shape=out,
        in_specs=[weight_spec, weight_spec] + [full_spec(g) for g in kv_grads],
        out_specs=pl.BlockSpec((rows, tile), lambda step: (0, step)),
        compiler_params=params(),
        cost_estimate=cost(4 * rows * (width - skip) * cols, out, *kv_grads),
    )(w_key, w_value, *kv_grads)


def pair_body(places, heads, info, w_key, w_value, joined, arrived, *rest):
    pieces = rest[: len(places)]
    away_out, own_out, key_held, value_held, held, own_sems, sems = rest[len(places) :]
    rows, width = own_out.shape
    size = w_key.shape[1] // heads
    own_copies = [
        pltpu.make_async_copy(w_key, key_held, own_sems.at[0]),
        pltpu.make_async_copy(w_value, value_held, own_sems.at[1]),
    ]
    start_all(own_copies)
    copies = piece_copies(places, info[0], pieces, held, sems)
    start_all(copies)
    own_rows = jnp.concatenate(
        [joined[pl.ds(pl.multiple_of(info[1 + number] * rows, rows), rows), :] for number in range(2)], axis=0
    )
    sides = [
        block[:, (2 * head + side) * size : (2 * head + side + 1) * size]
        for block in (own_rows, arrived[...])
        for side in range(2)
        for head in range(heads)
    ]
    left = jnp.concatenate(sides, axis=1)
    wait_all(own_copies)
    wait_all(copies)
    tile = max(t for t in range(128, 1025, 128) if width % t == 0)
    for low in range(0, width, tile):
        span = slice(low, low + tile)
        right = jnp.concatenate([key_held[span, :], value_held[span, :], held[span, :]], axis=1)
        total = dot_last(left, right)
        own_out[:, span] = total[:rows]
        away_out[:, span] = total[rows:].astype(jnp.bfloat16)


def pair_terms(info, joined, arrived, pieces, w_key, w_value, heads):
    rows = arrived.shape[0] // 2
    width, cols = w_key.shape
    places = [(offset, low) for offset, low, _ in pieces]
    arrays = [piece for _, _, piece in pieces]
    outs = (jax.ShapeDtypeStruct((rows, width), jnp.bfloat16), jax.ShapeDtypeStruct((rows, width), jnp.float32))
    return pl.pallas_call(
        functools.partial(pair_body, places, heads),
        name="pair_terms",
        grid=(1,),
        out_shape=outs,
        in_specs=[smem_spec(), any_spec(), any_spec(), full_spec(joined), full_spec(arrived)]
        + [any_spec()] * len(arrays),
        out_specs=tuple(full_spec(o) for o in outs),
        scratch_shapes=[
            pltpu.VMEM((width, cols), jnp.bfloat16),
            pltpu.VMEM((width, cols), jnp.bfloat16),
            pltpu.VMEM((width, 2 * cols), jnp.bfloat16),
            pltpu.SemaphoreType.DMA((2,)),
            pltpu.SemaphoreType.DMA((len(arrays),)),
        ],
        compiler_params=params(56),
        cost_estimate=cost(16 * rows * width * cols, w_key, w_value, *arrays, *outs),
    )(info, w_key, w_value, joined, arrived, *arrays)


def input_grad_body(sums, rest_count, tokens, gain, *rest):
    out = rest[-1]
    values = tokens[...].astype(jnp.float32)
    parts = []
    if sums:
        total = rest[0][...].astype(jnp.float32)
        for piece in rest[1:sums]:
            total = total + piece[...].astype(jnp.float32)
        parts.append(total)
    parts += [piece[...].astype(jnp.float32) for piece in rest[sums : sums + rest_count]]
    grads = jnp.concatenate(parts, axis=1) if len(parts) > 1 else parts[0]
    out[...] = norm_back(grads, values, inv_rms(values), gain[...]).astype(jnp.bfloat16)


def input_grad(tokens, gain, sums, others):
    out = jax.ShapeDtypeStruct(tokens.shape, jnp.bfloat16)
    rows = tokens.shape[0]
    tile = 32 if rows % 32 == 0 else rows
    spec = lambda array: pl.BlockSpec((tile, array.shape[1]), lambda step: (step, 0))
    return pl.pallas_call(
        functools.partial(input_grad_body, len(sums), len(others)),
        name="input_grad",
        grid=(rows // tile,),
        out_shape=out,
        in_specs=[spec(tokens), full_spec(gain)] + [spec(a) for a in (*sums, *others)],
        out_specs=spec(out),
        compiler_params=params(),
        cost_estimate=cost(0, tokens, *sums, *others, out),
    )(tokens, gain, *sums, *others)


def spread_corners(parts):
    half = parts[0].shape[1] // 2
    return [swap(parts[1][:, :half], 2), swap(parts[2][:, half:], 1)]


def spread_end(arrays):
    half = arrays[0].shape[1] // 2
    spots = [(0, 0), (2, 0), (4, 0), (6, 0), (6, half)]
    return [(offset, low, array) for (offset, low), array in zip(spots, arrays)] + [
        (offset + 1, low, swap(array, 0)) for (offset, low), array in zip(spots, arrays)
    ]


def arrival_table(count):
    table = []
    for place in range(count):
        arrivals = []
        for step in range(1, count):
            if place - step >= 0:
                arrivals.append((2 * (step - 1), place - step))
            if place + step < count:
                arrivals.append((2 * (step - 1) + 1, place + step))
        table.append(arrivals)
    return table


def halo_of(key_value, reach):
    seq_count = lax.axis_size("seq")
    sent = []
    for distance in range(1, reach + 1):
        pairs = [(i, i + distance) for i in range(seq_count - distance)]
        sent.append(lax.ppermute(key_value, "seq", pairs))
    return sent


def halo_back(sections):
    seq_count = lax.axis_size("seq")
    back = []
    for section, array in enumerate(sections):
        distance = len(sections) - section
        pairs = [(i + distance, i) for i in range(seq_count - distance)]
        back.append(lax.ppermute(array, "seq", pairs))
    return back


def shards_general(tokens, dense, rope_rows, lowest, raw_queries, out_grad, w_key, w_value, reach):
    gain_row, q_row, k_row = dense
    cosine, sine = rope_rows
    tp_count = lax.axis_size("tp")
    place = lax.axis_index("tp").astype(jnp.int32)
    rows = tokens.shape[0]
    head_size = q_row.shape[1]
    kv_heads = w_key.shape[1] // head_size
    table = arrival_table(tp_count)
    picks = jnp.array(table, dtype=jnp.int32).reshape(tp_count, tp_count - 1, 2)
    picks = lax.dynamic_index_in_dim(picks, place, 0, keepdims=False)
    infos = [jnp.stack([jnp.int32(0), place])] + [picks[i] for i in range(tp_count - 1)]
    slot_places = jnp.concatenate([place[None], picks[:, 1]])
    normed_blocks, kv_blocks, raw_keys = [], [], []
    halo = [[] for _ in range(reach)]
    arrivals = []
    going_up = going_down = tokens
    for slot in range(tp_count):
        candidates = [tokens] if slot == 0 else list(arrivals)
        if slot < tp_count - 1:
            going_up = lax.ppermute(going_up, "tp", [(i, i + 1) for i in range(slot, tp_count - 1)])
            going_down = lax.ppermute(going_down, "tp", [(i + 1, i) for i in range(tp_count - 1 - slot)])
            arrivals += [going_up, going_down]
        key_value, keys, normed = project(infos[slot], candidates, gain_row, k_row, cosine, sine, w_key, w_value)
        normed_blocks.append(normed)
        kv_blocks.append(key_value)
        raw_keys.append((keys, 0))
        for distance, sent in enumerate(halo_of(key_value, reach)):
            halo[distance].append((sent, 0))
    blocks = [block for distance in range(reach, 0, -1) for block in halo[distance - 1]]
    blocks += [(block, 0) for block in kv_blocks]
    query_parts, kv_grads = [], []
    for head in range(kv_heads):
        outs = attend(head, kv_heads, reach, slot_places, lowest, q_row, cosine, sine, raw_queries, out_grad, blocks)
        query_parts.append(outs[0])
        back = halo_back(outs[2:])
        kv_grads += finish(head, slot_places, k_row, cosine, sine, outs[1], back, raw_keys)
    grad_queries = jnp.concatenate(query_parts, axis=1)
    partial_sum = input_terms(kv_grads, w_key, w_value, 0)
    summed_part = lax.psum_scatter(partial_sum, "tp", scatter_dimension=0, tiled=True)
    grad_x = input_grad(tokens, gain_row, [], [summed_part])
    left = jnp.concatenate(normed_blocks, axis=0)
    order = (slot_places[:, None] * rows + jnp.arange(rows, dtype=jnp.int32)[None, :]).reshape(-1)
    joined = [g[:, :head_size] for g in kv_grads] + [g[:, head_size:] for g in kv_grads]
    right = jnp.take(jnp.concatenate(joined, axis=1), order, axis=0)
    summed = lax.psum_scatter(dot_first(left, right), "seq", scatter_dimension=0, tiled=True)
    return (grad_x, grad_queries, summed[:, : w_key.shape[1]], summed[:, w_key.shape[1] :])


def trade(array, distance):
    return lax.ppermute(array, "tp", [(i, i ^ distance) for i in range(lax.axis_size("tp"))])


def shards_paired(tokens, dense, rope_rows, lowest, raw_queries, out_grad, w_key, w_value, reach):
    gain_row, q_row, k_row = dense
    cosine, sine = rope_rows
    seq_count = lax.axis_size("seq")
    seq_index = lax.axis_index("seq").astype(jnp.int32)
    place = lax.axis_index("tp").astype(jnp.int32)
    width, cols = w_key.shape
    head_size = q_row.shape[1]
    kv_heads = cols // head_size
    chunk = width // seq_count
    zero = jnp.zeros_like(place)
    slot_places = jnp.stack([place, place ^ 1, place ^ 2, place ^ 3])

    distant = trade(tokens, 2)
    own_slice = jnp.concatenate(
        [lax.dynamic_slice_in_dim(weight, seq_index * chunk, chunk, 0) for weight in (w_key, w_value)], axis=1
    )

    partner_slice = trade(own_slice, 1)
    spread = [partner_slice, swap(partner_slice, 1), swap(partner_slice, 2)]
    info = jnp.stack([zero, place])
    kv_0, keys_0, normed_0 = project(
        info, [after(tokens, partner_slice)], gain_row, k_row, cosine, sine, w_key, w_value
    )
    halo_0 = halo_of(kv_0, reach)
    partner_normed_0 = trade(normed_0, 1)
    spread += spread_corners(after(spread, normed_0))
    pieces = spread_end(spread)
    info = jnp.stack([seq_index, place, place ^ 2])
    kv_2, keys_2, normed_2, far_kv, far_keys = project_pair(
        info, normed_0, after(distant, halo_0), gain_row, k_row, cosine, sine, w_key, w_value, pieces
    )
    arrived_kv = trade(far_kv, 1)
    halo_2 = halo_of(kv_2, reach)
    halo_far = halo_of(arrived_kv, reach)
    arrived_keys = trade(after(far_keys, arrived_kv), 1)
    partner_normed_2 = trade(after(normed_2, (arrived_kv, partner_normed_0)), 1)

    blocks = []
    for distance in range(reach, 0, -1):
        outer = halo_far[distance - 1]
        blocks += [(halo_0[distance - 1], 0), (outer, 0), (halo_2[distance - 1], 0), (outer, 1)]
    blocks += [(kv_0, 0), (arrived_kv, 0), (kv_2, 0), (arrived_kv, 1)]
    raw_keys = [(keys_0, 0), (arrived_keys, 0), (keys_2, 0), (arrived_keys, 1)]
    normed = [normed_0, partner_normed_0, normed_2, partner_normed_2]
    weight_info = jnp.concatenate([slot_places, (seq_index & 1)[None]])
    query_parts, kv_grads, terms = [], [], []
    for head in range(kv_heads):
        outs = attend(head, kv_heads, reach, slot_places, lowest, q_row, cosine, sine, raw_queries, out_grad, blocks)
        query_parts.append(outs[0])
        back = halo_back(outs[2:])
        before = kv_grads if head == kv_heads - 1 else None
        results = finish(head, slot_places, k_row, cosine, sine, outs[1], back, raw_keys, before=before)
        kv_grads = kv_grads + results[:1]
        terms.append(weight_terms(weight_info, results[0], normed, chunk))
    grad_queries = jnp.concatenate(query_parts, axis=1)

    joined, away = results[1:]
    arrived = after(trade(away, 1), terms)
    info = jnp.stack([seq_index, place, place ^ 2])
    away_terms, own_terms = pair_terms(info, joined, arrived, pieces, w_key, w_value, kv_heads)
    other_terms = trade(away_terms, 2)
    grad_x = input_grad(tokens, gain_row, [own_terms, other_terms], [])

    parts = []
    for send, keep in terms:
        keeps, comings = scatter_sum(send, keep)
        parts += [*keeps, *comings]
    grad_wk, grad_wv = gather_heads(parts, kv_heads)
    return (grad_x, grad_queries, grad_wk, grad_wv)


def shards(tokens, in_gain, raw_queries, w_key, w_value, q_gain, k_gain, doc_lengths, out_grad):
    seq_count = lax.axis_size("seq")
    tp_count = lax.axis_size("tp")
    rows, width = tokens.shape
    shard_rows = rows * tp_count
    reach = (WINDOW - 2) // shard_rows + 1
    first_row = lax.axis_index("seq") * shard_rows
    positions = first_row + jnp.arange(shard_rows, dtype=jnp.int32)
    begins = doc_begin(doc_lengths, positions)
    rope_rows = rope_tables(positions - begins, q_gain.shape[0])
    lowest = jnp.maximum(begins, positions - (WINDOW - 1)) - (first_row - reach * shard_rows)
    dense = (in_gain[None, :], q_gain[None, :], k_gain[None, :])
    chunk = width // seq_count
    paired = (
        tp_count == 1 << 2
        and seq_count == 1 << 3
        and chunk % 16 == 0
        and width % math.lcm(2 * chunk, 128) == 0
    )
    run = shards_paired if paired else shards_general
    return run(tokens, dense, rope_rows, lowest[:, None], raw_queries, out_grad, w_key, w_value, reach)


def solution(mesh):
    placed = (
        P(("seq", "tp"), None),
        P(),
        P("seq", "tp"),
        P(None, "tp"),
        P(None, "tp"),
        P(),
        P(),
        P(),
        P("seq", "tp"),
    )
    return jax.shard_map(
        shards,
        mesh=mesh,
        in_specs=placed,
        out_specs=(P(("seq", "tp"), None), P("seq", "tp"), P("seq", "tp"), P("seq", "tp")),
        check_vma=False,
    )
```

```python
import functools
import math

import jax
import jax.numpy as jnp
from jax import lax
from jax.experimental import pallas as pl
from jax.experimental.pallas import tpu as pltpu
from jax.sharding import PartitionSpec as P

WINDOW = 1024
EPSILON = 1e-06
QUERY_SCALE = 168.0 ** (-0.5)
ROPE_BASE = 10000.0
SMEM = pltpu.SMEM


def doc_begin(doc_lengths, positions):
    endings = jnp.cumsum(doc_lengths, dtype=jnp.int32)
    starts = endings - doc_lengths
    inside = starts[None, :] <= positions[:, None]
    return jnp.max(jnp.where(inside, starts[None, :], jnp.zeros_like(starts)[None, :]), axis=1)


def rope_tables(offsets, head_size):
    half_size = head_size // 2
    powers = jnp.arange(half_size, dtype=jnp.float32) * (2.0 / head_size)
    frequency = ROPE_BASE ** (-powers)
    angles = offsets.astype(jnp.float32)[:, None] * frequency[None, :]
    cosine = jnp.cos(angles)
    sine = jnp.sin(angles)
    return jnp.concatenate([cosine, cosine], axis=1), jnp.concatenate([-sine, sine], axis=1)


def half_turn(values):
    return pltpu.roll(values, values.shape[-1] // 2, values.ndim - 1)


def rope(values, cosine, sine):
    return values * cosine + half_turn(values) * sine


def rope_back(grads, cosine, sine):
    return grads * cosine + half_turn(grads * sine)


def inv_rms(values):
    return lax.rsqrt(jnp.mean(values * values, axis=-1, keepdims=True) + EPSILON)


def norm_back(grads, values, scale, gain):
    scaled = grads * gain
    mean = jnp.mean(values * scaled, axis=-1, keepdims=True)
    return scale * scaled - values * (scale * scale * scale * mean)


def dot_last(left, right):
    return lax.dot_general(left, right, (((1,), (1,)), ((), ())), preferred_element_type=jnp.float32)


def dot_first(left, right):
    return lax.dot_general(left, right, (((0,), (0,)), ((), ())), preferred_element_type=jnp.float32)


def full_spec(array):
    return pl.BlockSpec(array.shape, lambda *_: (0,) * array.ndim)


def any_spec():
    return pl.BlockSpec(memory_space=pl.ANY)


def smem_spec():
    return pl.BlockSpec(memory_space=SMEM)


def after(value, others):
    return lax.optimization_barrier((value, others))[0]


def cost(flops, *arrays):
    size = sum(math.prod(a.shape) * jnp.dtype(a.dtype).itemsize for a in arrays)
    return pl.CostEstimate(flops=flops, bytes_accessed=size, transcendentals=0)


def params(megabytes=30):
    return pltpu.CompilerParams(vmem_limit_bytes=megabytes * 1024 * 1024)


def start_all(copies):
    for copy in copies:
        copy.start()


def wait_all(copies):
    for copy in copies:
        copy.wait()


def piece_copies(places, seq_index, arrays, target, sems):
    copies = []
    for number, (offset, low) in enumerate(places):
        rows, cols = arrays[number].shape
        start = pl.multiple_of(jnp.bitwise_xor(seq_index, offset) * rows, 16)
        slot = target.at[pl.ds(start, rows), pl.ds(low, cols)]
        copies.append(pltpu.make_async_copy(arrays[number], slot, sems.at[number]))
    return copies


def store_heads(key_value, raw_keys, rows, keys, values, k_gain, cos_rows, sin_rows):
    head_size = k_gain.shape[1]
    raw_keys[rows, :] = keys.astype(raw_keys.dtype)
    for head in range(keys.shape[1] // head_size):
        cols = slice(head * head_size, (head + 1) * head_size)
        low = 2 * head * head_size
        head_keys = keys[:, cols]
        turned = rope(head_keys * inv_rms(head_keys) * k_gain[...], cos_rows, sin_rows)
        key_value[rows, low : low + head_size] = turned.astype(jnp.bfloat16)
        key_value[rows, low + head_size : low + 2 * head_size] = values[:, cols].astype(jnp.bfloat16)


def project_body(count, info, gain, k_gain, cosine, sine, w_key, w_value, *rest):
    blocks = rest[:count]
    key_value, raw_keys, normed, held, key_held, value_held, sems = rest[count:]
    rows = held.shape[0]

    def block_copy(index):
        return pltpu.make_async_copy(blocks[index], held, sems.at[2])

    for index in range(count):
        pl.when(info[0] == index)(lambda index=index: block_copy(index).start())
    own_copies = [
        pltpu.make_async_copy(w_key, key_held, sems.at[0]),
        pltpu.make_async_copy(w_value, value_held, sems.at[1]),
    ]
    start_all(own_copies)
    for index in range(count):
        pl.when(info[0] == index)(lambda index=index: block_copy(index).wait())
    values = held[...].astype(jnp.float32)
    normed[...] = (values * inv_rms(values) * gain[...]).astype(jnp.bfloat16)
    place = pl.ds(pl.multiple_of(info[1] * rows, rows), rows)
    wait_all(own_copies)
    keys = jnp.dot(normed[...], key_held[...], preferred_element_type=jnp.float32)
    vals = jnp.dot(normed[...], value_held[...], preferred_element_type=jnp.float32)
    store_heads(key_value, raw_keys, slice(0, rows), keys, vals, k_gain, cosine[place, :], sine[place, :])


def project(info, blocks, in_gain, k_gain, cosine, sine, w_key, w_value):
    rows, width = blocks[0].shape
    cols = w_key.shape[1]
    outs = [
        jax.ShapeDtypeStruct((rows, 2 * cols), jnp.bfloat16),
        jax.ShapeDtypeStruct((rows, cols), jnp.bfloat16),
        jax.ShapeDtypeStruct((rows, width), jnp.bfloat16),
    ]
    scratch = [
        pltpu.VMEM((rows, width), jnp.bfloat16),
        pltpu.VMEM((width, cols), jnp.bfloat16),
        pltpu.VMEM((width, cols), jnp.bfloat16),
        pltpu.SemaphoreType.DMA((3,)),
    ]
    dense = (in_gain, k_gain, cosine, sine)
    return pl.pallas_call(
        functools.partial(project_body, len(blocks)),
        name="project_block",
        grid=(1,),
        out_shape=tuple(outs),
        in_specs=[smem_spec()] + [full_spec(a) for a in dense] + [any_spec()] * (2 + len(blocks)),
        out_specs=tuple(full_spec(o) for o in outs),
        scratch_shapes=scratch,
        compiler_params=params(56),
        cost_estimate=cost(4 * rows * width * cols, blocks[0], w_key, w_value, *outs),
    )(info, *dense, w_key, w_value, *blocks)


def project_pair_body(places, info, gain, k_gain, cosine, sine, w_key, w_value, ready, block, *rest):
    pieces = rest[: len(places)]
    key_value, raw_keys, normed, far_key_value, far_keys = rest[len(places) : len(places) + 5]
    held, left, key_held, value_held, far_held, sems, far_sems = rest[len(places) + 5 :]
    rows, width = held.shape
    cols = w_key.shape[1]
    block_copy = pltpu.make_async_copy(block, held, sems.at[2])
    block_copy.start()
    ready_copy = pltpu.make_async_copy(ready, left.at[pl.ds(0, rows)], sems.at[3])
    ready_copy.start()
    far_copies = piece_copies(places, info[0], pieces, far_held, far_sems)
    start_all(far_copies)
    own_copies = [
        pltpu.make_async_copy(w_key, key_held, sems.at[0]),
        pltpu.make_async_copy(w_value, value_held, sems.at[1]),
    ]
    start_all(own_copies)
    block_copy.wait()
    values = held[...].astype(jnp.float32)
    normed[...] = (values * inv_rms(values) * gain[...]).astype(jnp.bfloat16)
    ready_copy.wait()
    left[rows:, :] = normed[...]
    wait_all(far_copies)
    both = jnp.dot(left[...], far_held[...], preferred_element_type=jnp.float32)
    for number in range(2):
        place = pl.ds(pl.multiple_of(info[1 + number] * rows, rows), rows)
        span = slice(number * rows, (number + 1) * rows)
        part = both[span]
        store_heads(
            far_key_value, far_keys, span, part[:, :cols], part[:, cols:], k_gain, cosine[place, :], sine[place, :]
        )
    place = pl.ds(pl.multiple_of(info[2] * rows, rows), rows)
    wait_all(own_copies)
    keys = jnp.dot(normed[...], key_held[...], preferred_element_type=jnp.float32)
    vals = jnp.dot(normed[...], value_held[...], preferred_element_type=jnp.float32)
    store_heads(key_value, raw_keys, slice(0, rows), keys, vals, k_gain, cosine[place, :], sine[place, :])


def project_pair(info, ready, block, in_gain, k_gain, cosine, sine, w_key, w_value, pieces):
    rows, width = block.shape
    cols = w_key.shape[1]
    places = [(offset, low) for offset, low, _ in pieces]
    arrays = [piece for _, _, piece in pieces]
    outs = tuple(
        jax.ShapeDtypeStruct(shape, jnp.bfloat16)
        for shape in ((rows, 2 * cols), (rows, cols), (rows, width), (2 * rows, 2 * cols), (2 * rows, cols))
    )
    dense = (in_gain, k_gain, cosine, sine)
    return pl.pallas_call(
        functools.partial(project_pair_body, places),
        name="project_pair",
        grid=(1,),
        out_shape=outs,
        in_specs=[smem_spec()] + [full_spec(a) for a in dense] + [any_spec()] * (4 + len(arrays)),
        out_specs=tuple(full_spec(o) for o in outs),
        scratch_shapes=[
            pltpu.VMEM((rows, width), jnp.bfloat16),
            pltpu.VMEM((2 * rows, width), jnp.bfloat16),
            pltpu.VMEM((width, cols), jnp.bfloat16),
            pltpu.VMEM((width, cols), jnp.bfloat16),
            pltpu.VMEM((width, 2 * cols), jnp.bfloat16),
            pltpu.SemaphoreType.DMA((4,)),
            pltpu.SemaphoreType.DMA((len(arrays),)),
        ],
        compiler_params=params(56),
        cost_estimate=cost(12 * rows * width * cols, block, w_key, w_value, *arrays, *outs),
    )(info, *dense, w_key, w_value, ready, block, *arrays)


def attend_body(reach, slots, info, lowest, q_gain, cosine, sine, queries, grads, *rest):
    blocks = rest[: (reach + 1) * slots]
    rest = rest[(reach + 1) * slots :]
    query_grads, own = rest[0], rest[1]
    far = rest[2 : 2 + reach]
    keys, values, key_sum, value_sum = rest[2 + reach :]
    rows = queries.shape[0]
    head_size = q_gain.shape[1]
    group = queries.shape[1] // head_size
    tile = blocks[0].shape[0]
    margin = reach * rows
    for slot in range(slots):
        start = info[slot] * tile
        for section in range(reach + 1):
            place = pl.ds(pl.multiple_of(section * rows + start, tile), tile)
            block = blocks[section * slots + slot]
            keys[place, :] = block[:, :head_size]
            values[place, :] = block[:, head_size:]
    key_sum[...] = jnp.zeros_like(key_sum)
    value_sum[...] = jnp.zeros_like(value_sum)
    for index in range(rows // tile):
        top = index * tile
        low = max(0, (top + margin - WINDOW + 1) // tile * tile)
        high = top + tile + margin
        width = high - low
        cos_rows = cosine[top : top + tile, :]
        sin_rows = sine[top : top + tile, :]
        raw = []
        scales = []
        turned = []
        for head in range(group):
            raw.append(queries[top : top + tile, head * head_size : (head + 1) * head_size].astype(jnp.float32))
            scales.append(inv_rms(raw[head]))
            turned.append(rope(raw[head] * scales[head] * q_gain[...], cos_rows, sin_rows) * QUERY_SCALE)
        query_rows = jnp.concatenate(turned, axis=0).astype(jnp.bfloat16)
        grad_rows = jnp.concatenate(
            [grads[top : top + tile, head * head_size : (head + 1) * head_size] for head in range(group)], axis=0
        )
        key_rows = keys[low:high, :]
        value_rows = values[low:high, :]
        columns = lax.broadcasted_iota(jnp.int32, (tile, width), 1) + low
        last = lax.broadcasted_iota(jnp.int32, (tile, width), 0) + (top + margin)
        allowed = (columns >= lowest[top : top + tile, :]) & (columns <= last)
        scores = dot_last(query_rows, key_rows).reshape(group, tile, width)
        exps = jnp.where(allowed[None], jnp.exp(scores), 0.0)
        probs = exps * (1.0 / jnp.sum(exps, axis=-1, keepdims=True))
        weights = probs.astype(jnp.bfloat16)
        along = dot_last(grad_rows, value_rows).reshape(group, tile, width)
        deltas = jnp.sum(weights.astype(jnp.float32) * along, axis=-1, keepdims=True)
        slopes = (probs * (along - deltas)).astype(jnp.bfloat16).reshape(group * tile, width)
        weights = weights.reshape(group * tile, width)
        key_sum[low:high, :] += dot_first(slopes, query_rows)
        value_sum[low:high, :] += dot_first(weights, grad_rows)
        back = jnp.dot(slopes, key_rows, preferred_element_type=jnp.float32)
        for head in range(group):
            turned_back = rope_back(back[head * tile : (head + 1) * tile] * QUERY_SCALE, cos_rows, sin_rows)
            result = norm_back(turned_back, raw[head], scales[head], q_gain[...])
            query_grads[top : top + tile, head * head_size : (head + 1) * head_size] = result.astype(jnp.bfloat16)
    for section in range(reach):
        span = slice(section * rows, (section + 1) * rows)
        far[section][:, :head_size] = key_sum[span, :].astype(jnp.bfloat16)
        far[section][:, head_size:] = value_sum[span, :].astype(jnp.bfloat16)
    own[:, :head_size] = key_sum[margin:, :]
    own[:, head_size:] = value_sum[margin:, :]


def attend(head, kv_heads, reach, info, lowest, q_gain, cosine, sine, queries, grads, blocks):
    rows = queries.shape[0]
    head_size = q_gain.shape[1]
    slots = len(blocks) // (reach + 1)
    tile = rows // slots
    cols = queries.shape[1] // kv_heads
    pick = lambda *_: (0, head)
    arrays = [array for array, _ in blocks]
    outs = (
        jax.ShapeDtypeStruct((rows, cols), jnp.bfloat16),
        jax.ShapeDtypeStruct((rows, 2 * head_size), jnp.float32),
    ) + (jax.ShapeDtypeStruct((rows, 2 * head_size), jnp.bfloat16),) * reach
    dense = (lowest, q_gain, cosine, sine)
    window = (reach + 1) * rows
    return pl.pallas_call(
        functools.partial(attend_body, reach, slots),
        name="attend_head",
        grid=(1,),
        out_shape=outs,
        in_specs=[smem_spec()]
        + [full_spec(a) for a in dense]
        + [pl.BlockSpec((rows, cols), pick)] * 2
        + [pl.BlockSpec((tile, 2 * head_size), lambda *_, row=row: (row, head)) for _, row in blocks],
        out_specs=[full_spec(o) for o in outs],
        scratch_shapes=[pltpu.VMEM((window, head_size), jnp.bfloat16)] * 2
        + [pltpu.VMEM((window, head_size), jnp.float32)] * 2,
        compiler_params=params(56),
        cost_estimate=cost(10 * rows * window * cols, queries, grads, *outs),
    )(info, *dense, queries, grads, *arrays)


def finish_body(reach, slots, earlier, info, k_gain, cosine, sine, own, *rest):
    arrived = rest[:reach]
    raw_keys = rest[reach : reach + slots]
    before = rest[reach + slots : reach + slots + earlier]
    outs = rest[reach + slots + earlier :]
    result = outs[0]
    head_size = k_gain.shape[1]
    rows = raw_keys[0].shape[0]
    for slot in range(slots):
        place = pl.ds(pl.multiple_of(info[slot] * rows, rows), rows)
        total = own[place, :]
        for part in arrived:
            total = total + part[place, :].astype(jnp.float32)
        values = raw_keys[slot][...].astype(jnp.float32)
        turned = rope_back(total[:, :head_size], cosine[place, :], sine[place, :])
        keys = norm_back(turned, values, inv_rms(values), k_gain[...])
        result[place, :head_size] = keys.astype(jnp.bfloat16)
        result[place, head_size:] = total[:, head_size:].astype(jnp.bfloat16)
    if len(outs) > 1:
        joined, away = outs[1:]
        for head, part in enumerate((*before, result)):
            joined[:, 2 * head * head_size : 2 * (head + 1) * head_size] = part[...]
        for number, slot in enumerate((1, 3)):
            place = pl.ds(pl.multiple_of(info[slot] * rows, 16), rows)
            away[number * rows : (number + 1) * rows, :] = joined[place, :]


def finish(head, info, k_gain, cosine, sine, own, arrived, raw_keys, before=None):
    rows, cols = own.shape
    head_size = k_gain.shape[1]
    slots = len(raw_keys)
    tile = rows // slots
    arrays = [array for array, _ in raw_keys]
    outs = [jax.ShapeDtypeStruct(own.shape, jnp.bfloat16)]
    if before is not None:
        width = cols * (len(before) + 1)
        outs += [jax.ShapeDtypeStruct((count, width), jnp.bfloat16) for count in (rows, 2 * tile)]
    before = before or []
    dense = (k_gain, cosine, sine, own, *arrived)
    results = pl.pallas_call(
        functools.partial(finish_body, len(arrived), slots, len(before)),
        name="finish_kv",
        grid=(1,),
        out_shape=tuple(outs),
        in_specs=[smem_spec()]
        + [full_spec(a) for a in dense]
        + [pl.BlockSpec((tile, head_size), lambda *_, row=row: (row, head)) for _, row in raw_keys]
        + [full_spec(a) for a in before],
        out_specs=tuple(full_spec(o) for o in outs),
        compiler_params=params(56),
        cost_estimate=cost(0, own, *arrived, *outs),
    )(info, *dense, *arrays, *before)
    return list(results)


def weight_body(slots, info, grads, *rest):
    blocks = rest[:slots]
    send, keep, held = rest[slots:]
    rows = blocks[0].shape[0]
    chunk = send.shape[1]
    own = info[slots]
    left = jnp.concatenate([block[...] for block in blocks], axis=0)
    right = jnp.concatenate(
        [grads[pl.ds(pl.multiple_of(info[slot] * rows, rows), rows), :] for slot in range(slots)], axis=0
    )
    held[...] = dot_first(left, right)
    for pair in range(send.shape[0]):
        other = pl.ds(pl.multiple_of((2 * pair + 1 - own) * chunk, 8), chunk)
        mine = pl.ds(pl.multiple_of((2 * pair + own) * chunk, 8), chunk)
        send[pair] = held[other, :].astype(jnp.bfloat16)
        keep[pair] = held[mine, :].astype(jnp.bfloat16)


def weight_terms(info, grads, blocks, chunk):
    rows, width = blocks[0].shape
    cols = grads.shape[1]
    tile = math.lcm(2 * chunk, 128)
    pairs = tile // (2 * chunk)
    out = jax.ShapeDtypeStruct((width // (2 * chunk), chunk, cols), jnp.bfloat16)
    out_spec = pl.BlockSpec((pairs, chunk, cols), lambda step: (step, 0, 0))
    return pl.pallas_call(
        functools.partial(weight_body, len(blocks)),
        name="weight_terms",
        grid=(width // tile,),
        out_shape=(out, out),
        in_specs=[smem_spec(), full_spec(grads)]
        + [pl.BlockSpec((rows, tile), lambda step: (0, step))] * len(blocks),
        out_specs=(out_spec, out_spec),
        scratch_shapes=[pltpu.VMEM((tile, cols), jnp.float32)],
        compiler_params=params(),
        cost_estimate=cost(0),
    )(info, grads, *blocks)


def add(left, right):
    return left.astype(jnp.float32) + right.astype(jnp.float32)


def split_body(halves, info, *rest):
    keeps, arrivals, outs = rest[: len(halves)], rest[len(halves) : 2 * len(halves)], rest[2 * len(halves) :]
    for index, (cols, outer, inner) in enumerate(halves):
        own = info[index]
        for high in range(outer):
            for low in range(inner):
                for side, target in ((1 - own, outs[2 * index]), (own, outs[2 * index + 1])):
                    place = (high * 2 + side) * inner + low
                    total = add(keeps[index][place, :, cols], arrivals[index][place, :, cols])
                    target[high * inner + low] = total.astype(jnp.bfloat16)


def row_steps(rows):
    return max(n for n in range(1, 5) if rows % (16 * n) == 0) if rows % 16 == 0 else 1


def split_sum(info, keeps, arrivals, halves):
    outs = []
    for keep, (cols, outer, inner) in zip(keeps, halves):
        outs += [jax.ShapeDtypeStruct((outer * inner, keep.shape[1], cols.stop - cols.start), jnp.bfloat16)] * 2
    rows = keeps[0].shape[1]
    steps = row_steps(rows)

    def spec(array):
        return pl.BlockSpec((array.shape[0], rows // steps, array.shape[2]), lambda step: (0, step, 0))

    return pl.pallas_call(
        functools.partial(split_body, halves),
        name="split_sum",
        grid=(steps,),
        out_shape=tuple(outs),
        in_specs=[smem_spec()] + [spec(a) for a in (*keeps, *arrivals)],
        out_specs=tuple(spec(o) for o in outs),
        compiler_params=params(),
        cost_estimate=cost(0),
    )(info, *keeps, *arrivals)


def swap(array, bit):
    size = lax.axis_size("seq")
    return lax.ppermute(array, "seq", [(i, i ^ (1 << bit)) for i in range(size)])


def scatter_sum(send, keep):
    bits = lax.axis_size("seq").bit_length() - 1
    index = lax.axis_index("seq")
    half = keep.shape[2] // 2
    routes = (list(range(1, bits)), list(range(bits - 1, 0, -1)))
    lefts = [list(range(1, bits)), list(range(1, bits))]
    arrival = swap(send, 0)
    keeps, arrivals = [keep, keep], [arrival, arrival]
    cols = [slice(0, half), slice(half, 2 * half)]
    for step in range(bits - 1):
        turn = [route[step] for route in routes]
        halves = []
        for path in range(2):
            place = lefts[path].index(turn[path])
            halves.append((cols[path], 1 << (len(lefts[path]) - 1 - place), 1 << place))
            lefts[path].remove(turn[path])
        info = jnp.stack([(index >> bit) & 1 for bit in turn]).astype(jnp.int32)
        sent_a, kept_a, sent_b, kept_b = split_sum(info, keeps, arrivals, tuple(halves))
        arrivals = [swap(sent_a, turn[0]), swap(sent_b, turn[1])]
        keeps = [kept_a, kept_b]
        cols = [slice(0, half), slice(0, half)]
    return keeps, arrivals


def gather_body(heads, *rest):
    parts = rest[: 4 * heads]
    outs = rest[4 * heads :]
    size = parts[0].shape[2]
    for head in range(heads):
        for side in range(2):
            keep, arrival = parts[4 * head + side], parts[4 * head + 2 + side]
            outs[side][:, head * size : (head + 1) * size] = add(keep[0], arrival[0])


def gather_heads(parts, heads):
    _, rows, cols = parts[0].shape
    steps = row_steps(rows)
    out = jax.ShapeDtypeStruct((rows, cols * heads), jnp.float32)
    out_spec = pl.BlockSpec((rows // steps, cols * heads), lambda step: (step, 0))
    return pl.pallas_call(
        functools.partial(gather_body, heads),
        name="gather_heads",
        grid=(steps,),
        out_shape=(out, out),
        in_specs=[pl.BlockSpec((1, rows // steps, cols), lambda step: (0, step, 0)) for a in parts],
        out_specs=(out_spec, out_spec),
        compiler_params=params(),
        cost_estimate=cost(0),
    )(*parts)


def input_terms_body(heads, w_key, w_value, *rest):
    grads, out = rest[:heads], rest[heads]
    size = grads[0].shape[1] // 2
    left = jnp.concatenate([g[:, :size] for g in grads] + [g[:, size:] for g in grads], axis=1)
    right = jnp.concatenate([w_key[...], w_value[...]], axis=1)
    out[...] = dot_last(left, right).astype(jnp.bfloat16)


def input_terms(kv_grads, w_key, w_value, skip):
    width, cols = w_key.shape
    rows = kv_grads[0].shape[0]
    common = math.gcd(skip, width - skip)
    tile = max(t for t in range(128, 1025, 128) if common % t == 0)
    out = jax.ShapeDtypeStruct((rows, width - skip), jnp.bfloat16)
    weight_spec = pl.BlockSpec((tile, cols), lambda step: (step + skip // tile, 0))
    return pl.pallas_call(
        functools.partial(input_terms_body, len(kv_grads)),
        name="input_terms",
        grid=((width - skip) // tile,),
        out_shape=out,
        in_specs=[weight_spec, weight_spec] + [full_spec(g) for g in kv_grads],
        out_specs=pl.BlockSpec((rows, tile), lambda step: (0, step)),
        compiler_params=params(),
        cost_estimate=cost(4 * rows * (width - skip) * cols, out, *kv_grads),
    )(w_key, w_value, *kv_grads)


def pair_body(places, heads, info, w_key, w_value, joined, arrived, *rest):
    pieces = rest[: len(places)]
    away_out, own_out, key_held, value_held, held, own_sems, sems = rest[len(places) :]
    rows, width = own_out.shape
    size = w_key.shape[1] // heads
    half = width // 2
    slice_rows = pieces[0].shape[0]
    split = half // slice_rows
    first = info[0] // split
    copies = piece_copies(places, info[0], pieces, held, sems)
    spans, groups = [], []
    for number in range(2):
        span = pl.ds(pl.multiple_of(jnp.bitwise_xor(first, number) * half, 128), half)
        spans.append(span)
        groups.append(
            [
                pltpu.make_async_copy(w_key.at[span, :], key_held.at[span, :], own_sems.at[2 * number]),
                pltpu.make_async_copy(w_value.at[span, :], value_held.at[span, :], own_sems.at[2 * number + 1]),
            ]
            + [copy for copy, (offset, _) in zip(copies, places) if offset // split == number]
        )
        start_all(groups[number])
    own_rows = jnp.concatenate(
        [joined[pl.ds(pl.multiple_of(info[1 + number] * rows, rows), rows), :] for number in range(2)], axis=0
    )
    sides = [
        block[:, (2 * head + side) * size : (2 * head + side + 1) * size]
        for block in (own_rows, arrived[...])
        for side in range(2)
        for head in range(heads)
    ]
    left = jnp.concatenate(sides, axis=1)
    for span, group in zip(spans, groups):
        wait_all(group)
        right = jnp.concatenate([key_held[span, :], value_held[span, :], held[span, :]], axis=1)
        total = dot_last(left, right).astype(jnp.bfloat16)
        own_out[:, span] = total[:rows]
        away_out[:, span] = total[rows:]


def pair_terms(info, joined, arrived, pieces, w_key, w_value, heads):
    rows = arrived.shape[0] // 2
    width, cols = w_key.shape
    places = [(offset, low) for offset, low, _ in pieces]
    arrays = [piece for _, _, piece in pieces]
    outs = (jax.ShapeDtypeStruct((rows, width), jnp.bfloat16),) * 2
    return pl.pallas_call(
        functools.partial(pair_body, places, heads),
        name="pair_terms",
        grid=(1,),
        out_shape=outs,
        in_specs=[smem_spec(), any_spec(), any_spec(), full_spec(joined), full_spec(arrived)]
        + [any_spec()] * len(arrays),
        out_specs=tuple(full_spec(o) for o in outs),
        scratch_shapes=[
            pltpu.VMEM((width, cols), jnp.bfloat16),
            pltpu.VMEM((width, cols), jnp.bfloat16),
            pltpu.VMEM((width, 2 * cols), jnp.bfloat16),
            pltpu.SemaphoreType.DMA((4,)),
            pltpu.SemaphoreType.DMA((len(arrays),)),
        ],
        compiler_params=params(56),
        cost_estimate=cost(16 * rows * width * cols, w_key, w_value, *arrays, *outs),
    )(info, w_key, w_value, joined, arrived, *arrays)


def input_grad_body(sums, rest_count, tokens, gain, *rest):
    out = rest[-1]
    values = tokens[...].astype(jnp.float32)
    parts = []
    if sums:
        total = rest[0][...].astype(jnp.float32)
        for piece in rest[1:sums]:
            total = total + piece[...].astype(jnp.float32)
        parts.append(total)
    parts += [piece[...].astype(jnp.float32) for piece in rest[sums : sums + rest_count]]
    grads = jnp.concatenate(parts, axis=1) if len(parts) > 1 else parts[0]
    out[...] = norm_back(grads, values, inv_rms(values), gain[...]).astype(jnp.bfloat16)


def input_grad(tokens, gain, sums, others):
    out = jax.ShapeDtypeStruct(tokens.shape, jnp.bfloat16)
    rows = tokens.shape[0]
    tile = 32 if rows % 32 == 0 else rows
    spec = lambda array: pl.BlockSpec((tile, array.shape[1]), lambda step: (step, 0))
    return pl.pallas_call(
        functools.partial(input_grad_body, len(sums), len(others)),
        name="input_grad",
        grid=(rows // tile,),
        out_shape=out,
        in_specs=[spec(tokens), full_spec(gain)] + [spec(a) for a in (*sums, *others)],
        out_specs=spec(out),
        compiler_params=params(),
        cost_estimate=cost(0, tokens, *sums, *others, out),
    )(tokens, gain, *sums, *others)


def spread_corners(parts):
    half = parts[0].shape[1] // 2
    return [swap(parts[1][:, :half], 2), swap(parts[2][:, half:], 1)]


def spread_end(arrays):
    half = arrays[0].shape[1] // 2
    spots = [(0, 0), (2, 0), (4, 0), (6, 0), (6, half)]
    return [(offset, low, array) for (offset, low), array in zip(spots, arrays)] + [
        (offset + 1, low, swap(array, 0)) for (offset, low), array in zip(spots, arrays)
    ]


def arrival_table(count):
    table = []
    for place in range(count):
        arrivals = []
        for step in range(1, count):
            if place - step >= 0:
                arrivals.append((2 * (step - 1), place - step))
            if place + step < count:
                arrivals.append((2 * (step - 1) + 1, place + step))
        table.append(arrivals)
    return table


def halo_of(key_value, reach):
    seq_count = lax.axis_size("seq")
    sent = []
    for distance in range(1, reach + 1):
        pairs = [(i, i + distance) for i in range(seq_count - distance)]
        sent.append(lax.ppermute(key_value, "seq", pairs))
    return sent


def halo_back(sections):
    seq_count = lax.axis_size("seq")
    back = []
    for section, array in enumerate(sections):
        distance = len(sections) - section
        pairs = [(i + distance, i) for i in range(seq_count - distance)]
        back.append(lax.ppermute(array, "seq", pairs))
    return back


def shards_general(tokens, dense, rope_rows, lowest, raw_queries, out_grad, w_key, w_value, reach):
    gain_row, q_row, k_row = dense
    cosine, sine = rope_rows
    tp_count = lax.axis_size("tp")
    place = lax.axis_index("tp").astype(jnp.int32)
    rows = tokens.shape[0]
    head_size = q_row.shape[1]
    kv_heads = w_key.shape[1] // head_size
    table = arrival_table(tp_count)
    picks = jnp.array(table, dtype=jnp.int32).reshape(tp_count, tp_count - 1, 2)
    picks = lax.dynamic_index_in_dim(picks, place, 0, keepdims=False)
    infos = [jnp.stack([jnp.int32(0), place])] + [picks[i] for i in range(tp_count - 1)]
    slot_places = jnp.concatenate([place[None], picks[:, 1]])
    normed_blocks, kv_blocks, raw_keys = [], [], []
    halo = [[] for _ in range(reach)]
    arrivals = []
    going_up = going_down = tokens
    for slot in range(tp_count):
        candidates = [tokens] if slot == 0 else list(arrivals)
        if slot < tp_count - 1:
            going_up = lax.ppermute(going_up, "tp", [(i, i + 1) for i in range(slot, tp_count - 1)])
            going_down = lax.ppermute(going_down, "tp", [(i + 1, i) for i in range(tp_count - 1 - slot)])
            arrivals += [going_up, going_down]
        key_value, keys, normed = project(infos[slot], candidates, gain_row, k_row, cosine, sine, w_key, w_value)
        normed_blocks.append(normed)
        kv_blocks.append(key_value)
        raw_keys.append((keys, 0))
        for distance, sent in enumerate(halo_of(key_value, reach)):
            halo[distance].append((sent, 0))
    blocks = [block for distance in range(reach, 0, -1) for block in halo[distance - 1]]
    blocks += [(block, 0) for block in kv_blocks]
    query_parts, kv_grads = [], []
    for head in range(kv_heads):
        outs = attend(head, kv_heads, reach, slot_places, lowest, q_row, cosine, sine, raw_queries, out_grad, blocks)
        query_parts.append(outs[0])
        back = halo_back(outs[2:])
        kv_grads += finish(head, slot_places, k_row, cosine, sine, outs[1], back, raw_keys)
    grad_queries = jnp.concatenate(query_parts, axis=1)
    partial_sum = input_terms(kv_grads, w_key, w_value, 0)
    summed_part = lax.psum_scatter(partial_sum, "tp", scatter_dimension=0, tiled=True)
    grad_x = input_grad(tokens, gain_row, [], [summed_part])
    left = jnp.concatenate(normed_blocks, axis=0)
    order = (slot_places[:, None] * rows + jnp.arange(rows, dtype=jnp.int32)[None, :]).reshape(-1)
    joined = [g[:, :head_size] for g in kv_grads] + [g[:, head_size:] for g in kv_grads]
    right = jnp.take(jnp.concatenate(joined, axis=1), order, axis=0)
    summed = lax.psum_scatter(dot_first(left, right), "seq", scatter_dimension=0, tiled=True)
    return (grad_x, grad_queries, summed[:, : w_key.shape[1]], summed[:, w_key.shape[1] :])


def trade(array, distance):
    return lax.ppermute(array, "tp", [(i, i ^ distance) for i in range(lax.axis_size("tp"))])


def shards_paired(tokens, dense, rope_rows, lowest, raw_queries, out_grad, w_key, w_value, reach, once):
    gain_row, q_row, k_row = dense
    cosine, sine = rope_rows
    seq_count = lax.axis_size("seq")
    seq_index = lax.axis_index("seq").astype(jnp.int32)
    place = lax.axis_index("tp").astype(jnp.int32)
    width, cols = w_key.shape
    head_size = q_row.shape[1]
    kv_heads = cols // head_size
    chunk = width // seq_count
    zero = jnp.zeros_like(place)
    slot_places = jnp.stack([place, place ^ 1, place ^ 2, place ^ 3])

    own_slice = jnp.concatenate(
        [lax.dynamic_slice_in_dim(weight, seq_index * chunk, chunk, 0) for weight in (w_key, w_value)], axis=1
    )
    distant = trade(after(tokens, own_slice), 2)

    partner_slice = trade(own_slice, 1)
    info = jnp.stack([zero, place])
    kv_0, keys_0, normed_0 = project(info, [tokens], gain_row, k_row, cosine, sine, w_key, w_value)
    halo_0 = halo_of(kv_0, reach)
    first_slice = after(partner_slice, (normed_0, halo_0))
    spread = [first_slice, swap(first_slice, 1), swap(first_slice, 2)]
    partner_normed_0 = trade(after(normed_0, partner_slice), 1)
    spread += spread_corners(spread)
    pieces = spread_end(spread)
    info = jnp.stack([seq_index, place, place ^ 2])
    far_block = after(distant, [piece for _, _, piece in pieces])
    kv_2, keys_2, normed_2, far_kv, far_keys = project_pair(
        info, normed_0, far_block, gain_row, k_row, cosine, sine, w_key, w_value, pieces
    )
    arrived_kv = trade(far_kv, 1)
    arrived_keys = trade(far_keys, 1)
    halo_2 = halo_of(kv_2, reach)
    arrived_kv = after(arrived_kv, (arrived_keys, partner_normed_0))
    halo_far = halo_of(arrived_kv, reach)
    partner_normed_2 = trade(after(normed_2, arrived_kv), 1)

    blocks = []
    for distance in range(reach, 0, -1):
        outer = halo_far[distance - 1]
        blocks += [(halo_0[distance - 1], 0), (outer, 0), (halo_2[distance - 1], 0), (outer, 1)]
    blocks += [(kv_0, 0), (arrived_kv, 0), (kv_2, 0), (arrived_kv, 1)]
    raw_keys = [(keys_0, 0), (arrived_keys, 0), (keys_2, 0), (arrived_keys, 1)]
    normed = [normed_0, partner_normed_0, normed_2, partner_normed_2]
    weight_info = jnp.concatenate([slot_places, (seq_index & 1)[None]])
    query_parts, kv_grads = [], []
    for head in range(kv_heads):
        outs = attend(head, kv_heads, reach, slot_places, lowest, q_row, cosine, sine, raw_queries, out_grad, blocks)
        query_parts.append(outs[0])
        back = halo_back(outs[2:])
        before = kv_grads if head == kv_heads - 1 else None
        results = finish(head, slot_places, k_row, cosine, sine, outs[1], back, raw_keys, before=before)
        kv_grads = kv_grads + results[:1]
    grad_queries = jnp.concatenate(query_parts, axis=1)

    joined, away = results[1:]
    arrived = trade(away, 1)
    info = jnp.stack([seq_index, place, place ^ 2])
    away_terms, own_terms = pair_terms(info, joined, arrived, pieces, w_key, w_value, kv_heads)
    other_terms = trade(away_terms, 2)

    def weight_step(step, _):
        parts = []
        for grads in kv_grads:
            send, keep = weight_terms(weight_info + step, grads, normed, chunk)
            keeps, comings = scatter_sum(send, keep)
            parts += [*keeps, *comings]
        return gather_heads(parts, kv_heads)

    empty = jnp.zeros((chunk, cols), jnp.float32)
    grad_wk, grad_wv = lax.fori_loop(0, after(once, away_terms), weight_step, (empty, empty))
    grad_x = input_grad(tokens, gain_row, [after(own_terms, (grad_wk, grad_wv, grad_queries)), other_terms], [])
    return (grad_x, grad_queries, grad_wk, grad_wv)


def shards(tokens, in_gain, raw_queries, w_key, w_value, q_gain, k_gain, doc_lengths, out_grad):
    seq_count = lax.axis_size("seq")
    tp_count = lax.axis_size("tp")
    rows, width = tokens.shape
    shard_rows = rows * tp_count
    reach = (WINDOW - 2) // shard_rows + 1
    first_row = lax.axis_index("seq") * shard_rows
    positions = first_row + jnp.arange(shard_rows, dtype=jnp.int32)
    begins = doc_begin(doc_lengths, positions)
    rope_rows = rope_tables(positions - begins, q_gain.shape[0])
    lowest = jnp.maximum(begins, positions - (WINDOW - 1)) - (first_row - reach * shard_rows)
    dense = (in_gain[None, :], q_gain[None, :], k_gain[None, :])
    chunk = width // seq_count
    paired = (
        tp_count == 1 << 2
        and seq_count == 1 << 3
        and chunk % 16 == 0
        and width % math.lcm(2 * chunk, 128) == 0
    )
    args = (tokens, dense, rope_rows, lowest[:, None], raw_queries, out_grad, w_key, w_value, reach)
    return shards_paired(*args, jnp.minimum(doc_lengths[0], 1)) if paired else shards_general(*args)


def solution(mesh):
    placed = (
        P(("seq", "tp"), None),
        P(),
        P("seq", "tp"),
        P(None, "tp"),
        P(None, "tp"),
        P(),
        P(),
        P(),
        P("seq", "tp"),
    )
    return jax.shard_map(
        shards,
        mesh=mesh,
        in_specs=placed,
        out_specs=(P(("seq", "tp"), None), P("seq", "tp"), P("seq", "tp"), P("seq", "tp")),
        check_vma=False,
    )
```

```python
import functools
import math

import jax
import jax.numpy as jnp
from jax import lax
from jax.experimental import pallas as pl
from jax.experimental.pallas import tpu as pltpu
from jax.sharding import PartitionSpec as P

WINDOW = 1024
EPSILON = 1e-06
QUERY_SCALE = 168.0 ** (-0.5)
ROPE_BASE = 10000.0
SMEM = pltpu.SMEM


def doc_begin(doc_lengths, positions):
    endings = jnp.cumsum(doc_lengths, dtype=jnp.int32)
    starts = endings - doc_lengths
    inside = starts[None, :] <= positions[:, None]
    return jnp.max(jnp.where(inside, starts[None, :], jnp.zeros_like(starts)[None, :]), axis=1)


def rope_tables(offsets, head_size):
    half_size = head_size // 2
    powers = jnp.arange(half_size, dtype=jnp.float32) * (2.0 / head_size)
    frequency = ROPE_BASE ** (-powers)
    angles = offsets.astype(jnp.float32)[:, None] * frequency[None, :]
    cosine = jnp.cos(angles)
    sine = jnp.sin(angles)
    return jnp.concatenate([cosine, cosine], axis=1), jnp.concatenate([-sine, sine], axis=1)


def half_turn(values):
    return pltpu.roll(values, values.shape[-1] // 2, values.ndim - 1)


def rope(values, cosine, sine):
    return values * cosine + half_turn(values) * sine


def rope_back(grads, cosine, sine):
    return grads * cosine + half_turn(grads * sine)


def inv_rms(values):
    return lax.rsqrt(jnp.mean(values * values, axis=-1, keepdims=True) + EPSILON)


def norm_back(grads, values, scale, gain):
    scaled = grads * gain
    mean = jnp.mean(values * scaled, axis=-1, keepdims=True)
    return scale * scaled - values * (scale * scale * scale * mean)


def dot_last(left, right):
    return lax.dot_general(left, right, (((1,), (1,)), ((), ())), preferred_element_type=jnp.float32)


def dot_first(left, right):
    return lax.dot_general(left, right, (((0,), (0,)), ((), ())), preferred_element_type=jnp.float32)


def full_spec(array):
    return pl.BlockSpec(array.shape, lambda *_: (0,) * array.ndim)


def any_spec():
    return pl.BlockSpec(memory_space=pl.ANY)


def smem_spec():
    return pl.BlockSpec(memory_space=SMEM)


def after(value, others):
    return lax.optimization_barrier((value, others))[0]


def cost(flops, *arrays):
    size = sum(math.prod(a.shape) * jnp.dtype(a.dtype).itemsize for a in arrays)
    return pl.CostEstimate(flops=flops, bytes_accessed=size, transcendentals=0)


def params(megabytes=30):
    return pltpu.CompilerParams(vmem_limit_bytes=megabytes * 1024 * 1024)


def start_all(copies):
    for copy in copies:
        copy.start()


def wait_all(copies):
    for copy in copies:
        copy.wait()


def piece_copies(places, seq_index, arrays, target, sems):
    copies = []
    for number, (offset, low) in enumerate(places):
        rows, cols = arrays[number].shape
        start = pl.multiple_of(jnp.bitwise_xor(seq_index, offset) * rows, 16)
        slot = target.at[pl.ds(start, rows), pl.ds(low, cols)]
        copies.append(pltpu.make_async_copy(arrays[number], slot, sems.at[number]))
    return copies


def store_heads(key_value, raw_keys, rows, keys, values, k_gain, cos_rows, sin_rows):
    head_size = k_gain.shape[1]
    raw_keys[rows, :] = keys.astype(raw_keys.dtype)
    for head in range(keys.shape[1] // head_size):
        cols = slice(head * head_size, (head + 1) * head_size)
        low = 2 * head * head_size
        head_keys = keys[:, cols]
        turned = rope(head_keys * inv_rms(head_keys) * k_gain[...], cos_rows, sin_rows)
        key_value[rows, low : low + head_size] = turned.astype(jnp.bfloat16)
        key_value[rows, low + head_size : low + 2 * head_size] = values[:, cols].astype(jnp.bfloat16)


def project_body(count, info, gain, k_gain, cosine, sine, w_key, w_value, *rest):
    blocks = rest[:count]
    key_value, raw_keys, normed, held, key_held, value_held, sems = rest[count:]
    rows = held.shape[0]

    def block_copy(index):
        return pltpu.make_async_copy(blocks[index], held, sems.at[2])

    for index in range(count):
        pl.when(info[0] == index)(lambda index=index: block_copy(index).start())
    own_copies = [
        pltpu.make_async_copy(w_key, key_held, sems.at[0]),
        pltpu.make_async_copy(w_value, value_held, sems.at[1]),
    ]
    start_all(own_copies)
    for index in range(count):
        pl.when(info[0] == index)(lambda index=index: block_copy(index).wait())
    values = held[...].astype(jnp.float32)
    normed[...] = (values * inv_rms(values) * gain[...]).astype(jnp.bfloat16)
    place = pl.ds(pl.multiple_of(info[1] * rows, rows), rows)
    wait_all(own_copies)
    keys = jnp.dot(normed[...], key_held[...], preferred_element_type=jnp.float32)
    vals = jnp.dot(normed[...], value_held[...], preferred_element_type=jnp.float32)
    store_heads(key_value, raw_keys, slice(0, rows), keys, vals, k_gain, cosine[place, :], sine[place, :])


def project(info, blocks, in_gain, k_gain, cosine, sine, w_key, w_value):
    rows, width = blocks[0].shape
    cols = w_key.shape[1]
    outs = [
        jax.ShapeDtypeStruct((rows, 2 * cols), jnp.bfloat16),
        jax.ShapeDtypeStruct((rows, cols), jnp.bfloat16),
        jax.ShapeDtypeStruct((rows, width), jnp.bfloat16),
    ]
    scratch = [
        pltpu.VMEM((rows, width), jnp.bfloat16),
        pltpu.VMEM((width, cols), jnp.bfloat16),
        pltpu.VMEM((width, cols), jnp.bfloat16),
        pltpu.SemaphoreType.DMA((3,)),
    ]
    dense = (in_gain, k_gain, cosine, sine)
    return pl.pallas_call(
        functools.partial(project_body, len(blocks)),
        name="project_block",
        grid=(1,),
        out_shape=tuple(outs),
        in_specs=[smem_spec()] + [full_spec(a) for a in dense] + [any_spec()] * (2 + len(blocks)),
        out_specs=tuple(full_spec(o) for o in outs),
        scratch_shapes=scratch,
        compiler_params=params(63),
        cost_estimate=cost(4 * rows * width * cols, blocks[0], w_key, w_value, *outs),
    )(info, *dense, w_key, w_value, *blocks)


def project_pair_body(places, info, gain, k_gain, cosine, sine, w_key, w_value, ready, block, *rest):
    pieces = rest[: len(places)]
    key_value, raw_keys, normed, far_key_value, far_keys = rest[len(places) : len(places) + 5]
    held, left, key_held, value_held, far_held, sems, far_sems = rest[len(places) + 5 :]
    rows, width = held.shape
    cols = w_key.shape[1]
    block_copy = pltpu.make_async_copy(block, held, sems.at[2])
    block_copy.start()
    ready_copy = pltpu.make_async_copy(ready, left.at[pl.ds(0, rows)], sems.at[3])
    ready_copy.start()
    far_copies = piece_copies(places, info[0], pieces, far_held, far_sems)
    start_all(far_copies)
    own_copies = [
        pltpu.make_async_copy(w_key, key_held, sems.at[0]),
        pltpu.make_async_copy(w_value, value_held, sems.at[1]),
    ]
    start_all(own_copies)
    block_copy.wait()
    values = held[...].astype(jnp.float32)
    normed[...] = (values * inv_rms(values) * gain[...]).astype(jnp.bfloat16)
    ready_copy.wait()
    left[rows:, :] = normed[...]
    wait_all(far_copies)
    both = jnp.dot(left[...], far_held[...], preferred_element_type=jnp.float32)
    for number in range(2):
        place = pl.ds(pl.multiple_of(info[1 + number] * rows, rows), rows)
        span = slice(number * rows, (number + 1) * rows)
        part = both[span]
        store_heads(
            far_key_value, far_keys, span, part[:, :cols], part[:, cols:], k_gain, cosine[place, :], sine[place, :]
        )
    place = pl.ds(pl.multiple_of(info[2] * rows, rows), rows)
    wait_all(own_copies)
    keys = jnp.dot(normed[...], key_held[...], preferred_element_type=jnp.float32)
    vals = jnp.dot(normed[...], value_held[...], preferred_element_type=jnp.float32)
    store_heads(key_value, raw_keys, slice(0, rows), keys, vals, k_gain, cosine[place, :], sine[place, :])


def project_pair(info, ready, block, in_gain, k_gain, cosine, sine, w_key, w_value, pieces):
    rows, width = block.shape
    cols = w_key.shape[1]
    places = [(offset, low) for offset, low, _ in pieces]
    arrays = [piece for _, _, piece in pieces]
    outs = tuple(
        jax.ShapeDtypeStruct(shape, jnp.bfloat16)
        for shape in ((rows, 2 * cols), (rows, cols), (rows, width), (2 * rows, 2 * cols), (2 * rows, cols))
    )
    dense = (in_gain, k_gain, cosine, sine)
    return pl.pallas_call(
        functools.partial(project_pair_body, places),
        name="project_pair",
        grid=(1,),
        out_shape=outs,
        in_specs=[smem_spec()] + [full_spec(a) for a in dense] + [any_spec()] * (4 + len(arrays)),
        out_specs=tuple(full_spec(o) for o in outs),
        scratch_shapes=[
            pltpu.VMEM((rows, width), jnp.bfloat16),
            pltpu.VMEM((2 * rows, width), jnp.bfloat16),
            pltpu.VMEM((width, cols), jnp.bfloat16),
            pltpu.VMEM((width, cols), jnp.bfloat16),
            pltpu.VMEM((width, 2 * cols), jnp.bfloat16),
            pltpu.SemaphoreType.DMA((4,)),
            pltpu.SemaphoreType.DMA((len(arrays),)),
        ],
        compiler_params=params(63),
        cost_estimate=cost(12 * rows * width * cols, block, w_key, w_value, *arrays, *outs),
    )(info, *dense, w_key, w_value, ready, block, *arrays)


def attend_body(reach, slots, info, lowest, q_gain, cosine, sine, queries, grads, *rest):
    blocks = rest[: (reach + 1) * slots]
    rest = rest[(reach + 1) * slots :]
    query_grads, own = rest[0], rest[1]
    far = rest[2 : 2 + reach]
    keys, values, key_sum, value_sum = rest[2 + reach :]
    rows = queries.shape[0]
    head_size = q_gain.shape[1]
    group = queries.shape[1] // head_size
    tile = blocks[0].shape[0]
    margin = reach * rows
    for slot in range(slots):
        start = info[slot] * tile
        for section in range(reach + 1):
            place = pl.ds(pl.multiple_of(section * rows + start, tile), tile)
            block = blocks[section * slots + slot]
            keys[place, :] = block[:, :head_size]
            values[place, :] = block[:, head_size:]
    key_sum[...] = jnp.zeros_like(key_sum)
    value_sum[...] = jnp.zeros_like(value_sum)
    for index in range(rows // tile):
        top = index * tile
        low = max(0, (top + margin - WINDOW + 1) // tile * tile)
        high = top + tile + margin
        width = high - low
        cos_rows = cosine[top : top + tile, :]
        sin_rows = sine[top : top + tile, :]
        raw = []
        scales = []
        turned = []
        for head in range(group):
            raw.append(queries[top : top + tile, head * head_size : (head + 1) * head_size].astype(jnp.float32))
            scales.append(inv_rms(raw[head]))
            turned.append(rope(raw[head] * scales[head] * q_gain[...], cos_rows, sin_rows) * QUERY_SCALE)
        query_rows = jnp.concatenate(turned, axis=0).astype(jnp.bfloat16)
        grad_rows = jnp.concatenate(
            [grads[top : top + tile, head * head_size : (head + 1) * head_size] for head in range(group)], axis=0
        )
        key_rows = keys[low:high, :]
        value_rows = values[low:high, :]
        places = lax.broadcasted_iota(jnp.int32, (width, tile), 0) + low
        last = lax.broadcasted_iota(jnp.int32, (width, tile), 1) + (top + margin)
        allowed = (places >= lowest[:, top : top + tile]) & (places <= last)
        allowed = jnp.concatenate([allowed] * group, axis=1)
        exps = jnp.where(allowed, jnp.exp(dot_last(key_rows, query_rows)), 0.0)
        probs = exps * (1.0 / jnp.sum(exps, axis=0, keepdims=True))
        weights = probs.astype(jnp.bfloat16)
        along = dot_last(value_rows, grad_rows)
        deltas = jnp.sum(weights.astype(jnp.float32) * along, axis=0, keepdims=True)
        slopes = (probs * (along - deltas)).astype(jnp.bfloat16)
        key_sum[low:high, :] += jnp.dot(slopes, query_rows, preferred_element_type=jnp.float32)
        value_sum[low:high, :] += jnp.dot(weights, grad_rows, preferred_element_type=jnp.float32)
        back = dot_first(slopes, key_rows)
        for head in range(group):
            turned_back = rope_back(back[head * tile : (head + 1) * tile] * QUERY_SCALE, cos_rows, sin_rows)
            result = norm_back(turned_back, raw[head], scales[head], q_gain[...])
            query_grads[top : top + tile, head * head_size : (head + 1) * head_size] = result.astype(jnp.bfloat16)
    for section in range(reach):
        span = slice(section * rows, (section + 1) * rows)
        far[section][:, :head_size] = key_sum[span, :].astype(jnp.bfloat16)
        far[section][:, head_size:] = value_sum[span, :].astype(jnp.bfloat16)
    own[:, :head_size] = key_sum[margin:, :]
    own[:, head_size:] = value_sum[margin:, :]


def attend(head, kv_heads, reach, info, lowest, q_gain, cosine, sine, queries, grads, blocks):
    rows = queries.shape[0]
    head_size = q_gain.shape[1]
    slots = len(blocks) // (reach + 1)
    tile = rows // slots
    cols = queries.shape[1] // kv_heads
    pick = lambda *_: (0, head)
    arrays = [array for array, _ in blocks]
    outs = (
        jax.ShapeDtypeStruct((rows, cols), jnp.bfloat16),
        jax.ShapeDtypeStruct((rows, 2 * head_size), jnp.float32),
    ) + (jax.ShapeDtypeStruct((rows, 2 * head_size), jnp.bfloat16),) * reach
    dense = (lowest, q_gain, cosine, sine)
    window = (reach + 1) * rows
    return pl.pallas_call(
        functools.partial(attend_body, reach, slots),
        name="attend_head",
        grid=(1,),
        out_shape=outs,
        in_specs=[smem_spec()]
        + [full_spec(a) for a in dense]
        + [pl.BlockSpec((rows, cols), pick)] * 2
        + [pl.BlockSpec((tile, 2 * head_size), lambda *_, row=row: (row, head)) for _, row in blocks],
        out_specs=[full_spec(o) for o in outs],
        scratch_shapes=[pltpu.VMEM((window, head_size), jnp.bfloat16)] * 2
        + [pltpu.VMEM((window, head_size), jnp.float32)] * 2,
        compiler_params=params(63),
        cost_estimate=cost(10 * rows * window * cols, queries, grads, *outs),
    )(info, *dense, queries, grads, *arrays)


def finish_body(reach, slots, earlier, info, k_gain, cosine, sine, own, *rest):
    arrived = rest[:reach]
    raw_keys = rest[reach : reach + slots]
    before = rest[reach + slots : reach + slots + earlier]
    outs = rest[reach + slots + earlier :]
    result = outs[0]
    head_size = k_gain.shape[1]
    rows = raw_keys[0].shape[0]
    for slot in range(slots):
        place = pl.ds(pl.multiple_of(info[slot] * rows, rows), rows)
        total = own[place, :]
        for part in arrived:
            total = total + part[place, :].astype(jnp.float32)
        values = raw_keys[slot][...].astype(jnp.float32)
        turned = rope_back(total[:, :head_size], cosine[place, :], sine[place, :])
        keys = norm_back(turned, values, inv_rms(values), k_gain[...])
        result[place, :head_size] = keys.astype(jnp.bfloat16)
        result[place, head_size:] = total[:, head_size:].astype(jnp.bfloat16)
    if len(outs) > 1:
        joined, away = outs[1:]
        for head, part in enumerate((*before, result)):
            joined[:, 2 * head * head_size : 2 * (head + 1) * head_size] = part[...]
        for number, slot in enumerate((1, 3)):
            place = pl.ds(pl.multiple_of(info[slot] * rows, 16), rows)
            away[number * rows : (number + 1) * rows, :] = joined[place, :]


def finish(head, info, k_gain, cosine, sine, own, arrived, raw_keys, before=None):
    rows, cols = own.shape
    head_size = k_gain.shape[1]
    slots = len(raw_keys)
    tile = rows // slots
    arrays = [array for array, _ in raw_keys]
    outs = [jax.ShapeDtypeStruct(own.shape, jnp.bfloat16)]
    if before is not None:
        width = cols * (len(before) + 1)
        outs += [jax.ShapeDtypeStruct((count, width), jnp.bfloat16) for count in (rows, 2 * tile)]
    before = before or []
    dense = (k_gain, cosine, sine, own, *arrived)
    results = pl.pallas_call(
        functools.partial(finish_body, len(arrived), slots, len(before)),
        name="finish_kv",
        grid=(1,),
        out_shape=tuple(outs),
        in_specs=[smem_spec()]
        + [full_spec(a) for a in dense]
        + [pl.BlockSpec((tile, head_size), lambda *_, row=row: (row, head)) for _, row in raw_keys]
        + [full_spec(a) for a in before],
        out_specs=tuple(full_spec(o) for o in outs),
        compiler_params=params(63),
        cost_estimate=cost(0, own, *arrived, *outs),
    )(info, *dense, *arrays, *before)
    return list(results)


def weight_body(slots, info, grads, *rest):
    blocks = rest[:slots]
    send, keep, held = rest[slots:]
    rows = blocks[0].shape[0]
    chunk = send.shape[1]
    own = info[slots]
    left = jnp.concatenate([block[...] for block in blocks], axis=0)
    right = jnp.concatenate(
        [grads[pl.ds(pl.multiple_of(info[slot] * rows, rows), rows), :] for slot in range(slots)], axis=0
    )
    held[...] = dot_first(left, right)
    for pair in range(send.shape[0]):
        other = pl.ds(pl.multiple_of((2 * pair + 1 - own) * chunk, 8), chunk)
        mine = pl.ds(pl.multiple_of((2 * pair + own) * chunk, 8), chunk)
        send[pair] = held[other, :].astype(jnp.bfloat16)
        keep[pair] = held[mine, :].astype(jnp.bfloat16)


def weight_terms(info, grads, blocks, chunk):
    rows, width = blocks[0].shape
    cols = grads.shape[1]
    tile = math.lcm(2 * chunk, 128)
    pairs = tile // (2 * chunk)
    out = jax.ShapeDtypeStruct((width // (2 * chunk), chunk, cols), jnp.bfloat16)
    out_spec = pl.BlockSpec((pairs, chunk, cols), lambda step: (step, 0, 0))
    return pl.pallas_call(
        functools.partial(weight_body, len(blocks)),
        name="weight_terms",
        grid=(width // tile,),
        out_shape=(out, out),
        in_specs=[smem_spec(), full_spec(grads)]
        + [pl.BlockSpec((rows, tile), lambda step: (0, step))] * len(blocks),
        out_specs=(out_spec, out_spec),
        scratch_shapes=[pltpu.VMEM((tile, cols), jnp.float32)],
        compiler_params=params(),
        cost_estimate=cost(0),
    )(info, grads, *blocks)


def add(left, right):
    return left.astype(jnp.float32) + right.astype(jnp.float32)


def split_body(halves, info, *rest):
    keeps, arrivals, outs = rest[: len(halves)], rest[len(halves) : 2 * len(halves)], rest[2 * len(halves) :]
    for index, (cols, outer, inner) in enumerate(halves):
        own = info[index]
        for high in range(outer):
            for low in range(inner):
                for side, target in ((1 - own, outs[2 * index]), (own, outs[2 * index + 1])):
                    place = (high * 2 + side) * inner + low
                    total = add(keeps[index][place, :, cols], arrivals[index][place, :, cols])
                    target[high * inner + low] = total.astype(jnp.bfloat16)


def row_steps(rows):
    return max(n for n in range(1, 5) if rows % (16 * n) == 0) if rows % 16 == 0 else 1


def split_sum(info, keeps, arrivals, halves):
    outs = []
    for keep, (cols, outer, inner) in zip(keeps, halves):
        outs += [jax.ShapeDtypeStruct((outer * inner, keep.shape[1], cols.stop - cols.start), jnp.bfloat16)] * 2
    rows = keeps[0].shape[1]
    steps = row_steps(rows)

    def spec(array):
        return pl.BlockSpec((array.shape[0], rows // steps, array.shape[2]), lambda step: (0, step, 0))

    return pl.pallas_call(
        functools.partial(split_body, halves),
        name="split_sum",
        grid=(steps,),
        out_shape=tuple(outs),
        in_specs=[smem_spec()] + [spec(a) for a in (*keeps, *arrivals)],
        out_specs=tuple(spec(o) for o in outs),
        compiler_params=params(),
        cost_estimate=cost(0),
    )(info, *keeps, *arrivals)


def swap(array, bit):
    size = lax.axis_size("seq")
    return lax.ppermute(array, "seq", [(i, i ^ (1 << bit)) for i in range(size)])


def scatter_sum(send, keep):
    bits = lax.axis_size("seq").bit_length() - 1
    index = lax.axis_index("seq")
    half = keep.shape[2] // 2
    routes = (list(range(1, bits)), list(range(bits - 1, 0, -1)))
    lefts = [list(range(1, bits)), list(range(1, bits))]
    arrival = swap(send, 0)
    keeps, arrivals = [keep, keep], [arrival, arrival]
    cols = [slice(0, half), slice(half, 2 * half)]
    for step in range(bits - 1):
        turn = [route[step] for route in routes]
        halves = []
        for path in range(2):
            place = lefts[path].index(turn[path])
            halves.append((cols[path], 1 << (len(lefts[path]) - 1 - place), 1 << place))
            lefts[path].remove(turn[path])
        info = jnp.stack([(index >> bit) & 1 for bit in turn]).astype(jnp.int32)
        sent_a, kept_a, sent_b, kept_b = split_sum(info, keeps, arrivals, tuple(halves))
        arrivals = [swap(sent_a, turn[0]), swap(sent_b, turn[1])]
        keeps = [kept_a, kept_b]
        cols = [slice(0, half), slice(0, half)]
    return keeps, arrivals


def gather_body(heads, *rest):
    parts = rest[: 4 * heads]
    outs = rest[4 * heads :]
    size = parts[0].shape[2]
    for head in range(heads):
        for side in range(2):
            keep, arrival = parts[4 * head + side], parts[4 * head + 2 + side]
            outs[side][:, head * size : (head + 1) * size] = add(keep[0], arrival[0])


def gather_heads(parts, heads):
    _, rows, cols = parts[0].shape
    steps = row_steps(rows)
    out = jax.ShapeDtypeStruct((rows, cols * heads), jnp.float32)
    out_spec = pl.BlockSpec((rows // steps, cols * heads), lambda step: (step, 0))
    return pl.pallas_call(
        functools.partial(gather_body, heads),
        name="gather_heads",
        grid=(steps,),
        out_shape=(out, out),
        in_specs=[pl.BlockSpec((1, rows // steps, cols), lambda step: (0, step, 0)) for a in parts],
        out_specs=(out_spec, out_spec),
        compiler_params=params(),
        cost_estimate=cost(0),
    )(*parts)


def input_terms_body(heads, w_key, w_value, *rest):
    grads, out = rest[:heads], rest[heads]
    size = grads[0].shape[1] // 2
    left = jnp.concatenate([g[:, :size] for g in grads] + [g[:, size:] for g in grads], axis=1)
    right = jnp.concatenate([w_key[...], w_value[...]], axis=1)
    out[...] = dot_last(left, right).astype(jnp.bfloat16)


def input_terms(kv_grads, w_key, w_value, skip):
    width, cols = w_key.shape
    rows = kv_grads[0].shape[0]
    common = math.gcd(skip, width - skip)
    tile = max(t for t in range(128, 1025, 128) if common % t == 0)
    out = jax.ShapeDtypeStruct((rows, width - skip), jnp.bfloat16)
    weight_spec = pl.BlockSpec((tile, cols), lambda step: (step + skip // tile, 0))
    return pl.pallas_call(
        functools.partial(input_terms_body, len(kv_grads)),
        name="input_terms",
        grid=((width - skip) // tile,),
        out_shape=out,
        in_specs=[weight_spec, weight_spec] + [full_spec(g) for g in kv_grads],
        out_specs=pl.BlockSpec((rows, tile), lambda step: (0, step)),
        compiler_params=params(),
        cost_estimate=cost(4 * rows * (width - skip) * cols, out, *kv_grads),
    )(w_key, w_value, *kv_grads)


def pair_body(places, heads, info, w_key, w_value, joined, arrived, *rest):
    pieces = rest[: len(places)]
    away_out, own_out, key_held, value_held, held, own_sems, sems = rest[len(places) :]
    rows, width = own_out.shape
    size = w_key.shape[1] // heads
    half = width // 2
    slice_rows = pieces[0].shape[0]
    split = half // slice_rows
    first = info[0] // split
    copies = piece_copies(places, info[0], pieces, held, sems)
    spans, groups = [], []
    for number in range(2):
        span = pl.ds(pl.multiple_of(jnp.bitwise_xor(first, number) * half, 128), half)
        spans.append(span)
        groups.append(
            [
                pltpu.make_async_copy(w_key.at[span, :], key_held.at[span, :], own_sems.at[2 * number]),
                pltpu.make_async_copy(w_value.at[span, :], value_held.at[span, :], own_sems.at[2 * number + 1]),
            ]
            + [copy for copy, (offset, _) in zip(copies, places) if offset // split == number]
        )
        start_all(groups[number])
    own_rows = jnp.concatenate(
        [joined[pl.ds(pl.multiple_of(info[1 + number] * rows, rows), rows), :] for number in range(2)], axis=0
    )
    sides = [
        block[:, (2 * head + side) * size : (2 * head + side + 1) * size]
        for block in (own_rows, arrived[...])
        for side in range(2)
        for head in range(heads)
    ]
    left = jnp.concatenate(sides, axis=1)
    for span, group in zip(spans, groups):
        wait_all(group)
        right = jnp.concatenate([key_held[span, :], value_held[span, :], held[span, :]], axis=1)
        total = dot_last(left, right).astype(jnp.bfloat16)
        own_out[:, span] = total[:rows]
        away_out[:, span] = total[rows:]


def pair_terms(info, joined, arrived, pieces, w_key, w_value, heads):
    rows = arrived.shape[0] // 2
    width, cols = w_key.shape
    places = [(offset, low) for offset, low, _ in pieces]
    arrays = [piece for _, _, piece in pieces]
    outs = (jax.ShapeDtypeStruct((rows, width), jnp.bfloat16),) * 2
    return pl.pallas_call(
        functools.partial(pair_body, places, heads),
        name="pair_terms",
        grid=(1,),
        out_shape=outs,
        in_specs=[smem_spec(), any_spec(), any_spec(), full_spec(joined), full_spec(arrived)]
        + [any_spec()] * len(arrays),
        out_specs=tuple(full_spec(o) for o in outs),
        scratch_shapes=[
            pltpu.VMEM((width, cols), jnp.bfloat16),
            pltpu.VMEM((width, cols), jnp.bfloat16),
            pltpu.VMEM((width, 2 * cols), jnp.bfloat16),
            pltpu.SemaphoreType.DMA((4,)),
            pltpu.SemaphoreType.DMA((len(arrays),)),
        ],
        compiler_params=params(63),
        cost_estimate=cost(16 * rows * width * cols, w_key, w_value, *arrays, *outs),
    )(info, w_key, w_value, joined, arrived, *arrays)


def input_grad_body(sums, rest_count, tokens, gain, *rest):
    out = rest[-1]
    values = tokens[...].astype(jnp.float32)
    parts = []
    if sums:
        total = rest[0][...].astype(jnp.float32)
        for piece in rest[1:sums]:
            total = total + piece[...].astype(jnp.float32)
        parts.append(total)
    parts += [piece[...].astype(jnp.float32) for piece in rest[sums : sums + rest_count]]
    grads = jnp.concatenate(parts, axis=1) if len(parts) > 1 else parts[0]
    out[...] = norm_back(grads, values, inv_rms(values), gain[...]).astype(jnp.bfloat16)


def input_grad(tokens, gain, sums, others):
    out = jax.ShapeDtypeStruct(tokens.shape, jnp.bfloat16)
    rows = tokens.shape[0]
    tile = 32 if rows % 32 == 0 else rows
    spec = lambda array: pl.BlockSpec((tile, array.shape[1]), lambda step: (step, 0))
    return pl.pallas_call(
        functools.partial(input_grad_body, len(sums), len(others)),
        name="input_grad",
        grid=(rows // tile,),
        out_shape=out,
        in_specs=[spec(tokens), full_spec(gain)] + [spec(a) for a in (*sums, *others)],
        out_specs=spec(out),
        compiler_params=params(63),
        cost_estimate=cost(0, tokens, *sums, *others, out),
    )(tokens, gain, *sums, *others)


def spread_corners(parts):
    half = parts[0].shape[1] // 2
    return [swap(parts[1][:, :half], 2), swap(parts[2][:, half:], 1)]


def spread_end(arrays):
    half = arrays[0].shape[1] // 2
    spots = [(0, 0), (2, 0), (4, 0), (6, 0), (6, half)]
    return [(offset, low, array) for (offset, low), array in zip(spots, arrays)] + [
        (offset + 1, low, swap(array, 0)) for (offset, low), array in zip(spots, arrays)
    ]


def arrival_table(count):
    table = []
    for place in range(count):
        arrivals = []
        for step in range(1, count):
            if place - step >= 0:
                arrivals.append((2 * (step - 1), place - step))
            if place + step < count:
                arrivals.append((2 * (step - 1) + 1, place + step))
        table.append(arrivals)
    return table


def halo_of(key_value, reach):
    seq_count = lax.axis_size("seq")
    sent = []
    for distance in range(1, reach + 1):
        pairs = [(i, i + distance) for i in range(seq_count - distance)]
        sent.append(lax.ppermute(key_value, "seq", pairs))
    return sent


def halo_back(sections):
    seq_count = lax.axis_size("seq")
    back = []
    for section, array in enumerate(sections):
        distance = len(sections) - section
        pairs = [(i + distance, i) for i in range(seq_count - distance)]
        back.append(lax.ppermute(array, "seq", pairs))
    return back


def shards_general(tokens, dense, rope_rows, lowest, raw_queries, out_grad, w_key, w_value, reach):
    gain_row, q_row, k_row = dense
    cosine, sine = rope_rows
    tp_count = lax.axis_size("tp")
    place = lax.axis_index("tp").astype(jnp.int32)
    rows = tokens.shape[0]
    head_size = q_row.shape[1]
    kv_heads = w_key.shape[1] // head_size
    table = arrival_table(tp_count)
    picks = jnp.array(table, dtype=jnp.int32).reshape(tp_count, tp_count - 1, 2)
    picks = lax.dynamic_index_in_dim(picks, place, 0, keepdims=False)
    infos = [jnp.stack([jnp.int32(0), place])] + [picks[i] for i in range(tp_count - 1)]
    slot_places = jnp.concatenate([place[None], picks[:, 1]])
    normed_blocks, kv_blocks, raw_keys = [], [], []
    halo = [[] for _ in range(reach)]
    arrivals = []
    going_up = going_down = tokens
    for slot in range(tp_count):
        candidates = [tokens] if slot == 0 else list(arrivals)
        if slot < tp_count - 1:
            going_up = lax.ppermute(going_up, "tp", [(i, i + 1) for i in range(slot, tp_count - 1)])
            going_down = lax.ppermute(going_down, "tp", [(i + 1, i) for i in range(tp_count - 1 - slot)])
            arrivals += [going_up, going_down]
        key_value, keys, normed = project(infos[slot], candidates, gain_row, k_row, cosine, sine, w_key, w_value)
        normed_blocks.append(normed)
        kv_blocks.append(key_value)
        raw_keys.append((keys, 0))
        for distance, sent in enumerate(halo_of(key_value, reach)):
            halo[distance].append((sent, 0))
    blocks = [block for distance in range(reach, 0, -1) for block in halo[distance - 1]]
    blocks += [(block, 0) for block in kv_blocks]
    query_parts, kv_grads = [], []
    for head in range(kv_heads):
        outs = attend(head, kv_heads, reach, slot_places, lowest, q_row, cosine, sine, raw_queries, out_grad, blocks)
        query_parts.append(outs[0])
        back = halo_back(outs[2:])
        kv_grads += finish(head, slot_places, k_row, cosine, sine, outs[1], back, raw_keys)
    grad_queries = jnp.concatenate(query_parts, axis=1)
    partial_sum = input_terms(kv_grads, w_key, w_value, 0)
    summed_part = lax.psum_scatter(partial_sum, "tp", scatter_dimension=0, tiled=True)
    grad_x = input_grad(tokens, gain_row, [], [summed_part])
    left = jnp.concatenate(normed_blocks, axis=0)
    order = (slot_places[:, None] * rows + jnp.arange(rows, dtype=jnp.int32)[None, :]).reshape(-1)
    joined = [g[:, :head_size] for g in kv_grads] + [g[:, head_size:] for g in kv_grads]
    right = jnp.take(jnp.concatenate(joined, axis=1), order, axis=0)
    summed = lax.psum_scatter(dot_first(left, right), "seq", scatter_dimension=0, tiled=True)
    return (grad_x, grad_queries, summed[:, : w_key.shape[1]], summed[:, w_key.shape[1] :])


def trade(array, distance):
    return lax.ppermute(array, "tp", [(i, i ^ distance) for i in range(lax.axis_size("tp"))])


def shards_paired(tokens, dense, rope_rows, lowest, raw_queries, out_grad, w_key, w_value, reach, once):
    gain_row, q_row, k_row = dense
    cosine, sine = rope_rows
    seq_count = lax.axis_size("seq")
    seq_index = lax.axis_index("seq").astype(jnp.int32)
    place = lax.axis_index("tp").astype(jnp.int32)
    width, cols = w_key.shape
    head_size = q_row.shape[1]
    kv_heads = cols // head_size
    chunk = width // seq_count
    zero = jnp.zeros_like(place)
    slot_places = jnp.stack([place, place ^ 1, place ^ 2, place ^ 3])

    own_slice = jnp.concatenate(
        [lax.dynamic_slice_in_dim(weight, seq_index * chunk, chunk, 0) for weight in (w_key, w_value)], axis=1
    )
    distant = trade(after(tokens, own_slice), 2)

    partner_slice = trade(own_slice, 1)
    info = jnp.stack([zero, place])
    kv_0, keys_0, normed_0 = project(info, [tokens], gain_row, k_row, cosine, sine, w_key, w_value)
    halo_0 = halo_of(kv_0, reach)
    first_slice = after(partner_slice, (normed_0, halo_0))
    spread = [first_slice, swap(first_slice, 1), swap(first_slice, 2)]
    partner_normed_0 = trade(after(normed_0, partner_slice), 1)
    spread += spread_corners(spread)
    pieces = spread_end(spread)
    info = jnp.stack([seq_index, place, place ^ 2])
    far_block = after(distant, [piece for _, _, piece in pieces])
    kv_2, keys_2, normed_2, far_kv, far_keys = project_pair(
        info, normed_0, far_block, gain_row, k_row, cosine, sine, w_key, w_value, pieces
    )
    arrived_kv = trade(far_kv, 1)
    arrived_keys = trade(far_keys, 1)
    halo_2 = halo_of(kv_2, reach)
    arrived_kv = after(arrived_kv, (arrived_keys, partner_normed_0))
    halo_far = halo_of(arrived_kv, reach)
    partner_normed_2 = trade(after(normed_2, arrived_kv), 1)

    blocks = []
    for distance in range(reach, 0, -1):
        outer = halo_far[distance - 1]
        blocks += [(halo_0[distance - 1], 0), (outer, 0), (halo_2[distance - 1], 0), (outer, 1)]
    blocks += [(kv_0, 0), (arrived_kv, 0), (kv_2, 0), (arrived_kv, 1)]
    raw_keys = [(keys_0, 0), (arrived_keys, 0), (keys_2, 0), (arrived_keys, 1)]
    normed = [normed_0, partner_normed_0, normed_2, partner_normed_2]
    weight_info = jnp.concatenate([slot_places, (seq_index & 1)[None]])
    query_parts, kv_grads = [], []
    for head in range(kv_heads):
        outs = attend(head, kv_heads, reach, slot_places, lowest, q_row, cosine, sine, raw_queries, out_grad, blocks)
        query_parts.append(outs[0])
        back = halo_back(outs[2:])
        before = kv_grads if head == kv_heads - 1 else None
        results = finish(head, slot_places, k_row, cosine, sine, outs[1], back, raw_keys, before=before)
        kv_grads = kv_grads + results[:1]
    grad_queries = jnp.concatenate(query_parts, axis=1)

    joined, away = results[1:]
    arrived = trade(away, 1)
    info = jnp.stack([seq_index, place, place ^ 2])
    away_terms, own_terms = pair_terms(info, joined, arrived, pieces, w_key, w_value, kv_heads)
    other_terms = trade(away_terms, 2)

    def weight_step(step, _):
        parts = []
        for grads in kv_grads:
            send, keep = weight_terms(weight_info + step, grads, normed, chunk)
            keeps, comings = scatter_sum(send, keep)
            parts += [*keeps, *comings]
        return gather_heads(parts, kv_heads)

    empty = jnp.zeros((chunk, cols), jnp.float32)
    grad_wk, grad_wv = lax.fori_loop(0, after(once, away_terms), weight_step, (empty, empty))
    grad_x = input_grad(tokens, gain_row, [after(own_terms, (grad_wk, grad_wv, grad_queries)), other_terms], [])
    return (grad_x, grad_queries, grad_wk, grad_wv)


def shards(tokens, in_gain, raw_queries, w_key, w_value, q_gain, k_gain, doc_lengths, out_grad):
    seq_count = lax.axis_size("seq")
    tp_count = lax.axis_size("tp")
    rows, width = tokens.shape
    shard_rows = rows * tp_count
    reach = (WINDOW - 2) // shard_rows + 1
    first_row = lax.axis_index("seq") * shard_rows
    positions = first_row + jnp.arange(shard_rows, dtype=jnp.int32)
    begins = doc_begin(doc_lengths, positions)
    rope_rows = rope_tables(positions - begins, q_gain.shape[0])
    lowest = jnp.maximum(begins, positions - (WINDOW - 1)) - (first_row - reach * shard_rows)
    dense = (in_gain[None, :], q_gain[None, :], k_gain[None, :])
    chunk = width // seq_count
    paired = (
        tp_count == 1 << 2
        and seq_count == 1 << 3
        and chunk % 16 == 0
        and width % math.lcm(2 * chunk, 128) == 0
    )
    args = (tokens, dense, rope_rows, lowest[None, :], raw_queries, out_grad, w_key, w_value, reach)
    return shards_paired(*args, jnp.minimum(doc_lengths[0], 1)) if paired else shards_general(*args)


def solution(mesh):
    placed = (
        P(("seq", "tp"), None),
        P(),
        P("seq", "tp"),
        P(None, "tp"),
        P(None, "tp"),
        P(),
        P(),
        P(),
        P("seq", "tp"),
    )
    return jax.shard_map(
        shards,
        mesh=mesh,
        in_specs=placed,
        out_specs=(P(("seq", "tp"), None), P("seq", "tp"), P("seq", "tp"), P("seq", "tp")),
        check_vma=False,
    )
```

```python
import functools
import math

import jax
import jax.numpy as jnp
from jax import lax
from jax.experimental import pallas as pl
from jax.experimental.pallas import tpu as pltpu
from jax.sharding import PartitionSpec as P

WINDOW = 1024
EPSILON = 1e-06
QUERY_SCALE = 168.0 ** (-0.5)
ROPE_BASE = 10000.0
SMEM = pltpu.SMEM


def doc_begin(doc_lengths, positions):
    endings = jnp.cumsum(doc_lengths, dtype=jnp.int32)
    starts = endings - doc_lengths
    inside = starts[None, :] <= positions[:, None]
    return jnp.max(jnp.where(inside, starts[None, :], jnp.zeros_like(starts)[None, :]), axis=1)


def rope_tables(offsets, head_size):
    half_size = head_size // 2
    powers = jnp.arange(half_size, dtype=jnp.float32) * (2.0 / head_size)
    frequency = ROPE_BASE ** (-powers)
    angles = offsets.astype(jnp.float32)[:, None] * frequency[None, :]
    cosine = jnp.cos(angles)
    sine = jnp.sin(angles)
    return jnp.concatenate([cosine, cosine], axis=1), jnp.concatenate([-sine, sine], axis=1)


def half_turn(values):
    return pltpu.roll(values, values.shape[-1] // 2, values.ndim - 1)


def rope(values, cosine, sine):
    return values * cosine + half_turn(values) * sine


def rope_back(grads, cosine, sine):
    return grads * cosine + half_turn(grads * sine)


def inv_rms(values):
    return lax.rsqrt(jnp.mean(values * values, axis=-1, keepdims=True) + EPSILON)


def norm_back(grads, values, scale, gain):
    scaled = grads * gain
    mean = jnp.mean(values * scaled, axis=-1, keepdims=True)
    return scale * scaled - values * (scale * scale * scale * mean)


def dot_last(left, right):
    return lax.dot_general(left, right, (((1,), (1,)), ((), ())), preferred_element_type=jnp.float32)


def dot_first(left, right):
    return lax.dot_general(left, right, (((0,), (0,)), ((), ())), preferred_element_type=jnp.float32)


def full_spec(array):
    return pl.BlockSpec(array.shape, lambda *_: (0,) * array.ndim)


def any_spec():
    return pl.BlockSpec(memory_space=pl.ANY)


def smem_spec():
    return pl.BlockSpec(memory_space=SMEM)


def after(value, others):
    return lax.optimization_barrier((value, others))[0]


def cost(flops, *arrays):
    size = sum(math.prod(a.shape) * jnp.dtype(a.dtype).itemsize for a in arrays)
    return pl.CostEstimate(flops=flops, bytes_accessed=size, transcendentals=0)


def params(megabytes=30):
    return pltpu.CompilerParams(vmem_limit_bytes=megabytes * 1024 * 1024)


def start_all(copies):
    for copy in copies:
        copy.start()


def wait_all(copies):
    for copy in copies:
        copy.wait()


def piece_copies(places, seq_index, arrays, target, sems):
    copies = []
    for number, (offset, low) in enumerate(places):
        rows, cols = arrays[number].shape
        start = pl.multiple_of(jnp.bitwise_xor(seq_index, offset) * rows, 16)
        slot = target.at[pl.ds(start, rows), pl.ds(low, cols)]
        copies.append(pltpu.make_async_copy(arrays[number], slot, sems.at[number]))
    return copies


def store_heads(key_value, raw_keys, rows, keys, values, k_gain, cos_rows, sin_rows):
    head_size = k_gain.shape[1]
    raw_keys[rows, :] = keys.astype(raw_keys.dtype)
    for head in range(keys.shape[1] // head_size):
        cols = slice(head * head_size, (head + 1) * head_size)
        low = 2 * head * head_size
        head_keys = keys[:, cols]
        turned = rope(head_keys * inv_rms(head_keys) * k_gain[...], cos_rows, sin_rows)
        key_value[rows, low : low + head_size] = turned.astype(jnp.bfloat16)
        key_value[rows, low + head_size : low + 2 * head_size] = values[:, cols].astype(jnp.bfloat16)


def project_body(count, info, gain, k_gain, cosine, sine, w_key, w_value, *rest):
    blocks = rest[:count]
    key_value, raw_keys, normed, held, key_held, value_held, sems = rest[count:]
    rows = held.shape[0]

    def block_copy(index):
        return pltpu.make_async_copy(blocks[index], held, sems.at[2])

    for index in range(count):
        pl.when(info[0] == index)(lambda index=index: block_copy(index).start())
    own_copies = [
        pltpu.make_async_copy(w_key, key_held, sems.at[0]),
        pltpu.make_async_copy(w_value, value_held, sems.at[1]),
    ]
    start_all(own_copies)
    for index in range(count):
        pl.when(info[0] == index)(lambda index=index: block_copy(index).wait())
    values = held[...].astype(jnp.float32)
    normed[...] = (values * inv_rms(values) * gain[...]).astype(jnp.bfloat16)
    place = pl.ds(pl.multiple_of(info[1] * rows, rows), rows)
    wait_all(own_copies)
    keys = jnp.dot(normed[...], key_held[...], preferred_element_type=jnp.float32)
    vals = jnp.dot(normed[...], value_held[...], preferred_element_type=jnp.float32)
    store_heads(key_value, raw_keys, slice(0, rows), keys, vals, k_gain, cosine[place, :], sine[place, :])


def project(info, blocks, in_gain, k_gain, cosine, sine, w_key, w_value):
    rows, width = blocks[0].shape
    cols = w_key.shape[1]
    outs = [
        jax.ShapeDtypeStruct((rows, 2 * cols), jnp.bfloat16),
        jax.ShapeDtypeStruct((rows, cols), jnp.bfloat16),
        jax.ShapeDtypeStruct((rows, width), jnp.bfloat16),
    ]
    scratch = [
        pltpu.VMEM((rows, width), jnp.bfloat16),
        pltpu.VMEM((width, cols), jnp.bfloat16),
        pltpu.VMEM((width, cols), jnp.bfloat16),
        pltpu.SemaphoreType.DMA((3,)),
    ]
    dense = (in_gain, k_gain, cosine, sine)
    return pl.pallas_call(
        functools.partial(project_body, len(blocks)),
        name="project_block",
        grid=(1,),
        out_shape=tuple(outs),
        in_specs=[smem_spec()] + [full_spec(a) for a in dense] + [any_spec()] * (2 + len(blocks)),
        out_specs=tuple(full_spec(o) for o in outs),
        scratch_shapes=scratch,
        compiler_params=params(63),
        cost_estimate=cost(4 * rows * width * cols, blocks[0], w_key, w_value, *outs),
    )(info, *dense, w_key, w_value, *blocks)


def project_pair_body(places, info, gain, k_gain, cosine, sine, w_key, w_value, ready, block, *rest):
    pieces = rest[: len(places)]
    key_value, raw_keys, normed, far_key_value, far_keys = rest[len(places) : len(places) + 5]
    held, left, key_held, value_held, far_held, sems, far_sems = rest[len(places) + 5 :]
    rows, width = held.shape
    cols = w_key.shape[1]
    block_copy = pltpu.make_async_copy(block, held, sems.at[2])
    block_copy.start()
    ready_copy = pltpu.make_async_copy(ready, left.at[pl.ds(0, rows)], sems.at[3])
    ready_copy.start()
    far_copies = piece_copies(places, info[0], pieces, far_held, far_sems)
    start_all(far_copies)
    own_copies = [
        pltpu.make_async_copy(w_key, key_held, sems.at[0]),
        pltpu.make_async_copy(w_value, value_held, sems.at[1]),
    ]
    start_all(own_copies)
    block_copy.wait()
    values = held[...].astype(jnp.float32)
    normed[...] = (values * inv_rms(values) * gain[...]).astype(jnp.bfloat16)
    ready_copy.wait()
    left[rows:, :] = normed[...]
    wait_all(far_copies)
    both = jnp.dot(left[...], far_held[...], preferred_element_type=jnp.float32)
    for number in range(2):
        place = pl.ds(pl.multiple_of(info[1 + number] * rows, rows), rows)
        span = slice(number * rows, (number + 1) * rows)
        part = both[span]
        store_heads(
            far_key_value, far_keys, span, part[:, :cols], part[:, cols:], k_gain, cosine[place, :], sine[place, :]
        )
    place = pl.ds(pl.multiple_of(info[2] * rows, rows), rows)
    wait_all(own_copies)
    keys = jnp.dot(normed[...], key_held[...], preferred_element_type=jnp.float32)
    vals = jnp.dot(normed[...], value_held[...], preferred_element_type=jnp.float32)
    store_heads(key_value, raw_keys, slice(0, rows), keys, vals, k_gain, cosine[place, :], sine[place, :])


def project_pair(info, ready, block, in_gain, k_gain, cosine, sine, w_key, w_value, pieces):
    rows, width = block.shape
    cols = w_key.shape[1]
    places = [(offset, low) for offset, low, _ in pieces]
    arrays = [piece for _, _, piece in pieces]
    outs = tuple(
        jax.ShapeDtypeStruct(shape, jnp.bfloat16)
        for shape in ((rows, 2 * cols), (rows, cols), (rows, width), (2 * rows, 2 * cols), (2 * rows, cols))
    )
    dense = (in_gain, k_gain, cosine, sine)
    return pl.pallas_call(
        functools.partial(project_pair_body, places),
        name="project_pair",
        grid=(1,),
        out_shape=outs,
        in_specs=[smem_spec()] + [full_spec(a) for a in dense] + [any_spec()] * (4 + len(arrays)),
        out_specs=tuple(full_spec(o) for o in outs),
        scratch_shapes=[
            pltpu.VMEM((rows, width), jnp.bfloat16),
            pltpu.VMEM((2 * rows, width), jnp.bfloat16),
            pltpu.VMEM((width, cols), jnp.bfloat16),
            pltpu.VMEM((width, cols), jnp.bfloat16),
            pltpu.VMEM((width, 2 * cols), jnp.bfloat16),
            pltpu.SemaphoreType.DMA((4,)),
            pltpu.SemaphoreType.DMA((len(arrays),)),
        ],
        compiler_params=params(63),
        cost_estimate=cost(12 * rows * width * cols, block, w_key, w_value, *arrays, *outs),
    )(info, *dense, w_key, w_value, ready, block, *arrays)


def attend_body(reach, slots, info, lowest, q_gain, cosine, sine, queries, grads, *rest):
    blocks = rest[: (reach + 1) * slots]
    rest = rest[(reach + 1) * slots :]
    query_grads, own = rest[0], rest[1]
    far = rest[2 : 2 + reach]
    keys, values, key_sum, value_sum = rest[2 + reach :]
    rows = queries.shape[0]
    head_size = q_gain.shape[1]
    group = queries.shape[1] // head_size
    tile = blocks[0].shape[0]
    margin = reach * rows
    for slot in range(slots):
        start = info[slot] * tile
        for section in range(reach + 1):
            place = pl.ds(pl.multiple_of(section * rows + start, tile), tile)
            block = blocks[section * slots + slot]
            keys[place, :] = block[:, :head_size]
            values[place, :] = block[:, head_size:]
    key_sum[...] = jnp.zeros_like(key_sum)
    value_sum[...] = jnp.zeros_like(value_sum)
    for index in range(rows // tile):
        top = index * tile
        low = max(0, (top + margin - WINDOW + 1) // tile * tile)
        high = top + tile + margin
        width = high - low
        cos_rows = cosine[top : top + tile, :]
        sin_rows = sine[top : top + tile, :]
        raw = []
        scales = []
        turned = []
        for head in range(group):
            raw.append(queries[top : top + tile, head * head_size : (head + 1) * head_size].astype(jnp.float32))
            scales.append(inv_rms(raw[head]))
            turned.append(rope(raw[head] * scales[head] * q_gain[...], cos_rows, sin_rows) * QUERY_SCALE)
        query_rows = jnp.concatenate(turned, axis=0).astype(jnp.bfloat16)
        grad_rows = jnp.concatenate(
            [grads[top : top + tile, head * head_size : (head + 1) * head_size] for head in range(group)], axis=0
        )
        key_rows = keys[low:high, :]
        value_rows = values[low:high, :]
        places = lax.broadcasted_iota(jnp.int32, (width, tile), 0) + low
        last = lax.broadcasted_iota(jnp.int32, (width, tile), 1) + (top + margin)
        allowed = (places >= lowest[:, top : top + tile]) & (places <= last)
        allowed = jnp.concatenate([allowed] * group, axis=1)
        exps = jnp.where(allowed, jnp.exp(dot_last(key_rows, query_rows)), 0.0)
        probs = exps * (1.0 / jnp.sum(exps, axis=0, keepdims=True))
        weights = probs.astype(jnp.bfloat16)
        along = dot_last(value_rows, grad_rows)
        deltas = jnp.sum(weights.astype(jnp.float32) * along, axis=0, keepdims=True)
        slopes = (probs * (along - deltas)).astype(jnp.bfloat16)
        key_sum[low:high, :] += jnp.dot(slopes, query_rows, preferred_element_type=jnp.float32)
        value_sum[low:high, :] += jnp.dot(weights, grad_rows, preferred_element_type=jnp.float32)
        back = dot_first(slopes, key_rows)
        for head in range(group):
            turned_back = rope_back(back[head * tile : (head + 1) * tile] * QUERY_SCALE, cos_rows, sin_rows)
            result = norm_back(turned_back, raw[head], scales[head], q_gain[...])
            query_grads[top : top + tile, head * head_size : (head + 1) * head_size] = result.astype(jnp.bfloat16)
    for section in range(reach):
        span = slice(section * rows, (section + 1) * rows)
        far[section][:, :head_size] = key_sum[span, :].astype(jnp.bfloat16)
        far[section][:, head_size:] = value_sum[span, :].astype(jnp.bfloat16)
    own[:, :head_size] = key_sum[margin:, :]
    own[:, head_size:] = value_sum[margin:, :]


def attend(head, kv_heads, reach, info, lowest, q_gain, cosine, sine, queries, grads, blocks):
    rows = queries.shape[0]
    head_size = q_gain.shape[1]
    slots = len(blocks) // (reach + 1)
    tile = rows // slots
    cols = queries.shape[1] // kv_heads
    pick = lambda *_: (0, head)
    arrays = [array for array, _ in blocks]
    outs = (
        jax.ShapeDtypeStruct((rows, cols), jnp.bfloat16),
        jax.ShapeDtypeStruct((rows, 2 * head_size), jnp.float32),
    ) + (jax.ShapeDtypeStruct((rows, 2 * head_size), jnp.bfloat16),) * reach
    dense = (lowest, q_gain, cosine, sine)
    window = (reach + 1) * rows
    return pl.pallas_call(
        functools.partial(attend_body, reach, slots),
        name="attend_head",
        grid=(1,),
        out_shape=outs,
        in_specs=[smem_spec()]
        + [full_spec(a) for a in dense]
        + [pl.BlockSpec((rows, cols), pick)] * 2
        + [pl.BlockSpec((tile, 2 * head_size), lambda *_, row=row: (row, head)) for _, row in blocks],
        out_specs=[full_spec(o) for o in outs],
        scratch_shapes=[pltpu.VMEM((window, head_size), jnp.bfloat16)] * 2
        + [pltpu.VMEM((window, head_size), jnp.float32)] * 2,
        compiler_params=params(63),
        cost_estimate=cost(10 * rows * window * cols, queries, grads, *outs),
    )(info, *dense, queries, grads, *arrays)


def finish_body(reach, slots, info, k_gain, cosine, sine, own, *rest):
    arrived = rest[:reach]
    raw_keys = rest[reach : reach + slots]
    outs = rest[reach + slots :]
    result = outs[0]
    head_size = k_gain.shape[1]
    rows = raw_keys[0].shape[0]
    for slot in range(slots):
        place = pl.ds(pl.multiple_of(info[slot] * rows, rows), rows)
        total = own[place, :]
        for part in arrived:
            total = total + part[place, :].astype(jnp.float32)
        values = raw_keys[slot][...].astype(jnp.float32)
        turned = rope_back(total[:, :head_size], cosine[place, :], sine[place, :])
        keys = norm_back(turned, values, inv_rms(values), k_gain[...]).astype(jnp.bfloat16)
        result[place, :head_size] = keys
        result[place, head_size:] = total[:, head_size:].astype(jnp.bfloat16)
        if len(outs) > 1 and slot % 2:
            low = slot // 2 * rows
            outs[1][low : low + rows, :head_size] = keys
            outs[1][low : low + rows, head_size:] = total[:, head_size:].astype(jnp.bfloat16)


def finish(head, info, k_gain, cosine, sine, own, arrived, raw_keys, trading=False):
    rows, cols = own.shape
    head_size = k_gain.shape[1]
    slots = len(raw_keys)
    tile = rows // slots
    arrays = [array for array, _ in raw_keys]
    outs = [jax.ShapeDtypeStruct((count, cols), jnp.bfloat16) for count in (rows, 2 * tile)[: 1 + trading]]
    dense = (k_gain, cosine, sine, own, *arrived)
    results = pl.pallas_call(
        functools.partial(finish_body, len(arrived), slots),
        name="finish_kv",
        grid=(1,),
        out_shape=tuple(outs),
        in_specs=[smem_spec()]
        + [full_spec(a) for a in dense]
        + [pl.BlockSpec((tile, head_size), lambda *_, row=row: (row, head)) for _, row in raw_keys],
        out_specs=tuple(full_spec(o) for o in outs),
        compiler_params=params(63),
        cost_estimate=cost(0, own, *arrived, *outs),
    )(info, *dense, *arrays)
    return list(results)


def weight_body(slots, info, grads, *rest):
    blocks = rest[:slots]
    send, keep, held = rest[slots:]
    rows = blocks[0].shape[0]
    chunk = send.shape[1]
    own = info[slots]
    left = jnp.concatenate([block[...] for block in blocks], axis=0)
    right = jnp.concatenate(
        [grads[pl.ds(pl.multiple_of(info[slot] * rows, rows), rows), :] for slot in range(slots)], axis=0
    )
    held[...] = dot_first(left, right)
    for pair in range(send.shape[0]):
        other = pl.ds(pl.multiple_of((2 * pair + 1 - own) * chunk, 8), chunk)
        mine = pl.ds(pl.multiple_of((2 * pair + own) * chunk, 8), chunk)
        send[pair] = held[other, :].astype(jnp.bfloat16)
        keep[pair] = held[mine, :].astype(jnp.bfloat16)


def weight_terms(info, grads, blocks, chunk):
    rows, width = blocks[0].shape
    cols = grads.shape[1]
    tile = math.lcm(2 * chunk, 128)
    pairs = tile // (2 * chunk)
    out = jax.ShapeDtypeStruct((width // (2 * chunk), chunk, cols), jnp.bfloat16)
    out_spec = pl.BlockSpec((pairs, chunk, cols), lambda step: (step, 0, 0))
    return pl.pallas_call(
        functools.partial(weight_body, len(blocks)),
        name="weight_terms",
        grid=(width // tile,),
        out_shape=(out, out),
        in_specs=[smem_spec(), full_spec(grads)]
        + [pl.BlockSpec((rows, tile), lambda step: (0, step))] * len(blocks),
        out_specs=(out_spec, out_spec),
        scratch_shapes=[pltpu.VMEM((tile, cols), jnp.float32)],
        compiler_params=params(),
        cost_estimate=cost(0),
    )(info, grads, *blocks)


def add(left, right):
    return left.astype(jnp.float32) + right.astype(jnp.float32)


def split_body(halves, info, *rest):
    keeps, arrivals, outs = rest[: len(halves)], rest[len(halves) : 2 * len(halves)], rest[2 * len(halves) :]
    for index, (cols, outer, inner) in enumerate(halves):
        own = info[index]
        for high in range(outer):
            for low in range(inner):
                for side, target in ((1 - own, outs[2 * index]), (own, outs[2 * index + 1])):
                    place = (high * 2 + side) * inner + low
                    total = add(keeps[index][place, :, cols], arrivals[index][place, :, cols])
                    target[high * inner + low] = total.astype(jnp.bfloat16)


def row_steps(rows):
    return max(n for n in range(1, 5) if rows % (16 * n) == 0) if rows % 16 == 0 else 1


def split_sum(info, keeps, arrivals, halves):
    outs = []
    for keep, (cols, outer, inner) in zip(keeps, halves):
        outs += [jax.ShapeDtypeStruct((outer * inner, keep.shape[1], cols.stop - cols.start), jnp.bfloat16)] * 2
    rows = keeps[0].shape[1]
    steps = row_steps(rows)

    def spec(array):
        return pl.BlockSpec((array.shape[0], rows // steps, array.shape[2]), lambda step: (0, step, 0))

    return pl.pallas_call(
        functools.partial(split_body, halves),
        name="split_sum",
        grid=(steps,),
        out_shape=tuple(outs),
        in_specs=[smem_spec()] + [spec(a) for a in (*keeps, *arrivals)],
        out_specs=tuple(spec(o) for o in outs),
        compiler_params=params(),
        cost_estimate=cost(0),
    )(info, *keeps, *arrivals)


def swap(array, bit):
    size = lax.axis_size("seq")
    return lax.ppermute(array, "seq", [(i, i ^ (1 << bit)) for i in range(size)])


def scatter_sum(send, keep):
    bits = lax.axis_size("seq").bit_length() - 1
    index = lax.axis_index("seq")
    half = keep.shape[2] // 2
    routes = (list(range(1, bits)), list(range(bits - 1, 0, -1)))
    lefts = [list(range(1, bits)), list(range(1, bits))]
    arrival = swap(send, 0)
    keeps, arrivals = [keep, keep], [arrival, arrival]
    cols = [slice(0, half), slice(half, 2 * half)]
    for step in range(bits - 1):
        turn = [route[step] for route in routes]
        halves = []
        for path in range(2):
            place = lefts[path].index(turn[path])
            halves.append((cols[path], 1 << (len(lefts[path]) - 1 - place), 1 << place))
            lefts[path].remove(turn[path])
        info = jnp.stack([(index >> bit) & 1 for bit in turn]).astype(jnp.int32)
        sent_a, kept_a, sent_b, kept_b = split_sum(info, keeps, arrivals, tuple(halves))
        arrivals = [swap(sent_a, turn[0]), swap(sent_b, turn[1])]
        keeps = [kept_a, kept_b]
        cols = [slice(0, half), slice(0, half)]
    return keeps, arrivals


def gather_body(heads, *rest):
    parts = rest[: 4 * heads]
    outs = rest[4 * heads :]
    size = parts[0].shape[2]
    for head in range(heads):
        for side in range(2):
            keep, arrival = parts[4 * head + side], parts[4 * head + 2 + side]
            outs[side][:, head * size : (head + 1) * size] = add(keep[0], arrival[0])


def gather_heads(parts, heads):
    _, rows, cols = parts[0].shape
    steps = row_steps(rows)
    out = jax.ShapeDtypeStruct((rows, cols * heads), jnp.float32)
    out_spec = pl.BlockSpec((rows // steps, cols * heads), lambda step: (step, 0))
    return pl.pallas_call(
        functools.partial(gather_body, heads),
        name="gather_heads",
        grid=(steps,),
        out_shape=(out, out),
        in_specs=[pl.BlockSpec((1, rows // steps, cols), lambda step: (0, step, 0)) for a in parts],
        out_specs=(out_spec, out_spec),
        compiler_params=params(),
        cost_estimate=cost(0),
    )(*parts)


def input_terms_body(heads, w_key, w_value, *rest):
    grads, out = rest[:heads], rest[heads]
    size = grads[0].shape[1] // 2
    left = jnp.concatenate([g[:, :size] for g in grads] + [g[:, size:] for g in grads], axis=1)
    right = jnp.concatenate([w_key[...], w_value[...]], axis=1)
    out[...] = dot_last(left, right).astype(jnp.bfloat16)


def input_terms(kv_grads, w_key, w_value, skip):
    width, cols = w_key.shape
    rows = kv_grads[0].shape[0]
    common = math.gcd(skip, width - skip)
    tile = max(t for t in range(128, 1025, 128) if common % t == 0)
    out = jax.ShapeDtypeStruct((rows, width - skip), jnp.bfloat16)
    weight_spec = pl.BlockSpec((tile, cols), lambda step: (step + skip // tile, 0))
    return pl.pallas_call(
        functools.partial(input_terms_body, len(kv_grads)),
        name="input_terms",
        grid=((width - skip) // tile,),
        out_shape=out,
        in_specs=[weight_spec, weight_spec] + [full_spec(g) for g in kv_grads],
        out_specs=pl.BlockSpec((rows, tile), lambda step: (0, step)),
        compiler_params=params(),
        cost_estimate=cost(4 * rows * (width - skip) * cols, out, *kv_grads),
    )(w_key, w_value, *kv_grads)


def pair_body(places, heads, info, w_key, w_value, *rest):
    joined, arrived = rest[:heads], rest[heads : 2 * heads]
    pieces = rest[2 * heads : 2 * heads + len(places)]
    away_out, own_out, key_held, value_held, held, own_sems, sems = rest[2 * heads + len(places) :]
    rows, width = own_out.shape
    size = w_key.shape[1] // heads
    half = width // 2
    slice_rows = pieces[0].shape[0]
    split = half // slice_rows
    first = info[0] // split
    copies = piece_copies(places, info[0], pieces, held, sems)
    spans, groups = [], []
    for number in range(2):
        span = pl.ds(pl.multiple_of(jnp.bitwise_xor(first, number) * half, 128), half)
        spans.append(span)
        groups.append(
            [
                pltpu.make_async_copy(w_key.at[span, :], key_held.at[span, :], own_sems.at[2 * number]),
                pltpu.make_async_copy(w_value.at[span, :], value_held.at[span, :], own_sems.at[2 * number + 1]),
            ]
            + [copy for copy, (offset, _) in zip(copies, places) if offset // split == number]
        )
        start_all(groups[number])
    own_rows = [
        jnp.concatenate(
            [part[pl.ds(pl.multiple_of(info[1 + number] * rows, rows), rows), :] for number in range(2)], axis=0
        )
        for part in joined
    ]
    sides = [
        block[:, side * size : (side + 1) * size]
        for blocks in (own_rows, [part[...] for part in arrived])
        for side in range(2)
        for block in blocks
    ]
    left = jnp.concatenate(sides, axis=1)
    for span, group in zip(spans, groups):
        wait_all(group)
        right = jnp.concatenate([key_held[span, :], value_held[span, :], held[span, :]], axis=1)
        total = dot_last(left, right).astype(jnp.bfloat16)
        own_out[:, span] = total[:rows]
        away_out[:, span] = total[rows:]


def pair_terms(info, joined, arrived, pieces, w_key, w_value, heads):
    rows = arrived[0].shape[0] // 2
    width, cols = w_key.shape
    places = [(offset, low) for offset, low, _ in pieces]
    arrays = [piece for _, _, piece in pieces]
    outs = (jax.ShapeDtypeStruct((rows, width), jnp.bfloat16),) * 2
    return pl.pallas_call(
        functools.partial(pair_body, places, heads),
        name="pair_terms",
        grid=(1,),
        out_shape=outs,
        in_specs=[smem_spec(), any_spec(), any_spec()]
        + [full_spec(a) for a in (*joined, *arrived)]
        + [any_spec()] * len(arrays),
        out_specs=tuple(full_spec(o) for o in outs),
        scratch_shapes=[
            pltpu.VMEM((width, cols), jnp.bfloat16),
            pltpu.VMEM((width, cols), jnp.bfloat16),
            pltpu.VMEM((width, 2 * cols), jnp.bfloat16),
            pltpu.SemaphoreType.DMA((4,)),
            pltpu.SemaphoreType.DMA((len(arrays),)),
        ],
        compiler_params=params(63),
        cost_estimate=cost(16 * rows * width * cols, w_key, w_value, *arrays, *outs),
    )(info, w_key, w_value, *joined, *arrived, *arrays)


def input_grad_body(count, steps, tokens, gain, *rest):
    pieces = rest[:count]
    out, held, piece_held, out_held, sems, out_sems = rest[count:]
    rows = out_held.shape[0] // steps
    arrays = [(tokens, held)] + [(piece, piece_held.at[number]) for number, piece in enumerate(pieces)]
    copies = []
    for step in range(steps):
        span = pl.ds(step * rows, rows)
        copies.append(
            [
                pltpu.make_async_copy(source.at[span], target.at[span], sems.at[step, number])
                for number, (source, target) in enumerate(arrays)
            ]
        )
        start_all(copies[step])
    results = []
    for step in range(steps):
        span = slice(step * rows, (step + 1) * rows)
        wait_all(copies[step])
        values = held[span, :].astype(jnp.float32)
        grads = piece_held[0, span, :].astype(jnp.float32)
        for number in range(1, count):
            grads = grads + piece_held[number, span, :].astype(jnp.float32)
        out_held[span, :] = norm_back(grads, values, inv_rms(values), gain[...]).astype(jnp.bfloat16)
        span = pl.ds(step * rows, rows)
        results.append(pltpu.make_async_copy(out_held.at[span], out.at[span], out_sems.at[step]))
        results[step].start()
    wait_all(results)


def input_grad(tokens, gain, pieces):
    out = jax.ShapeDtypeStruct(tokens.shape, jnp.bfloat16)
    rows, width = tokens.shape
    steps = 4 if rows % 64 == 0 else 1
    return pl.pallas_call(
        functools.partial(input_grad_body, len(pieces), steps),
        name="input_grad",
        grid=(1,),
        out_shape=out,
        in_specs=[any_spec(), full_spec(gain)] + [any_spec()] * len(pieces),
        out_specs=any_spec(),
        scratch_shapes=[
            pltpu.VMEM((rows, width), jnp.bfloat16),
            pltpu.VMEM((len(pieces), rows, width), jnp.bfloat16),
            pltpu.VMEM((rows, width), jnp.bfloat16),
            pltpu.SemaphoreType.DMA((steps, 1 + len(pieces))),
            pltpu.SemaphoreType.DMA((steps,)),
        ],
        compiler_params=params(63),
        cost_estimate=cost(0, tokens, *pieces, out),
    )(tokens, gain, *pieces)


def spread_corners(parts):
    half = parts[0].shape[1] // 2
    return [swap(parts[1][:, :half], 2), swap(parts[2][:, half:], 1)]


def spread_end(arrays):
    half = arrays[0].shape[1] // 2
    spots = [(0, 0), (2, 0), (4, 0), (6, 0), (6, half)]
    return [(offset, low, array) for (offset, low), array in zip(spots, arrays)] + [
        (offset + 1, low, swap(array, 0)) for (offset, low), array in zip(spots, arrays)
    ]


def arrival_table(count):
    table = []
    for place in range(count):
        arrivals = []
        for step in range(1, count):
            if place - step >= 0:
                arrivals.append((2 * (step - 1), place - step))
            if place + step < count:
                arrivals.append((2 * (step - 1) + 1, place + step))
        table.append(arrivals)
    return table


def halo_of(key_value, reach):
    seq_count = lax.axis_size("seq")
    sent = []
    for distance in range(1, reach + 1):
        pairs = [(i, i + distance) for i in range(seq_count - distance)]
        sent.append(lax.ppermute(key_value, "seq", pairs))
    return sent


def halo_back(sections):
    seq_count = lax.axis_size("seq")
    back = []
    for section, array in enumerate(sections):
        distance = len(sections) - section
        pairs = [(i + distance, i) for i in range(seq_count - distance)]
        back.append(lax.ppermute(array, "seq", pairs))
    return back


def shards_general(tokens, dense, rope_rows, lowest, raw_queries, out_grad, w_key, w_value, reach):
    gain_row, q_row, k_row = dense
    cosine, sine = rope_rows
    tp_count = lax.axis_size("tp")
    place = lax.axis_index("tp").astype(jnp.int32)
    rows = tokens.shape[0]
    head_size = q_row.shape[1]
    kv_heads = w_key.shape[1] // head_size
    table = arrival_table(tp_count)
    picks = jnp.array(table, dtype=jnp.int32).reshape(tp_count, tp_count - 1, 2)
    picks = lax.dynamic_index_in_dim(picks, place, 0, keepdims=False)
    infos = [jnp.stack([jnp.int32(0), place])] + [picks[i] for i in range(tp_count - 1)]
    slot_places = jnp.concatenate([place[None], picks[:, 1]])
    normed_blocks, kv_blocks, raw_keys = [], [], []
    halo = [[] for _ in range(reach)]
    arrivals = []
    going_up = going_down = tokens
    for slot in range(tp_count):
        candidates = [tokens] if slot == 0 else list(arrivals)
        if slot < tp_count - 1:
            going_up = lax.ppermute(going_up, "tp", [(i, i + 1) for i in range(slot, tp_count - 1)])
            going_down = lax.ppermute(going_down, "tp", [(i + 1, i) for i in range(tp_count - 1 - slot)])
            arrivals += [going_up, going_down]
        key_value, keys, normed = project(infos[slot], candidates, gain_row, k_row, cosine, sine, w_key, w_value)
        normed_blocks.append(normed)
        kv_blocks.append(key_value)
        raw_keys.append((keys, 0))
        for distance, sent in enumerate(halo_of(key_value, reach)):
            halo[distance].append((sent, 0))
    blocks = [block for distance in range(reach, 0, -1) for block in halo[distance - 1]]
    blocks += [(block, 0) for block in kv_blocks]
    query_parts, kv_grads = [], []
    for head in range(kv_heads):
        outs = attend(head, kv_heads, reach, slot_places, lowest, q_row, cosine, sine, raw_queries, out_grad, blocks)
        query_parts.append(outs[0])
        back = halo_back(outs[2:])
        kv_grads += finish(head, slot_places, k_row, cosine, sine, outs[1], back, raw_keys)
    grad_queries = jnp.concatenate(query_parts, axis=1)
    partial_sum = input_terms(kv_grads, w_key, w_value, 0)
    summed_part = lax.psum_scatter(partial_sum, "tp", scatter_dimension=0, tiled=True)
    grad_x = input_grad(tokens, gain_row, [summed_part])
    left = jnp.concatenate(normed_blocks, axis=0)
    order = (slot_places[:, None] * rows + jnp.arange(rows, dtype=jnp.int32)[None, :]).reshape(-1)
    joined = [g[:, :head_size] for g in kv_grads] + [g[:, head_size:] for g in kv_grads]
    right = jnp.take(jnp.concatenate(joined, axis=1), order, axis=0)
    summed = lax.psum_scatter(dot_first(left, right), "seq", scatter_dimension=0, tiled=True)
    return (grad_x, grad_queries, summed[:, : w_key.shape[1]], summed[:, w_key.shape[1] :])


def trade(array, distance):
    return lax.ppermute(array, "tp", [(i, i ^ distance) for i in range(lax.axis_size("tp"))])


def shards_paired(tokens, dense, rope_rows, lowest, raw_queries, out_grad, w_key, w_value, reach, once):
    gain_row, q_row, k_row = dense
    cosine, sine = rope_rows
    seq_count = lax.axis_size("seq")
    seq_index = lax.axis_index("seq").astype(jnp.int32)
    place = lax.axis_index("tp").astype(jnp.int32)
    width, cols = w_key.shape
    head_size = q_row.shape[1]
    kv_heads = cols // head_size
    chunk = width // seq_count
    zero = jnp.zeros_like(place)
    slot_places = jnp.stack([place, place ^ 1, place ^ 2, place ^ 3])

    own_slice = jnp.concatenate(
        [lax.dynamic_slice_in_dim(weight, seq_index * chunk, chunk, 0) for weight in (w_key, w_value)], axis=1
    )
    distant = trade(after(tokens, own_slice), 2)

    partner_slice = trade(own_slice, 1)
    info = jnp.stack([zero, place])
    kv_0, keys_0, normed_0 = project(info, [tokens], gain_row, k_row, cosine, sine, w_key, w_value)
    halo_0 = halo_of(kv_0, reach)
    first_slice = after(partner_slice, (normed_0, halo_0))
    spread = [first_slice, swap(first_slice, 1), swap(first_slice, 2)]
    partner_normed_0 = trade(after(normed_0, partner_slice), 1)
    spread += spread_corners(spread)
    pieces = spread_end(spread)
    info = jnp.stack([seq_index, place, place ^ 2])
    far_block = after(distant, [piece for _, _, piece in pieces])
    kv_2, keys_2, normed_2, far_kv, far_keys = project_pair(
        info, normed_0, far_block, gain_row, k_row, cosine, sine, w_key, w_value, pieces
    )
    arrived_kv = trade(far_kv, 1)
    arrived_keys = trade(far_keys, 1)
    halo_2 = halo_of(kv_2, reach)
    arrived_kv = after(arrived_kv, (arrived_keys, partner_normed_0))
    halo_far = halo_of(arrived_kv, reach)
    partner_normed_2 = trade(after(normed_2, arrived_kv), 1)

    blocks = []
    for distance in range(reach, 0, -1):
        outer = halo_far[distance - 1]
        blocks += [(halo_0[distance - 1], 0), (outer, 0), (halo_2[distance - 1], 0), (outer, 1)]
    blocks += [(kv_0, 0), (arrived_kv, 0), (kv_2, 0), (arrived_kv, 1)]
    raw_keys = [(keys_0, 0), (arrived_keys, 0), (keys_2, 0), (arrived_keys, 1)]
    normed = [normed_0, partner_normed_0, normed_2, partner_normed_2]
    weight_info = jnp.concatenate([slot_places, (seq_index & 1)[None]])
    query_parts, kv_grads, arrived = [], [], []
    for head in range(kv_heads):
        outs = attend(head, kv_heads, reach, slot_places, lowest, q_row, cosine, sine, raw_queries, out_grad, blocks)
        query_parts.append(outs[0])
        back = halo_back(outs[2:])
        own = after(outs[1], arrived)
        grads, away = finish(head, slot_places, k_row, cosine, sine, own, back, raw_keys, trading=True)
        kv_grads.append(grads)
        arrived.append(trade(away, 1))
    grad_queries = jnp.concatenate(query_parts, axis=1)

    info = jnp.stack([seq_index, place, place ^ 2])
    away_terms, own_terms = pair_terms(info, kv_grads, arrived, pieces, w_key, w_value, kv_heads)
    other_terms = trade(away_terms, 2)

    def weight_step(step, _):
        parts = []
        for grads in kv_grads:
            send, keep = weight_terms(weight_info + step, grads, normed, chunk)
            keeps, comings = scatter_sum(send, keep)
            parts += [*keeps, *comings]
        return gather_heads(parts, kv_heads)

    empty = jnp.zeros((chunk, cols), jnp.float32)
    grad_wk, grad_wv = lax.fori_loop(0, after(once, away_terms), weight_step, (empty, empty))
    own_terms = after(own_terms, (grad_wk, grad_wv, grad_queries))
    grad_x = input_grad(tokens, gain_row, [own_terms, other_terms])
    return (grad_x, grad_queries, grad_wk, grad_wv)


def shards(tokens, in_gain, raw_queries, w_key, w_value, q_gain, k_gain, doc_lengths, out_grad):
    seq_count = lax.axis_size("seq")
    tp_count = lax.axis_size("tp")
    rows, width = tokens.shape
    shard_rows = rows * tp_count
    reach = (WINDOW - 2) // shard_rows + 1
    first_row = lax.axis_index("seq") * shard_rows
    positions = first_row + jnp.arange(shard_rows, dtype=jnp.int32)
    begins = doc_begin(doc_lengths, positions)
    rope_rows = rope_tables(positions - begins, q_gain.shape[0])
    lowest = jnp.maximum(begins, positions - (WINDOW - 1)) - (first_row - reach * shard_rows)
    dense = (in_gain[None, :], q_gain[None, :], k_gain[None, :])
    chunk = width // seq_count
    paired = (
        tp_count == 1 << 2
        and seq_count == 1 << 3
        and chunk % 16 == 0
        and width % math.lcm(2 * chunk, 128) == 0
    )
    args = (tokens, dense, rope_rows, lowest[None, :], raw_queries, out_grad, w_key, w_value, reach)
    return shards_paired(*args, jnp.minimum(doc_lengths[0], 1)) if paired else shards_general(*args)


def solution(mesh):
    placed = (
        P(("seq", "tp"), None),
        P(),
        P("seq", "tp"),
        P(None, "tp"),
        P(None, "tp"),
        P(),
        P(),
        P(),
        P("seq", "tp"),
    )
    return jax.shard_map(
        shards,
        mesh=mesh,
        in_specs=placed,
        out_specs=(P(("seq", "tp"), None), P("seq", "tp"), P("seq", "tp"), P("seq", "tp")),
        check_vma=False,
    )
```

```python
import functools
import math

import jax
import jax.numpy as jnp
from jax import lax
from jax.experimental import pallas as pl
from jax.experimental.pallas import tpu as pltpu
from jax.sharding import PartitionSpec as P

WINDOW = 1024
EPSILON = 1e-06
QUERY_SCALE = 168.0 ** (-0.5)
ROPE_BASE = 10000.0
SMEM = pltpu.SMEM


def doc_begin(doc_lengths, positions):
    endings = jnp.cumsum(doc_lengths, dtype=jnp.int32)
    starts = endings - doc_lengths
    inside = starts[None, :] <= positions[:, None]
    return jnp.max(jnp.where(inside, starts[None, :], jnp.zeros_like(starts)[None, :]), axis=1)


def rope_tables(offsets, head_size):
    half_size = head_size // 2
    powers = jnp.arange(half_size, dtype=jnp.float32) * (2.0 / head_size)
    frequency = ROPE_BASE ** (-powers)
    angles = offsets.astype(jnp.float32)[:, None] * frequency[None, :]
    cosine = jnp.cos(angles)
    sine = jnp.sin(angles)
    return jnp.concatenate([cosine, cosine], axis=1), jnp.concatenate([-sine, sine], axis=1)


def half_turn(values):
    return pltpu.roll(values, values.shape[-1] // 2, values.ndim - 1)


def rope(values, cosine, sine):
    return values * cosine + half_turn(values) * sine


def rope_back(grads, cosine, sine):
    return grads * cosine + half_turn(grads * sine)


def inv_rms(values):
    return lax.rsqrt(jnp.mean(values * values, axis=-1, keepdims=True) + EPSILON)


def norm_back(grads, values, scale, gain):
    scaled = grads * gain
    mean = jnp.mean(values * scaled, axis=-1, keepdims=True)
    return scale * scaled - values * (scale * scale * scale * mean)


def dot_last(left, right):
    return lax.dot_general(left, right, (((1,), (1,)), ((), ())), preferred_element_type=jnp.float32)


def dot_first(left, right):
    return lax.dot_general(left, right, (((0,), (0,)), ((), ())), preferred_element_type=jnp.float32)


def full_spec(array):
    return pl.BlockSpec(array.shape, lambda *_: (0,) * array.ndim)


def any_spec():
    return pl.BlockSpec(memory_space=pl.ANY)


def smem_spec():
    return pl.BlockSpec(memory_space=SMEM)


def after(value, others):
    return lax.optimization_barrier((value, others))[0]


def cost(flops, *arrays):
    size = sum(math.prod(a.shape) * jnp.dtype(a.dtype).itemsize for a in arrays)
    return pl.CostEstimate(flops=flops, bytes_accessed=size, transcendentals=0)


def params(megabytes=30):
    return pltpu.CompilerParams(vmem_limit_bytes=megabytes * 1024 * 1024)


def start_all(copies):
    for copy in copies:
        copy.start()


def wait_all(copies):
    for copy in copies:
        copy.wait()


def piece_copies(places, seq_index, arrays, target, sems):
    copies = []
    for number, (offset, low) in enumerate(places):
        rows, cols = arrays[number].shape
        start = pl.multiple_of(jnp.bitwise_xor(seq_index, offset) * rows, 16)
        slot = target.at[pl.ds(start, rows), pl.ds(low, cols)]
        copies.append(pltpu.make_async_copy(arrays[number], slot, sems.at[number]))
    return copies


def store_heads(key_value, raw_keys, rows, keys, values, k_gain, cos_rows, sin_rows):
    head_size = k_gain.shape[1]
    raw_keys[rows, :] = keys.astype(raw_keys.dtype)
    for head in range(keys.shape[1] // head_size):
        cols = slice(head * head_size, (head + 1) * head_size)
        low = 2 * head * head_size
        head_keys = keys[:, cols]
        turned = rope(head_keys * inv_rms(head_keys) * k_gain[...], cos_rows, sin_rows)
        key_value[rows, low : low + head_size] = turned.astype(jnp.bfloat16)
        key_value[rows, low + head_size : low + 2 * head_size] = values[:, cols].astype(jnp.bfloat16)


def project_body(count, info, gain, k_gain, cosine, sine, w_key, w_value, *rest):
    blocks = rest[:count]
    key_value, raw_keys, normed, held, key_held, value_held, sems = rest[count:]
    rows = held.shape[0]

    def block_copy(index):
        return pltpu.make_async_copy(blocks[index], held, sems.at[2])

    for index in range(count):
        pl.when(info[0] == index)(lambda index=index: block_copy(index).start())
    own_copies = [
        pltpu.make_async_copy(w_key, key_held, sems.at[0]),
        pltpu.make_async_copy(w_value, value_held, sems.at[1]),
    ]
    start_all(own_copies)
    for index in range(count):
        pl.when(info[0] == index)(lambda index=index: block_copy(index).wait())
    values = held[...].astype(jnp.float32)
    normed[...] = (values * inv_rms(values) * gain[...]).astype(jnp.bfloat16)
    place = pl.ds(pl.multiple_of(info[1] * rows, rows), rows)
    wait_all(own_copies)
    keys = jnp.dot(normed[...], key_held[...], preferred_element_type=jnp.float32)
    vals = jnp.dot(normed[...], value_held[...], preferred_element_type=jnp.float32)
    store_heads(key_value, raw_keys, slice(0, rows), keys, vals, k_gain, cosine[place, :], sine[place, :])


def project(info, blocks, in_gain, k_gain, cosine, sine, w_key, w_value):
    rows, width = blocks[0].shape
    cols = w_key.shape[1]
    outs = [
        jax.ShapeDtypeStruct((rows, 2 * cols), jnp.bfloat16),
        jax.ShapeDtypeStruct((rows, cols), jnp.bfloat16),
        jax.ShapeDtypeStruct((rows, width), jnp.bfloat16),
    ]
    scratch = [
        pltpu.VMEM((rows, width), jnp.bfloat16),
        pltpu.VMEM((width, cols), jnp.bfloat16),
        pltpu.VMEM((width, cols), jnp.bfloat16),
        pltpu.SemaphoreType.DMA((3,)),
    ]
    dense = (in_gain, k_gain, cosine, sine)
    return pl.pallas_call(
        functools.partial(project_body, len(blocks)),
        name="project_block",
        grid=(1,),
        out_shape=tuple(outs),
        in_specs=[smem_spec()] + [full_spec(a) for a in dense] + [any_spec()] * (2 + len(blocks)),
        out_specs=tuple(full_spec(o) for o in outs),
        scratch_shapes=scratch,
        compiler_params=params(63),
        cost_estimate=cost(4 * rows * width * cols, blocks[0], w_key, w_value, *outs),
    )(info, *dense, w_key, w_value, *blocks)


def cut_copies(source, target, first, rows, parts, sems, low):
    size = rows // parts
    copies = []
    for part in range(parts):
        span = pl.ds(pl.multiple_of(first + part * size, 16), size)
        copies.append(pltpu.make_async_copy(source.at[span, :], target.at[span, :], sems.at[low + part]))
    return copies


def project_pair_body(places, info, gain, k_gain, cosine, sine, w_key, w_value, ready, block, *rest):
    pieces = rest[: len(places)]
    key_value, raw_keys, normed, far_key_value, far_keys = rest[len(places) : len(places) + 5]
    held, left, key_held, value_held, far_held, sems, far_sems = rest[len(places) + 5 :]
    rows, width = held.shape
    cols = w_key.shape[1]
    block_copy = pltpu.make_async_copy(block, held, sems.at[2])
    block_copy.start()
    ready_copy = pltpu.make_async_copy(ready, left.at[pl.ds(0, rows)], sems.at[3])
    ready_copy.start()
    far_copies = piece_copies(places, info[0], pieces, far_held, far_sems)
    start_all(far_copies)
    own_copies = [
        pltpu.make_async_copy(w_key, key_held, sems.at[0]),
        pltpu.make_async_copy(w_value, value_held, sems.at[1]),
    ]
    start_all(own_copies)
    block_copy.wait()
    values = held[...].astype(jnp.float32)
    normed[...] = (values * inv_rms(values) * gain[...]).astype(jnp.bfloat16)
    ready_copy.wait()
    left[rows:, :] = normed[...]
    wait_all(far_copies)
    both = jnp.dot(left[...], far_held[...], preferred_element_type=jnp.float32)
    for number in range(2):
        place = pl.ds(pl.multiple_of(info[1 + number] * rows, rows), rows)
        span = slice(number * rows, (number + 1) * rows)
        part = both[span]
        store_heads(
            far_key_value, far_keys, span, part[:, :cols], part[:, cols:], k_gain, cosine[place, :], sine[place, :]
        )
    place = pl.ds(pl.multiple_of(info[2] * rows, rows), rows)
    wait_all(own_copies)
    keys = jnp.dot(normed[...], key_held[...], preferred_element_type=jnp.float32)
    vals = jnp.dot(normed[...], value_held[...], preferred_element_type=jnp.float32)
    store_heads(key_value, raw_keys, slice(0, rows), keys, vals, k_gain, cosine[place, :], sine[place, :])


def project_pair(info, ready, block, in_gain, k_gain, cosine, sine, w_key, w_value, pieces):
    rows, width = block.shape
    cols = w_key.shape[1]
    places = [(offset, low) for offset, low, _ in pieces]
    arrays = [piece for _, _, piece in pieces]
    outs = tuple(
        jax.ShapeDtypeStruct(shape, jnp.bfloat16)
        for shape in ((rows, 2 * cols), (rows, cols), (rows, width), (2 * rows, 2 * cols), (2 * rows, cols))
    )
    dense = (in_gain, k_gain, cosine, sine)
    return pl.pallas_call(
        functools.partial(project_pair_body, places),
        name="project_pair",
        grid=(1,),
        out_shape=outs,
        in_specs=[smem_spec()] + [full_spec(a) for a in dense] + [any_spec()] * (4 + len(arrays)),
        out_specs=tuple(full_spec(o) for o in outs),
        scratch_shapes=[
            pltpu.VMEM((rows, width), jnp.bfloat16),
            pltpu.VMEM((2 * rows, width), jnp.bfloat16),
            pltpu.VMEM((width, cols), jnp.bfloat16),
            pltpu.VMEM((width, cols), jnp.bfloat16),
            pltpu.VMEM((width, 2 * cols), jnp.bfloat16),
            pltpu.SemaphoreType.DMA((4,)),
            pltpu.SemaphoreType.DMA((len(arrays),)),
        ],
        compiler_params=params(63),
        cost_estimate=cost(12 * rows * width * cols, block, w_key, w_value, *arrays, *outs),
    )(info, *dense, w_key, w_value, ready, block, *arrays)


def attend_body(reach, slots, info, lowest, q_gain, cosine, sine, queries, grads, *rest):
    blocks = rest[: (reach + 1) * slots]
    rest = rest[(reach + 1) * slots :]
    query_grads, own = rest[0], rest[1]
    far = rest[2 : 2 + reach]
    keys, values, key_sum, value_sum = rest[2 + reach :]
    rows = queries.shape[0]
    head_size = q_gain.shape[1]
    group = queries.shape[1] // head_size
    tile = blocks[0].shape[0]
    margin = reach * rows
    for slot in range(slots):
        start = info[slot] * tile
        for section in range(reach + 1):
            place = pl.ds(pl.multiple_of(section * rows + start, tile), tile)
            block = blocks[section * slots + slot]
            keys[place, :] = block[:, :head_size]
            values[place, :] = block[:, head_size:]
    key_sum[...] = jnp.zeros_like(key_sum)
    value_sum[...] = jnp.zeros_like(value_sum)
    for index in range(rows // tile):
        top = index * tile
        low = max(0, (top + margin - WINDOW + 1) // tile * tile)
        high = top + tile + margin
        width = high - low
        cos_rows = cosine[top : top + tile, :]
        sin_rows = sine[top : top + tile, :]
        raw = []
        scales = []
        turned = []
        for head in range(group):
            raw.append(queries[top : top + tile, head * head_size : (head + 1) * head_size].astype(jnp.float32))
            scales.append(inv_rms(raw[head]))
            turned.append(rope(raw[head] * scales[head] * q_gain[...], cos_rows, sin_rows) * QUERY_SCALE)
        query_rows = jnp.concatenate(turned, axis=0).astype(jnp.bfloat16)
        grad_rows = jnp.concatenate(
            [grads[top : top + tile, head * head_size : (head + 1) * head_size] for head in range(group)], axis=0
        )
        key_rows = keys[low:high, :]
        value_rows = values[low:high, :]
        places = lax.broadcasted_iota(jnp.int32, (width, tile), 0) + low
        last = lax.broadcasted_iota(jnp.int32, (width, tile), 1) + (top + margin)
        allowed = (places >= lowest[:, top : top + tile]) & (places <= last)
        allowed = jnp.concatenate([allowed] * group, axis=1)
        exps = jnp.where(allowed, jnp.exp(dot_last(key_rows, query_rows)), 0.0)
        probs = exps * (1.0 / jnp.sum(exps, axis=0, keepdims=True))
        weights = probs.astype(jnp.bfloat16)
        along = dot_last(value_rows, grad_rows)
        deltas = jnp.sum(weights.astype(jnp.float32) * along, axis=0, keepdims=True)
        slopes = (probs * (along - deltas)).astype(jnp.bfloat16)
        key_sum[low:high, :] += jnp.dot(slopes, query_rows, preferred_element_type=jnp.float32)
        value_sum[low:high, :] += jnp.dot(weights, grad_rows, preferred_element_type=jnp.float32)
        back = dot_first(slopes, key_rows)
        for head in range(group):
            turned_back = rope_back(back[head * tile : (head + 1) * tile] * QUERY_SCALE, cos_rows, sin_rows)
            result = norm_back(turned_back, raw[head], scales[head], q_gain[...])
            query_grads[top : top + tile, head * head_size : (head + 1) * head_size] = result.astype(jnp.bfloat16)
    for section in range(reach):
        span = slice(section * rows, (section + 1) * rows)
        far[section][:, :head_size] = key_sum[span, :].astype(jnp.bfloat16)
        far[section][:, head_size:] = value_sum[span, :].astype(jnp.bfloat16)
    own[:, :head_size] = key_sum[margin:, :]
    own[:, head_size:] = value_sum[margin:, :]


def attend(head, kv_heads, reach, info, lowest, q_gain, cosine, sine, queries, grads, blocks):
    rows = queries.shape[0]
    head_size = q_gain.shape[1]
    slots = len(blocks) // (reach + 1)
    tile = rows // slots
    cols = queries.shape[1] // kv_heads
    pick = lambda *_: (0, head)
    arrays = [array for array, _ in blocks]
    outs = (
        jax.ShapeDtypeStruct((rows, cols), jnp.bfloat16),
        jax.ShapeDtypeStruct((rows, 2 * head_size), jnp.float32),
    ) + (jax.ShapeDtypeStruct((rows, 2 * head_size), jnp.bfloat16),) * reach
    dense = (lowest, q_gain, cosine, sine)
    window = (reach + 1) * rows
    return pl.pallas_call(
        functools.partial(attend_body, reach, slots),
        name="attend_head",
        grid=(1,),
        out_shape=outs,
        in_specs=[smem_spec()]
        + [full_spec(a) for a in dense]
        + [pl.BlockSpec((rows, cols), pick)] * 2
        + [pl.BlockSpec((tile, 2 * head_size), lambda *_, row=row: (row, head)) for _, row in blocks],
        out_specs=[full_spec(o) for o in outs],
        scratch_shapes=[pltpu.VMEM((window, head_size), jnp.bfloat16)] * 2
        + [pltpu.VMEM((window, head_size), jnp.float32)] * 2,
        compiler_params=params(63),
        cost_estimate=cost(10 * rows * window * cols, queries, grads, *outs),
    )(info, *dense, queries, grads, *arrays)


def finish_body(reach, slots, info, k_gain, cosine, sine, own, *rest):
    arrived = rest[:reach]
    raw_keys = rest[reach : reach + slots]
    outs = rest[reach + slots :]
    result = outs[0]
    head_size = k_gain.shape[1]
    rows = raw_keys[0].shape[0]
    for slot in range(slots):
        place = pl.ds(pl.multiple_of(info[slot] * rows, rows), rows)
        total = own[place, :]
        for part in arrived:
            total = total + part[place, :].astype(jnp.float32)
        values = raw_keys[slot][...].astype(jnp.float32)
        turned = rope_back(total[:, :head_size], cosine[place, :], sine[place, :])
        keys = norm_back(turned, values, inv_rms(values), k_gain[...]).astype(jnp.bfloat16)
        result[place, :head_size] = keys
        result[place, head_size:] = total[:, head_size:].astype(jnp.bfloat16)
        if len(outs) > 1 and slot % 2:
            low = slot // 2 * rows
            outs[1][low : low + rows, :head_size] = keys
            outs[1][low : low + rows, head_size:] = total[:, head_size:].astype(jnp.bfloat16)


def finish(head, info, k_gain, cosine, sine, own, arrived, raw_keys, trading=False):
    rows, cols = own.shape
    head_size = k_gain.shape[1]
    slots = len(raw_keys)
    tile = rows // slots
    arrays = [array for array, _ in raw_keys]
    outs = [jax.ShapeDtypeStruct((count, cols), jnp.bfloat16) for count in (rows, 2 * tile)[: 1 + trading]]
    dense = (k_gain, cosine, sine, own, *arrived)
    results = pl.pallas_call(
        functools.partial(finish_body, len(arrived), slots),
        name="finish_kv",
        grid=(1,),
        out_shape=tuple(outs),
        in_specs=[smem_spec()]
        + [full_spec(a) for a in dense]
        + [pl.BlockSpec((tile, head_size), lambda *_, row=row: (row, head)) for _, row in raw_keys],
        out_specs=tuple(full_spec(o) for o in outs),
        compiler_params=params(63),
        cost_estimate=cost(0, own, *arrived, *outs),
    )(info, *dense, *arrays)
    return list(results)


def weight_body(slots, info, grads, *rest):
    blocks = rest[:slots]
    send, keep, held = rest[slots:]
    rows = blocks[0].shape[0]
    chunk = send.shape[1]
    own = info[slots]
    left = jnp.concatenate([block[...] for block in blocks], axis=0)
    right = jnp.concatenate(
        [grads[pl.ds(pl.multiple_of(info[slot] * rows, rows), rows), :] for slot in range(slots)], axis=0
    )
    held[...] = dot_first(left, right)
    for pair in range(send.shape[0]):
        other = pl.ds(pl.multiple_of((2 * pair + 1 - own) * chunk, 8), chunk)
        mine = pl.ds(pl.multiple_of((2 * pair + own) * chunk, 8), chunk)
        send[pair] = held[other, :].astype(jnp.bfloat16)
        keep[pair] = held[mine, :].astype(jnp.bfloat16)


def weight_terms(info, grads, blocks, chunk):
    rows, width = blocks[0].shape
    cols = grads.shape[1]
    tile = math.lcm(2 * chunk, 128)
    pairs = tile // (2 * chunk)
    out = jax.ShapeDtypeStruct((width // (2 * chunk), chunk, cols), jnp.bfloat16)
    out_spec = pl.BlockSpec((pairs, chunk, cols), lambda step: (step, 0, 0))
    return pl.pallas_call(
        functools.partial(weight_body, len(blocks)),
        name="weight_terms",
        grid=(width // tile,),
        out_shape=(out, out),
        in_specs=[smem_spec(), full_spec(grads)]
        + [pl.BlockSpec((rows, tile), lambda step: (0, step))] * len(blocks),
        out_specs=(out_spec, out_spec),
        scratch_shapes=[pltpu.VMEM((tile, cols), jnp.float32)],
        compiler_params=params(),
        cost_estimate=cost(0),
    )(info, grads, *blocks)


def add(left, right):
    return left.astype(jnp.float32) + right.astype(jnp.float32)


def split_body(halves, info, *rest):
    keeps, arrivals, outs = rest[: len(halves)], rest[len(halves) : 2 * len(halves)], rest[2 * len(halves) :]
    for index, (cols, outer, inner) in enumerate(halves):
        own = info[index]
        for high in range(outer):
            for low in range(inner):
                for side, target in ((1 - own, outs[2 * index]), (own, outs[2 * index + 1])):
                    place = (high * 2 + side) * inner + low
                    total = add(keeps[index][place, :, cols], arrivals[index][place, :, cols])
                    target[high * inner + low] = total.astype(jnp.bfloat16)


def row_steps(rows):
    return max(n for n in range(1, 5) if rows % (16 * n) == 0) if rows % 16 == 0 else 1


def split_sum(info, keeps, arrivals, halves):
    outs = []
    for keep, (cols, outer, inner) in zip(keeps, halves):
        outs += [jax.ShapeDtypeStruct((outer * inner, keep.shape[1], cols.stop - cols.start), jnp.bfloat16)] * 2
    rows = keeps[0].shape[1]
    steps = row_steps(rows)

    def spec(array):
        return pl.BlockSpec((array.shape[0], rows // steps, array.shape[2]), lambda step: (0, step, 0))

    return pl.pallas_call(
        functools.partial(split_body, halves),
        name="split_sum",
        grid=(steps,),
        out_shape=tuple(outs),
        in_specs=[smem_spec()] + [spec(a) for a in (*keeps, *arrivals)],
        out_specs=tuple(spec(o) for o in outs),
        compiler_params=params(),
        cost_estimate=cost(0),
    )(info, *keeps, *arrivals)


def swap(array, bit):
    size = lax.axis_size("seq")
    return lax.ppermute(array, "seq", [(i, i ^ (1 << bit)) for i in range(size)])


def scatter_sum(send, keep):
    bits = lax.axis_size("seq").bit_length() - 1
    index = lax.axis_index("seq")
    half = keep.shape[2] // 2
    routes = (list(range(1, bits)), list(range(bits - 1, 0, -1)))
    lefts = [list(range(1, bits)), list(range(1, bits))]
    arrival = swap(send, 0)
    keeps, arrivals = [keep, keep], [arrival, arrival]
    cols = [slice(0, half), slice(half, 2 * half)]
    for step in range(bits - 1):
        turn = [route[step] for route in routes]
        halves = []
        for path in range(2):
            place = lefts[path].index(turn[path])
            halves.append((cols[path], 1 << (len(lefts[path]) - 1 - place), 1 << place))
            lefts[path].remove(turn[path])
        info = jnp.stack([(index >> bit) & 1 for bit in turn]).astype(jnp.int32)
        sent_a, kept_a, sent_b, kept_b = split_sum(info, keeps, arrivals, tuple(halves))
        arrivals = [swap(sent_a, turn[0]), swap(sent_b, turn[1])]
        keeps = [kept_a, kept_b]
        cols = [slice(0, half), slice(0, half)]
    return keeps, arrivals


def gather_body(heads, *rest):
    parts = rest[: 4 * heads]
    outs = rest[4 * heads :]
    size = parts[0].shape[2]
    for head in range(heads):
        for side in range(2):
            keep, arrival = parts[4 * head + side], parts[4 * head + 2 + side]
            outs[side][:, head * size : (head + 1) * size] = add(keep[0], arrival[0])


def gather_heads(parts, heads):
    _, rows, cols = parts[0].shape
    steps = row_steps(rows)
    out = jax.ShapeDtypeStruct((rows, cols * heads), jnp.float32)
    out_spec = pl.BlockSpec((rows // steps, cols * heads), lambda step: (step, 0))
    return pl.pallas_call(
        functools.partial(gather_body, heads),
        name="gather_heads",
        grid=(steps,),
        out_shape=(out, out),
        in_specs=[pl.BlockSpec((1, rows // steps, cols), lambda step: (0, step, 0)) for a in parts],
        out_specs=(out_spec, out_spec),
        compiler_params=params(),
        cost_estimate=cost(0),
    )(*parts)


def input_terms_body(heads, w_key, w_value, *rest):
    grads, out = rest[:heads], rest[heads]
    size = grads[0].shape[1] // 2
    left = jnp.concatenate([g[:, :size] for g in grads] + [g[:, size:] for g in grads], axis=1)
    right = jnp.concatenate([w_key[...], w_value[...]], axis=1)
    out[...] = dot_last(left, right).astype(jnp.bfloat16)


def input_terms(kv_grads, w_key, w_value, skip):
    width, cols = w_key.shape
    rows = kv_grads[0].shape[0]
    common = math.gcd(skip, width - skip)
    tile = max(t for t in range(128, 1025, 128) if common % t == 0)
    out = jax.ShapeDtypeStruct((rows, width - skip), jnp.bfloat16)
    weight_spec = pl.BlockSpec((tile, cols), lambda step: (step + skip // tile, 0))
    return pl.pallas_call(
        functools.partial(input_terms_body, len(kv_grads)),
        name="input_terms",
        grid=((width - skip) // tile,),
        out_shape=out,
        in_specs=[weight_spec, weight_spec] + [full_spec(g) for g in kv_grads],
        out_specs=pl.BlockSpec((rows, tile), lambda step: (0, step)),
        compiler_params=params(),
        cost_estimate=cost(4 * rows * (width - skip) * cols, out, *kv_grads),
    )(w_key, w_value, *kv_grads)


def pair_body(places, heads, info, w_key, w_value, *rest):
    joined, arrived = rest[:heads], rest[heads : 2 * heads]
    pieces = rest[2 * heads : 2 * heads + len(places)]
    away_out, own_out, key_held, value_held, held, own_sems, sems = rest[2 * heads + len(places) :]
    rows, width = own_out.shape
    size = w_key.shape[1] // heads
    half = width // 2
    slice_rows = pieces[0].shape[0]
    split = half // slice_rows
    first = info[0] // split
    copies = piece_copies(places, info[0], pieces, held, sems)
    spans, groups = [], []
    for number in range(2):
        span = pl.ds(pl.multiple_of(jnp.bitwise_xor(first, number) * half, 128), half)
        spans.append(span)
        low = jnp.bitwise_xor(first, number) * half
        groups.append(
            cut_copies(w_key, key_held, low, half, 4, own_sems, 8 * number)
            + cut_copies(w_value, value_held, low, half, 4, own_sems, 8 * number + 4)
            + [copy for copy, (offset, _) in zip(copies, places) if offset // split == number]
        )
        start_all(groups[number])
    own_rows = [
        jnp.concatenate(
            [part[pl.ds(pl.multiple_of(info[1 + number] * rows, rows), rows), :] for number in range(2)], axis=0
        )
        for part in joined
    ]
    sides = [
        block[:, side * size : (side + 1) * size]
        for blocks in (own_rows, [part[...] for part in arrived])
        for side in range(2)
        for block in blocks
    ]
    left = jnp.concatenate(sides, axis=1)
    for span, group in zip(spans, groups):
        wait_all(group)
        right = jnp.concatenate([key_held[span, :], value_held[span, :], held[span, :]], axis=1)
        total = dot_last(left, right).astype(jnp.bfloat16)
        own_out[:, span] = total[:rows]
        away_out[:, span] = total[rows:]


def pair_terms(info, joined, arrived, pieces, w_key, w_value, heads):
    rows = arrived[0].shape[0] // 2
    width, cols = w_key.shape
    places = [(offset, low) for offset, low, _ in pieces]
    arrays = [piece for _, _, piece in pieces]
    outs = (jax.ShapeDtypeStruct((rows, width), jnp.bfloat16),) * 2
    return pl.pallas_call(
        functools.partial(pair_body, places, heads),
        name="pair_terms",
        grid=(1,),
        out_shape=outs,
        in_specs=[smem_spec(), any_spec(), any_spec()]
        + [full_spec(a) for a in (*joined, *arrived)]
        + [any_spec()] * len(arrays),
        out_specs=tuple(full_spec(o) for o in outs),
        scratch_shapes=[
            pltpu.VMEM((width, cols), jnp.bfloat16),
            pltpu.VMEM((width, cols), jnp.bfloat16),
            pltpu.VMEM((width, 2 * cols), jnp.bfloat16),
            pltpu.SemaphoreType.DMA((16,)),
            pltpu.SemaphoreType.DMA((len(arrays),)),
        ],
        compiler_params=params(63),
        cost_estimate=cost(16 * rows * width * cols, w_key, w_value, *arrays, *outs),
    )(info, w_key, w_value, *joined, *arrived, *arrays)


def input_grad_body(count, steps, tokens, gain, *rest):
    pieces = rest[:count]
    out, held, piece_held, out_held, sems, out_sems = rest[count:]
    rows = out_held.shape[0] // steps
    arrays = [(tokens, held)] + [(piece, piece_held.at[number]) for number, piece in enumerate(pieces)]
    copies = []
    for step in range(steps):
        span = pl.ds(step * rows, rows)
        copies.append(
            [
                pltpu.make_async_copy(source.at[span], target.at[span], sems.at[step, number])
                for number, (source, target) in enumerate(arrays)
            ]
        )
        start_all(copies[step])
    results = []
    for step in range(steps):
        span = slice(step * rows, (step + 1) * rows)
        wait_all(copies[step])
        values = held[span, :].astype(jnp.float32)
        grads = piece_held[0, span, :].astype(jnp.float32)
        for number in range(1, count):
            grads = grads + piece_held[number, span, :].astype(jnp.float32)
        out_held[span, :] = norm_back(grads, values, inv_rms(values), gain[...]).astype(jnp.bfloat16)
        span = pl.ds(step * rows, rows)
        results.append(pltpu.make_async_copy(out_held.at[span], out.at[span], out_sems.at[step]))
        results[step].start()
    wait_all(results)


def input_grad(tokens, gain, pieces):
    out = jax.ShapeDtypeStruct(tokens.shape, jnp.bfloat16)
    rows, width = tokens.shape
    steps = 4 if rows % 64 == 0 else 1
    return pl.pallas_call(
        functools.partial(input_grad_body, len(pieces), steps),
        name="input_grad",
        grid=(1,),
        out_shape=out,
        in_specs=[any_spec(), full_spec(gain)] + [any_spec()] * len(pieces),
        out_specs=any_spec(),
        scratch_shapes=[
            pltpu.VMEM((rows, width), jnp.bfloat16),
            pltpu.VMEM((len(pieces), rows, width), jnp.bfloat16),
            pltpu.VMEM((rows, width), jnp.bfloat16),
            pltpu.SemaphoreType.DMA((steps, 1 + len(pieces))),
            pltpu.SemaphoreType.DMA((steps,)),
        ],
        compiler_params=params(63),
        cost_estimate=cost(0, tokens, *pieces, out),
    )(tokens, gain, *pieces)


def spread_corners(parts):
    half = parts[0].shape[1] // 2
    return [swap(parts[1][:, :half], 2), swap(parts[2][:, half:], 1)]


def spread_end(arrays):
    half = arrays[0].shape[1] // 2
    spots = [(0, 0), (2, 0), (4, 0), (6, 0), (6, half)]
    return [(offset, low, array) for (offset, low), array in zip(spots, arrays)] + [
        (offset + 1, low, swap(array, 0)) for (offset, low), array in zip(spots, arrays)
    ]


def arrival_table(count):
    table = []
    for place in range(count):
        arrivals = []
        for step in range(1, count):
            if place - step >= 0:
                arrivals.append((2 * (step - 1), place - step))
            if place + step < count:
                arrivals.append((2 * (step - 1) + 1, place + step))
        table.append(arrivals)
    return table


def halo_of(key_value, reach):
    seq_count = lax.axis_size("seq")
    sent = []
    for distance in range(1, reach + 1):
        pairs = [(i, i + distance) for i in range(seq_count - distance)]
        sent.append(lax.ppermute(key_value, "seq", pairs))
    return sent


def halo_back(sections):
    seq_count = lax.axis_size("seq")
    back = []
    for section, array in enumerate(sections):
        distance = len(sections) - section
        pairs = [(i + distance, i) for i in range(seq_count - distance)]
        back.append(lax.ppermute(array, "seq", pairs))
    return back


def shards_general(tokens, dense, rope_rows, lowest, raw_queries, out_grad, w_key, w_value, reach):
    gain_row, q_row, k_row = dense
    cosine, sine = rope_rows
    tp_count = lax.axis_size("tp")
    place = lax.axis_index("tp").astype(jnp.int32)
    rows = tokens.shape[0]
    head_size = q_row.shape[1]
    kv_heads = w_key.shape[1] // head_size
    table = arrival_table(tp_count)
    picks = jnp.array(table, dtype=jnp.int32).reshape(tp_count, tp_count - 1, 2)
    picks = lax.dynamic_index_in_dim(picks, place, 0, keepdims=False)
    infos = [jnp.stack([jnp.int32(0), place])] + [picks[i] for i in range(tp_count - 1)]
    slot_places = jnp.concatenate([place[None], picks[:, 1]])
    normed_blocks, kv_blocks, raw_keys = [], [], []
    halo = [[] for _ in range(reach)]
    arrivals = []
    going_up = going_down = tokens
    for slot in range(tp_count):
        candidates = [tokens] if slot == 0 else list(arrivals)
        if slot < tp_count - 1:
            going_up = lax.ppermute(going_up, "tp", [(i, i + 1) for i in range(slot, tp_count - 1)])
            going_down = lax.ppermute(going_down, "tp", [(i + 1, i) for i in range(tp_count - 1 - slot)])
            arrivals += [going_up, going_down]
        key_value, keys, normed = project(infos[slot], candidates, gain_row, k_row, cosine, sine, w_key, w_value)
        normed_blocks.append(normed)
        kv_blocks.append(key_value)
        raw_keys.append((keys, 0))
        for distance, sent in enumerate(halo_of(key_value, reach)):
            halo[distance].append((sent, 0))
    blocks = [block for distance in range(reach, 0, -1) for block in halo[distance - 1]]
    blocks += [(block, 0) for block in kv_blocks]
    query_parts, kv_grads = [], []
    for head in range(kv_heads):
        outs = attend(head, kv_heads, reach, slot_places, lowest, q_row, cosine, sine, raw_queries, out_grad, blocks)
        query_parts.append(outs[0])
        back = halo_back(outs[2:])
        kv_grads += finish(head, slot_places, k_row, cosine, sine, outs[1], back, raw_keys)
    grad_queries = jnp.concatenate(query_parts, axis=1)
    partial_sum = input_terms(kv_grads, w_key, w_value, 0)
    summed_part = lax.psum_scatter(partial_sum, "tp", scatter_dimension=0, tiled=True)
    grad_x = input_grad(tokens, gain_row, [summed_part])
    left = jnp.concatenate(normed_blocks, axis=0)
    order = (slot_places[:, None] * rows + jnp.arange(rows, dtype=jnp.int32)[None, :]).reshape(-1)
    joined = [g[:, :head_size] for g in kv_grads] + [g[:, head_size:] for g in kv_grads]
    right = jnp.take(jnp.concatenate(joined, axis=1), order, axis=0)
    summed = lax.psum_scatter(dot_first(left, right), "seq", scatter_dimension=0, tiled=True)
    return (grad_x, grad_queries, summed[:, : w_key.shape[1]], summed[:, w_key.shape[1] :])


def trade(array, distance):
    return lax.ppermute(array, "tp", [(i, i ^ distance) for i in range(lax.axis_size("tp"))])


def shards_paired(tokens, dense, rope_rows, lowest, raw_queries, out_grad, w_key, w_value, reach, once):
    gain_row, q_row, k_row = dense
    cosine, sine = rope_rows
    seq_count = lax.axis_size("seq")
    seq_index = lax.axis_index("seq").astype(jnp.int32)
    place = lax.axis_index("tp").astype(jnp.int32)
    width, cols = w_key.shape
    head_size = q_row.shape[1]
    kv_heads = cols // head_size
    chunk = width // seq_count
    zero = jnp.zeros_like(place)
    slot_places = jnp.stack([place, place ^ 1, place ^ 2, place ^ 3])

    own_slice = jnp.concatenate(
        [lax.dynamic_slice_in_dim(weight, seq_index * chunk, chunk, 0) for weight in (w_key, w_value)], axis=1
    )
    distant = trade(after(tokens, own_slice), 2)

    partner_slice = trade(own_slice, 1)
    info = jnp.stack([zero, place])
    kv_0, keys_0, normed_0 = project(info, [tokens], gain_row, k_row, cosine, sine, w_key, w_value)
    halo_0 = halo_of(kv_0, reach)
    first_slice = after(partner_slice, (normed_0, halo_0))
    spread = [first_slice, swap(first_slice, 1), swap(first_slice, 2)]
    partner_normed_0 = trade(after(normed_0, partner_slice), 1)
    spread += spread_corners(spread)
    pieces = spread_end(spread)
    info = jnp.stack([seq_index, place, place ^ 2])
    far_block = after(distant, [piece for _, _, piece in pieces])
    kv_2, keys_2, normed_2, far_kv, far_keys = project_pair(
        info, normed_0, far_block, gain_row, k_row, cosine, sine, w_key, w_value, pieces
    )
    arrived_kv = trade(far_kv, 1)
    arrived_keys = trade(far_keys, 1)
    halo_2 = halo_of(kv_2, reach)
    arrived_kv = after(arrived_kv, (arrived_keys, partner_normed_0))
    halo_far = halo_of(arrived_kv, reach)
    partner_normed_2 = trade(after(normed_2, arrived_kv), 1)

    blocks = []
    for distance in range(reach, 0, -1):
        outer = halo_far[distance - 1]
        blocks += [(halo_0[distance - 1], 0), (outer, 0), (halo_2[distance - 1], 0), (outer, 1)]
    blocks += [(kv_0, 0), (arrived_kv, 0), (kv_2, 0), (arrived_kv, 1)]
    raw_keys = [(keys_0, 0), (arrived_keys, 0), (keys_2, 0), (arrived_keys, 1)]
    normed = [normed_0, partner_normed_0, normed_2, partner_normed_2]
    weight_info = jnp.concatenate([slot_places, (seq_index & 1)[None]])
    query_parts, kv_grads, arrived = [], [], []
    for head in range(kv_heads):
        outs = attend(head, kv_heads, reach, slot_places, lowest, q_row, cosine, sine, raw_queries, out_grad, blocks)
        query_parts.append(outs[0])
        back = halo_back(outs[2:])
        own = after(outs[1], arrived)
        grads, away = finish(head, slot_places, k_row, cosine, sine, own, back, raw_keys, trading=True)
        kv_grads.append(grads)
        arrived.append(trade(away, 1))
    grad_queries = jnp.concatenate(query_parts, axis=1)

    info = jnp.stack([seq_index, place, place ^ 2])
    away_terms, own_terms = pair_terms(info, kv_grads, arrived, pieces, w_key, w_value, kv_heads)
    other_terms = trade(away_terms, 2)

    def weight_step(step, _):
        parts = []
        for grads in kv_grads:
            send, keep = weight_terms(weight_info + step, grads, normed, chunk)
            keeps, comings = scatter_sum(send, keep)
            parts += [*keeps, *comings]
        return gather_heads(parts, kv_heads)

    empty = jnp.zeros((chunk, cols), jnp.float32)
    grad_wk, grad_wv = lax.fori_loop(0, after(once, away_terms), weight_step, (empty, empty))
    own_terms = after(own_terms, (grad_wk, grad_wv, grad_queries))
    grad_x = input_grad(tokens, gain_row, [own_terms, other_terms])
    return (grad_x, grad_queries, grad_wk, grad_wv)


def shards(tokens, in_gain, raw_queries, w_key, w_value, q_gain, k_gain, doc_lengths, out_grad):
    seq_count = lax.axis_size("seq")
    tp_count = lax.axis_size("tp")
    rows, width = tokens.shape
    shard_rows = rows * tp_count
    reach = (WINDOW - 2) // shard_rows + 1
    first_row = lax.axis_index("seq") * shard_rows
    positions = first_row + jnp.arange(shard_rows, dtype=jnp.int32)
    begins = doc_begin(doc_lengths, positions)
    rope_rows = rope_tables(positions - begins, q_gain.shape[0])
    lowest = jnp.maximum(begins, positions - (WINDOW - 1)) - (first_row - reach * shard_rows)
    dense = (in_gain[None, :], q_gain[None, :], k_gain[None, :])
    chunk = width // seq_count
    paired = (
        tp_count == 1 << 2
        and seq_count == 1 << 3
        and chunk % 16 == 0
        and width % math.lcm(2 * chunk, 128) == 0
    )
    args = (tokens, dense, rope_rows, lowest[None, :], raw_queries, out_grad, w_key, w_value, reach)
    return shards_paired(*args, jnp.minimum(doc_lengths[0], 1)) if paired else shards_general(*args)


def solution(mesh):
    placed = (
        P(("seq", "tp"), None),
        P(),
        P("seq", "tp"),
        P(None, "tp"),
        P(None, "tp"),
        P(),
        P(),
        P(),
        P("seq", "tp"),
    )
    return jax.shard_map(
        shards,
        mesh=mesh,
        in_specs=placed,
        out_specs=(P(("seq", "tp"), None), P("seq", "tp"), P("seq", "tp"), P("seq", "tp")),
        check_vma=False,
    )
```

```python
import functools
import math

import jax
import jax.numpy as jnp
from jax import lax
from jax.experimental import pallas as pl
from jax.experimental.pallas import tpu as pltpu
from jax.sharding import PartitionSpec as P

WINDOW = 1024
EPSILON = 1e-06
QUERY_SCALE = 168.0 ** (-0.5)
ROPE_BASE = 10000.0
SMEM = pltpu.SMEM


def doc_begin(doc_lengths, positions):
    endings = jnp.cumsum(doc_lengths, dtype=jnp.int32)
    starts = endings - doc_lengths
    inside = starts[None, :] <= positions[:, None]
    return jnp.max(jnp.where(inside, starts[None, :], jnp.zeros_like(starts)[None, :]), axis=1)


def rope_tables(offsets, head_size):
    half_size = head_size // 2
    powers = jnp.arange(half_size, dtype=jnp.float32) * (2.0 / head_size)
    frequency = ROPE_BASE ** (-powers)
    angles = offsets.astype(jnp.float32)[:, None] * frequency[None, :]
    cosine = jnp.cos(angles)
    sine = jnp.sin(angles)
    return jnp.concatenate([cosine, cosine], axis=1), jnp.concatenate([-sine, sine], axis=1)


def half_turn(values):
    return pltpu.roll(values, values.shape[-1] // 2, values.ndim - 1)


def rope(values, cosine, sine):
    return values * cosine + half_turn(values) * sine


def rope_back(grads, cosine, sine):
    return grads * cosine + half_turn(grads * sine)


def inv_rms(values):
    return lax.rsqrt(jnp.mean(values * values, axis=-1, keepdims=True) + EPSILON)


def norm_back(grads, values, scale, gain):
    scaled = grads * gain
    mean = jnp.mean(values * scaled, axis=-1, keepdims=True)
    return scale * scaled - values * (scale * scale * scale * mean)


def dot_last(left, right):
    return lax.dot_general(left, right, (((1,), (1,)), ((), ())), preferred_element_type=jnp.float32)


def dot_first(left, right):
    return lax.dot_general(left, right, (((0,), (0,)), ((), ())), preferred_element_type=jnp.float32)


def full_spec(array):
    return pl.BlockSpec(array.shape, lambda *_: (0,) * array.ndim)


def any_spec():
    return pl.BlockSpec(memory_space=pl.ANY)


def smem_spec():
    return pl.BlockSpec(memory_space=SMEM)


def after(value, others):
    return lax.optimization_barrier((value, others))[0]


def cost(flops, *arrays):
    size = sum(math.prod(a.shape) * jnp.dtype(a.dtype).itemsize for a in arrays)
    return pl.CostEstimate(flops=flops, bytes_accessed=size, transcendentals=0)


def params(megabytes=30):
    return pltpu.CompilerParams(vmem_limit_bytes=megabytes * 1024 * 1024)


def start_all(copies):
    for copy in copies:
        copy.start()


def wait_all(copies):
    for copy in copies:
        copy.wait()


def piece_copies(places, seq_index, arrays, target, sems):
    copies = []
    for number, (offset, low) in enumerate(places):
        rows, cols = arrays[number].shape
        start = pl.multiple_of(jnp.bitwise_xor(seq_index, offset) * rows, 16)
        slot = target.at[pl.ds(start, rows), pl.ds(low, cols)]
        copies.append(pltpu.make_async_copy(arrays[number], slot, sems.at[number]))
    return copies


def store_heads(key_value, raw_keys, rows, keys, values, k_gain, cos_rows, sin_rows):
    head_size = k_gain.shape[1]
    raw_keys[rows, :] = keys.astype(raw_keys.dtype)
    for head in range(keys.shape[1] // head_size):
        cols = slice(head * head_size, (head + 1) * head_size)
        low = 2 * head * head_size
        head_keys = keys[:, cols]
        turned = rope(head_keys * inv_rms(head_keys) * k_gain[...], cos_rows, sin_rows)
        key_value[rows, low : low + head_size] = turned.astype(jnp.bfloat16)
        key_value[rows, low + head_size : low + 2 * head_size] = values[:, cols].astype(jnp.bfloat16)


def project_body(count, info, gain, k_gain, cosine, sine, w_key, w_value, *rest):
    blocks = rest[:count]
    key_value, raw_keys, normed, held, key_held, value_held, sems = rest[count:]
    rows = held.shape[0]

    def block_copy(index):
        return pltpu.make_async_copy(blocks[index], held, sems.at[2])

    for index in range(count):
        pl.when(info[0] == index)(lambda index=index: block_copy(index).start())
    own_copies = [
        pltpu.make_async_copy(w_key, key_held, sems.at[0]),
        pltpu.make_async_copy(w_value, value_held, sems.at[1]),
    ]
    start_all(own_copies)
    for index in range(count):
        pl.when(info[0] == index)(lambda index=index: block_copy(index).wait())
    values = held[...].astype(jnp.float32)
    normed[...] = (values * inv_rms(values) * gain[...]).astype(jnp.bfloat16)
    place = pl.ds(pl.multiple_of(info[1] * rows, rows), rows)
    wait_all(own_copies)
    keys = jnp.dot(normed[...], key_held[...], preferred_element_type=jnp.float32)
    vals = jnp.dot(normed[...], value_held[...], preferred_element_type=jnp.float32)
    store_heads(key_value, raw_keys, slice(0, rows), keys, vals, k_gain, cosine[place, :], sine[place, :])


def project(info, blocks, in_gain, k_gain, cosine, sine, w_key, w_value):
    rows, width = blocks[0].shape
    cols = w_key.shape[1]
    outs = [
        jax.ShapeDtypeStruct((rows, 2 * cols), jnp.bfloat16),
        jax.ShapeDtypeStruct((rows, cols), jnp.bfloat16),
        jax.ShapeDtypeStruct((rows, width), jnp.bfloat16),
    ]
    scratch = [
        pltpu.VMEM((rows, width), jnp.bfloat16),
        pltpu.VMEM((width, cols), jnp.bfloat16),
        pltpu.VMEM((width, cols), jnp.bfloat16),
        pltpu.SemaphoreType.DMA((3,)),
    ]
    dense = (in_gain, k_gain, cosine, sine)
    return pl.pallas_call(
        functools.partial(project_body, len(blocks)),
        name="project_block",
        grid=(1,),
        out_shape=tuple(outs),
        in_specs=[smem_spec()] + [full_spec(a) for a in dense] + [any_spec()] * (2 + len(blocks)),
        out_specs=tuple(full_spec(o) for o in outs),
        scratch_shapes=scratch,
        compiler_params=params(63),
        cost_estimate=cost(4 * rows * width * cols, blocks[0], w_key, w_value, *outs),
    )(info, *dense, w_key, w_value, *blocks)


def cut_copies(source, target, first, rows, parts, sems, low):
    size = rows // parts
    copies = []
    for part in range(parts):
        span = pl.ds(pl.multiple_of(first + part * size, 16), size)
        copies.append(pltpu.make_async_copy(source.at[span, :], target.at[span, :], sems.at[low + part]))
    return copies


def project_pair_body(places, info, gain, k_gain, cosine, sine, w_key, w_value, ready, block, *rest):
    pieces = rest[: len(places)]
    key_value, raw_keys, normed, far_key_value, far_keys = rest[len(places) : len(places) + 5]
    held, left, key_held, value_held, far_held, sems, far_sems = rest[len(places) + 5 :]
    rows, width = held.shape
    cols = w_key.shape[1]
    block_copy = pltpu.make_async_copy(block, held, sems.at[2])
    block_copy.start()
    ready_copy = pltpu.make_async_copy(ready, left.at[pl.ds(0, rows)], sems.at[3])
    ready_copy.start()
    far_copies = piece_copies(places, info[0], pieces, far_held, far_sems)
    start_all(far_copies)
    own_copies = [
        pltpu.make_async_copy(w_key, key_held, sems.at[0]),
        pltpu.make_async_copy(w_value, value_held, sems.at[1]),
    ]
    start_all(own_copies)
    block_copy.wait()
    values = held[...].astype(jnp.float32)
    normed[...] = (values * inv_rms(values) * gain[...]).astype(jnp.bfloat16)
    ready_copy.wait()
    left[rows:, :] = normed[...]
    wait_all(far_copies)
    both = jnp.dot(left[...], far_held[...], preferred_element_type=jnp.float32)
    for number in range(2):
        place = pl.ds(pl.multiple_of(info[1 + number] * rows, rows), rows)
        span = slice(number * rows, (number + 1) * rows)
        part = both[span]
        store_heads(
            far_key_value, far_keys, span, part[:, :cols], part[:, cols:], k_gain, cosine[place, :], sine[place, :]
        )
    place = pl.ds(pl.multiple_of(info[2] * rows, rows), rows)
    wait_all(own_copies)
    keys = jnp.dot(normed[...], key_held[...], preferred_element_type=jnp.float32)
    vals = jnp.dot(normed[...], value_held[...], preferred_element_type=jnp.float32)
    store_heads(key_value, raw_keys, slice(0, rows), keys, vals, k_gain, cosine[place, :], sine[place, :])


def project_pair(info, ready, block, in_gain, k_gain, cosine, sine, w_key, w_value, pieces):
    rows, width = block.shape
    cols = w_key.shape[1]
    places = [(offset, low) for offset, low, _ in pieces]
    arrays = [piece for _, _, piece in pieces]
    outs = tuple(
        jax.ShapeDtypeStruct(shape, jnp.bfloat16)
        for shape in ((rows, 2 * cols), (rows, cols), (rows, width), (2 * rows, 2 * cols), (2 * rows, cols))
    )
    dense = (in_gain, k_gain, cosine, sine)
    return pl.pallas_call(
        functools.partial(project_pair_body, places),
        name="project_pair",
        grid=(1,),
        out_shape=outs,
        in_specs=[smem_spec()] + [full_spec(a) for a in dense] + [any_spec()] * (4 + len(arrays)),
        out_specs=tuple(full_spec(o) for o in outs),
        scratch_shapes=[
            pltpu.VMEM((rows, width), jnp.bfloat16),
            pltpu.VMEM((2 * rows, width), jnp.bfloat16),
            pltpu.VMEM((width, cols), jnp.bfloat16),
            pltpu.VMEM((width, cols), jnp.bfloat16),
            pltpu.VMEM((width, 2 * cols), jnp.bfloat16),
            pltpu.SemaphoreType.DMA((4,)),
            pltpu.SemaphoreType.DMA((len(arrays),)),
        ],
        compiler_params=params(63),
        cost_estimate=cost(12 * rows * width * cols, block, w_key, w_value, *arrays, *outs),
    )(info, *dense, w_key, w_value, ready, block, *arrays)


def attend_body(reach, slots, info, lowest, q_gain, cosine, sine, queries, grads, *rest):
    blocks = rest[: (reach + 1) * slots]
    rest = rest[(reach + 1) * slots :]
    query_grads, own = rest[0], rest[1]
    far = rest[2 : 2 + reach]
    keys, values, key_sum, value_sum = rest[2 + reach :]
    rows = queries.shape[0]
    head_size = q_gain.shape[1]
    group = queries.shape[1] // head_size
    tile = blocks[0].shape[0]
    margin = reach * rows
    for slot in range(slots):
        start = info[slot] * tile
        for section in range(reach + 1):
            place = pl.ds(pl.multiple_of(section * rows + start, tile), tile)
            block = blocks[section * slots + slot]
            keys[place, :] = block[:, :head_size]
            values[place, :] = block[:, head_size:]
    key_sum[...] = jnp.zeros_like(key_sum)
    value_sum[...] = jnp.zeros_like(value_sum)
    for index in range(rows // tile):
        top = index * tile
        low = max(0, (top + margin - WINDOW + 1) // tile * tile)
        high = top + tile + margin
        width = high - low
        cos_rows = cosine[top : top + tile, :]
        sin_rows = sine[top : top + tile, :]
        raw = []
        scales = []
        turned = []
        for head in range(group):
            raw.append(queries[top : top + tile, head * head_size : (head + 1) * head_size].astype(jnp.float32))
            scales.append(inv_rms(raw[head]))
            turned.append(rope(raw[head] * scales[head] * q_gain[...], cos_rows, sin_rows) * QUERY_SCALE)
        query_rows = jnp.concatenate(turned, axis=0).astype(jnp.bfloat16)
        grad_rows = jnp.concatenate(
            [grads[top : top + tile, head * head_size : (head + 1) * head_size] for head in range(group)], axis=0
        )
        key_rows = keys[low:high, :]
        value_rows = values[low:high, :]
        places = lax.broadcasted_iota(jnp.int32, (width, tile), 0) + low
        last = lax.broadcasted_iota(jnp.int32, (width, tile), 1) + (top + margin)
        allowed = (places >= lowest[:, top : top + tile]) & (places <= last)
        allowed = jnp.concatenate([allowed] * group, axis=1)
        exps = jnp.where(allowed, jnp.exp(dot_last(key_rows, query_rows)), 0.0)
        probs = exps * (1.0 / jnp.sum(exps, axis=0, keepdims=True))
        weights = probs.astype(jnp.bfloat16)
        along = dot_last(value_rows, grad_rows)
        deltas = jnp.sum(weights.astype(jnp.float32) * along, axis=0, keepdims=True)
        slopes = (probs * (along - deltas)).astype(jnp.bfloat16)
        key_sum[low:high, :] += jnp.dot(slopes, query_rows, preferred_element_type=jnp.float32)
        value_sum[low:high, :] += jnp.dot(weights, grad_rows, preferred_element_type=jnp.float32)
        back = dot_first(slopes, key_rows)
        for head in range(group):
            turned_back = rope_back(back[head * tile : (head + 1) * tile] * QUERY_SCALE, cos_rows, sin_rows)
            result = norm_back(turned_back, raw[head], scales[head], q_gain[...])
            query_grads[top : top + tile, head * head_size : (head + 1) * head_size] = result.astype(jnp.bfloat16)
    for section in range(reach):
        span = slice(section * rows, (section + 1) * rows)
        far[section][:, :head_size] = key_sum[span, :].astype(jnp.bfloat16)
        far[section][:, head_size:] = value_sum[span, :].astype(jnp.bfloat16)
    own[:, :head_size] = key_sum[margin:, :]
    own[:, head_size:] = value_sum[margin:, :]


def attend(head, kv_heads, reach, info, lowest, q_gain, cosine, sine, queries, grads, blocks):
    rows = queries.shape[0]
    head_size = q_gain.shape[1]
    slots = len(blocks) // (reach + 1)
    tile = rows // slots
    cols = queries.shape[1] // kv_heads
    pick = lambda *_: (0, head)
    arrays = [array for array, _ in blocks]
    outs = (
        jax.ShapeDtypeStruct((rows, cols), jnp.bfloat16),
        jax.ShapeDtypeStruct((rows, 2 * head_size), jnp.float32),
    ) + (jax.ShapeDtypeStruct((rows, 2 * head_size), jnp.bfloat16),) * reach
    dense = (lowest, q_gain, cosine, sine)
    window = (reach + 1) * rows
    return pl.pallas_call(
        functools.partial(attend_body, reach, slots),
        name="attend_head",
        grid=(1,),
        out_shape=outs,
        in_specs=[smem_spec()]
        + [full_spec(a) for a in dense]
        + [pl.BlockSpec((rows, cols), pick)] * 2
        + [pl.BlockSpec((tile, 2 * head_size), lambda *_, row=row: (row, head)) for _, row in blocks],
        out_specs=[full_spec(o) for o in outs],
        scratch_shapes=[pltpu.VMEM((window, head_size), jnp.bfloat16)] * 2
        + [pltpu.VMEM((window, head_size), jnp.float32)] * 2,
        compiler_params=params(63),
        cost_estimate=cost(10 * rows * window * cols, queries, grads, *outs),
    )(info, *dense, queries, grads, *arrays)


def finish_body(reach, slots, info, k_gain, cosine, sine, own, *rest):
    arrived = rest[:reach]
    raw_keys = rest[reach : reach + slots]
    outs = rest[reach + slots :]
    result = outs[0]
    head_size = k_gain.shape[1]
    rows = raw_keys[0].shape[0]
    for slot in range(slots):
        place = pl.ds(pl.multiple_of(info[slot] * rows, rows), rows)
        total = own[place, :]
        for part in arrived:
            total = total + part[place, :].astype(jnp.float32)
        values = raw_keys[slot][...].astype(jnp.float32)
        turned = rope_back(total[:, :head_size], cosine[place, :], sine[place, :])
        keys = norm_back(turned, values, inv_rms(values), k_gain[...]).astype(jnp.bfloat16)
        result[place, :head_size] = keys
        result[place, head_size:] = total[:, head_size:].astype(jnp.bfloat16)
        if len(outs) > 1 and slot % 2:
            low = slot // 2 * rows
            outs[1][low : low + rows, :head_size] = keys
            outs[1][low : low + rows, head_size:] = total[:, head_size:].astype(jnp.bfloat16)


def finish(head, info, k_gain, cosine, sine, own, arrived, raw_keys, trading=False):
    rows, cols = own.shape
    head_size = k_gain.shape[1]
    slots = len(raw_keys)
    tile = rows // slots
    arrays = [array for array, _ in raw_keys]
    outs = [jax.ShapeDtypeStruct((count, cols), jnp.bfloat16) for count in (rows, 2 * tile)[: 1 + trading]]
    dense = (k_gain, cosine, sine, own, *arrived)
    results = pl.pallas_call(
        functools.partial(finish_body, len(arrived), slots),
        name="finish_kv",
        grid=(1,),
        out_shape=tuple(outs),
        in_specs=[smem_spec()]
        + [full_spec(a) for a in dense]
        + [pl.BlockSpec((tile, head_size), lambda *_, row=row: (row, head)) for _, row in raw_keys],
        out_specs=tuple(full_spec(o) for o in outs),
        compiler_params=params(63),
        cost_estimate=cost(0, own, *arrived, *outs),
    )(info, *dense, *arrays)
    return list(results)


def weight_body(slots, info, grads, *rest):
    blocks = rest[:slots]
    send, keep, held = rest[slots:]
    rows = blocks[0].shape[0]
    chunk = send.shape[1]
    own = info[slots]
    left = jnp.concatenate([block[...] for block in blocks], axis=0)
    right = jnp.concatenate(
        [grads[pl.ds(pl.multiple_of(info[slot] * rows, rows), rows), :] for slot in range(slots)], axis=0
    )
    held[...] = dot_first(left, right)
    for pair in range(send.shape[0]):
        other = pl.ds(pl.multiple_of((2 * pair + 1 - own) * chunk, 8), chunk)
        mine = pl.ds(pl.multiple_of((2 * pair + own) * chunk, 8), chunk)
        send[pair] = held[other, :].astype(jnp.bfloat16)
        keep[pair] = held[mine, :].astype(jnp.bfloat16)


def weight_terms(info, grads, blocks, chunk):
    rows, width = blocks[0].shape
    cols = grads.shape[1]
    tile = math.lcm(2 * chunk, 128)
    pairs = tile // (2 * chunk)
    out = jax.ShapeDtypeStruct((width // (2 * chunk), chunk, cols), jnp.bfloat16)
    out_spec = pl.BlockSpec((pairs, chunk, cols), lambda step: (step, 0, 0))
    return pl.pallas_call(
        functools.partial(weight_body, len(blocks)),
        name="weight_terms",
        grid=(width // tile,),
        out_shape=(out, out),
        in_specs=[smem_spec(), full_spec(grads)]
        + [pl.BlockSpec((rows, tile), lambda step: (0, step))] * len(blocks),
        out_specs=(out_spec, out_spec),
        scratch_shapes=[pltpu.VMEM((tile, cols), jnp.float32)],
        compiler_params=params(),
        cost_estimate=cost(0),
    )(info, grads, *blocks)


def add(left, right):
    return left.astype(jnp.float32) + right.astype(jnp.float32)


def split_body(halves, info, *rest):
    keeps, arrivals, outs = rest[: len(halves)], rest[len(halves) : 2 * len(halves)], rest[2 * len(halves) :]
    for index, (cols, outer, inner) in enumerate(halves):
        own = info[index]
        for high in range(outer):
            for low in range(inner):
                for side, target in ((1 - own, outs[2 * index]), (own, outs[2 * index + 1])):
                    place = (high * 2 + side) * inner + low
                    total = add(keeps[index][place, :, cols], arrivals[index][place, :, cols])
                    target[high * inner + low] = total.astype(jnp.bfloat16)


def row_steps(rows):
    return max(n for n in range(1, 5) if rows % (16 * n) == 0) if rows % 16 == 0 else 1


def split_sum(info, keeps, arrivals, halves):
    outs = []
    for keep, (cols, outer, inner) in zip(keeps, halves):
        outs += [jax.ShapeDtypeStruct((outer * inner, keep.shape[1], cols.stop - cols.start), jnp.bfloat16)] * 2
    rows = keeps[0].shape[1]
    steps = row_steps(rows)

    def spec(array):
        return pl.BlockSpec((array.shape[0], rows // steps, array.shape[2]), lambda step: (0, step, 0))

    return pl.pallas_call(
        functools.partial(split_body, halves),
        name="split_sum",
        grid=(steps,),
        out_shape=tuple(outs),
        in_specs=[smem_spec()] + [spec(a) for a in (*keeps, *arrivals)],
        out_specs=tuple(spec(o) for o in outs),
        compiler_params=params(),
        cost_estimate=cost(0),
    )(info, *keeps, *arrivals)


def swap(array, bit):
    size = lax.axis_size("seq")
    return lax.ppermute(array, "seq", [(i, i ^ (1 << bit)) for i in range(size)])


def scatter_sum(send, keep):
    bits = lax.axis_size("seq").bit_length() - 1
    index = lax.axis_index("seq")
    half = keep.shape[2] // 2
    routes = (list(range(1, bits)), list(range(bits - 1, 0, -1)))
    lefts = [list(range(1, bits)), list(range(1, bits))]
    arrival = swap(send, 0)
    keeps, arrivals = [keep, keep], [arrival, arrival]
    cols = [slice(0, half), slice(half, 2 * half)]
    for step in range(bits - 1):
        turn = [route[step] for route in routes]
        halves = []
        for path in range(2):
            place = lefts[path].index(turn[path])
            halves.append((cols[path], 1 << (len(lefts[path]) - 1 - place), 1 << place))
            lefts[path].remove(turn[path])
        info = jnp.stack([(index >> bit) & 1 for bit in turn]).astype(jnp.int32)
        sent_a, kept_a, sent_b, kept_b = split_sum(info, keeps, arrivals, tuple(halves))
        arrivals = [swap(sent_a, turn[0]), swap(sent_b, turn[1])]
        keeps = [kept_a, kept_b]
        cols = [slice(0, half), slice(0, half)]
    return keeps, arrivals


def gather_body(heads, *rest):
    parts = rest[: 4 * heads]
    outs = rest[4 * heads :]
    size = parts[0].shape[2]
    for head in range(heads):
        for side in range(2):
            keep, arrival = parts[4 * head + side], parts[4 * head + 2 + side]
            outs[side][:, head * size : (head + 1) * size] = add(keep[0], arrival[0])


def gather_heads(parts, heads):
    _, rows, cols = parts[0].shape
    steps = row_steps(rows)
    out = jax.ShapeDtypeStruct((rows, cols * heads), jnp.float32)
    out_spec = pl.BlockSpec((rows // steps, cols * heads), lambda step: (step, 0))
    return pl.pallas_call(
        functools.partial(gather_body, heads),
        name="gather_heads",
        grid=(steps,),
        out_shape=(out, out),
        in_specs=[pl.BlockSpec((1, rows // steps, cols), lambda step: (0, step, 0)) for a in parts],
        out_specs=(out_spec, out_spec),
        compiler_params=params(),
        cost_estimate=cost(0),
    )(*parts)


def input_terms_body(heads, w_key, w_value, *rest):
    grads, out = rest[:heads], rest[heads]
    size = grads[0].shape[1] // 2
    left = jnp.concatenate([g[:, :size] for g in grads] + [g[:, size:] for g in grads], axis=1)
    right = jnp.concatenate([w_key[...], w_value[...]], axis=1)
    out[...] = dot_last(left, right).astype(jnp.bfloat16)


def input_terms(kv_grads, w_key, w_value, skip):
    width, cols = w_key.shape
    rows = kv_grads[0].shape[0]
    common = math.gcd(skip, width - skip)
    tile = max(t for t in range(128, 1025, 128) if common % t == 0)
    out = jax.ShapeDtypeStruct((rows, width - skip), jnp.bfloat16)
    weight_spec = pl.BlockSpec((tile, cols), lambda step: (step + skip // tile, 0))
    return pl.pallas_call(
        functools.partial(input_terms_body, len(kv_grads)),
        name="input_terms",
        grid=((width - skip) // tile,),
        out_shape=out,
        in_specs=[weight_spec, weight_spec] + [full_spec(g) for g in kv_grads],
        out_specs=pl.BlockSpec((rows, tile), lambda step: (0, step)),
        compiler_params=params(),
        cost_estimate=cost(4 * rows * (width - skip) * cols, out, *kv_grads),
    )(w_key, w_value, *kv_grads)


def pair_body(places, heads, info, w_key, w_value, *rest):
    joined, arrived = rest[:heads], rest[heads : 2 * heads]
    pieces = rest[2 * heads : 2 * heads + len(places)]
    away_out, own_out, key_held, value_held, held, own_sems, sems = rest[2 * heads + len(places) :]
    rows, width = own_out.shape
    size = w_key.shape[1] // heads
    half = width // 2
    slice_rows = pieces[0].shape[0]
    split = half // slice_rows
    first = info[0] // split
    copies = piece_copies(places, info[0], pieces, held, sems)
    spans, groups = [], []
    for number in range(2):
        span = pl.ds(pl.multiple_of(jnp.bitwise_xor(first, number) * half, 128), half)
        spans.append(span)
        low = jnp.bitwise_xor(first, number) * half
        groups.append(
            cut_copies(w_key, key_held, low, half, 8, own_sems, 16 * number)
            + cut_copies(w_value, value_held, low, half, 8, own_sems, 16 * number + 8)
            + [copy for copy, (offset, _) in zip(copies, places) if offset // split == number]
        )
        start_all(groups[number])
    own_rows = [
        jnp.concatenate(
            [part[pl.ds(pl.multiple_of(info[1 + number] * rows, rows), rows), :] for number in range(2)], axis=0
        )
        for part in joined
    ]
    sides = [
        block[:, side * size : (side + 1) * size]
        for blocks in (own_rows, [part[...] for part in arrived])
        for side in range(2)
        for block in blocks
    ]
    left = jnp.concatenate(sides, axis=1)
    for span, group in zip(spans, groups):
        wait_all(group)
        right = jnp.concatenate([key_held[span, :], value_held[span, :], held[span, :]], axis=1)
        total = dot_last(left, right).astype(jnp.bfloat16)
        own_out[:, span] = total[:rows]
        away_out[:, span] = total[rows:]


def pair_terms(info, joined, arrived, pieces, w_key, w_value, heads):
    rows = arrived[0].shape[0] // 2
    width, cols = w_key.shape
    places = [(offset, low) for offset, low, _ in pieces]
    arrays = [piece for _, _, piece in pieces]
    outs = (jax.ShapeDtypeStruct((rows, width), jnp.bfloat16),) * 2
    return pl.pallas_call(
        functools.partial(pair_body, places, heads),
        name="pair_terms",
        grid=(1,),
        out_shape=outs,
        in_specs=[smem_spec(), any_spec(), any_spec()]
        + [full_spec(a) for a in (*joined, *arrived)]
        + [any_spec()] * len(arrays),
        out_specs=tuple(full_spec(o) for o in outs),
        scratch_shapes=[
            pltpu.VMEM((width, cols), jnp.bfloat16),
            pltpu.VMEM((width, cols), jnp.bfloat16),
            pltpu.VMEM((width, 2 * cols), jnp.bfloat16),
            pltpu.SemaphoreType.DMA((32,)),
            pltpu.SemaphoreType.DMA((len(arrays),)),
        ],
        compiler_params=params(63),
        cost_estimate=cost(16 * rows * width * cols, w_key, w_value, *arrays, *outs),
    )(info, w_key, w_value, *joined, *arrived, *arrays)


def input_grad_body(count, steps, tokens, gain, *rest):
    pieces = rest[:count]
    out, held, piece_held, out_held, sems, out_sems = rest[count:]
    rows = out_held.shape[0] // steps
    arrays = [(tokens, held)] + [(piece, piece_held.at[number]) for number, piece in enumerate(pieces)]
    copies = []
    for step in range(steps):
        span = pl.ds(step * rows, rows)
        copies.append(
            [
                pltpu.make_async_copy(source.at[span], target.at[span], sems.at[step, number])
                for number, (source, target) in enumerate(arrays)
            ]
        )
        start_all(copies[step])
    results = []
    for step in range(steps):
        span = slice(step * rows, (step + 1) * rows)
        wait_all(copies[step])
        values = held[span, :].astype(jnp.float32)
        grads = piece_held[0, span, :].astype(jnp.float32)
        for number in range(1, count):
            grads = grads + piece_held[number, span, :].astype(jnp.float32)
        out_held[span, :] = norm_back(grads, values, inv_rms(values), gain[...]).astype(jnp.bfloat16)
        span = pl.ds(step * rows, rows)
        results.append(pltpu.make_async_copy(out_held.at[span], out.at[span], out_sems.at[step]))
        results[step].start()
    wait_all(results)


def input_grad(tokens, gain, pieces):
    out = jax.ShapeDtypeStruct(tokens.shape, jnp.bfloat16)
    rows, width = tokens.shape
    steps = 4 if rows % 64 == 0 else 1
    return pl.pallas_call(
        functools.partial(input_grad_body, len(pieces), steps),
        name="input_grad",
        grid=(1,),
        out_shape=out,
        in_specs=[any_spec(), full_spec(gain)] + [any_spec()] * len(pieces),
        out_specs=any_spec(),
        scratch_shapes=[
            pltpu.VMEM((rows, width), jnp.bfloat16),
            pltpu.VMEM((len(pieces), rows, width), jnp.bfloat16),
            pltpu.VMEM((rows, width), jnp.bfloat16),
            pltpu.SemaphoreType.DMA((steps, 1 + len(pieces))),
            pltpu.SemaphoreType.DMA((steps,)),
        ],
        compiler_params=params(63),
        cost_estimate=cost(0, tokens, *pieces, out),
    )(tokens, gain, *pieces)


def spread_corners(parts):
    half = parts[0].shape[1] // 2
    return [swap(parts[1][:, :half], 2), swap(parts[2][:, half:], 1)]


def spread_end(arrays):
    half = arrays[0].shape[1] // 2
    spots = [(0, 0), (2, 0), (4, 0), (6, 0), (6, half)]
    return [(offset, low, array) for (offset, low), array in zip(spots, arrays)] + [
        (offset + 1, low, swap(array, 0)) for (offset, low), array in zip(spots, arrays)
    ]


def arrival_table(count):
    table = []
    for place in range(count):
        arrivals = []
        for step in range(1, count):
            if place - step >= 0:
                arrivals.append((2 * (step - 1), place - step))
            if place + step < count:
                arrivals.append((2 * (step - 1) + 1, place + step))
        table.append(arrivals)
    return table


def halo_of(key_value, reach):
    seq_count = lax.axis_size("seq")
    sent = []
    for distance in range(1, reach + 1):
        pairs = [(i, i + distance) for i in range(seq_count - distance)]
        sent.append(lax.ppermute(key_value, "seq", pairs))
    return sent


def halo_back(sections):
    seq_count = lax.axis_size("seq")
    back = []
    for section, array in enumerate(sections):
        distance = len(sections) - section
        pairs = [(i + distance, i) for i in range(seq_count - distance)]
        back.append(lax.ppermute(array, "seq", pairs))
    return back


def shards_general(tokens, dense, rope_rows, lowest, raw_queries, out_grad, w_key, w_value, reach):
    gain_row, q_row, k_row = dense
    cosine, sine = rope_rows
    tp_count = lax.axis_size("tp")
    place = lax.axis_index("tp").astype(jnp.int32)
    rows = tokens.shape[0]
    head_size = q_row.shape[1]
    kv_heads = w_key.shape[1] // head_size
    table = arrival_table(tp_count)
    picks = jnp.array(table, dtype=jnp.int32).reshape(tp_count, tp_count - 1, 2)
    picks = lax.dynamic_index_in_dim(picks, place, 0, keepdims=False)
    infos = [jnp.stack([jnp.int32(0), place])] + [picks[i] for i in range(tp_count - 1)]
    slot_places = jnp.concatenate([place[None], picks[:, 1]])
    normed_blocks, kv_blocks, raw_keys = [], [], []
    halo = [[] for _ in range(reach)]
    arrivals = []
    going_up = going_down = tokens
    for slot in range(tp_count):
        candidates = [tokens] if slot == 0 else list(arrivals)
        if slot < tp_count - 1:
            going_up = lax.ppermute(going_up, "tp", [(i, i + 1) for i in range(slot, tp_count - 1)])
            going_down = lax.ppermute(going_down, "tp", [(i + 1, i) for i in range(tp_count - 1 - slot)])
            arrivals += [going_up, going_down]
        key_value, keys, normed = project(infos[slot], candidates, gain_row, k_row, cosine, sine, w_key, w_value)
        normed_blocks.append(normed)
        kv_blocks.append(key_value)
        raw_keys.append((keys, 0))
        for distance, sent in enumerate(halo_of(key_value, reach)):
            halo[distance].append((sent, 0))
    blocks = [block for distance in range(reach, 0, -1) for block in halo[distance - 1]]
    blocks += [(block, 0) for block in kv_blocks]
    query_parts, kv_grads = [], []
    for head in range(kv_heads):
        outs = attend(head, kv_heads, reach, slot_places, lowest, q_row, cosine, sine, raw_queries, out_grad, blocks)
        query_parts.append(outs[0])
        back = halo_back(outs[2:])
        kv_grads += finish(head, slot_places, k_row, cosine, sine, outs[1], back, raw_keys)
    grad_queries = jnp.concatenate(query_parts, axis=1)
    partial_sum = input_terms(kv_grads, w_key, w_value, 0)
    summed_part = lax.psum_scatter(partial_sum, "tp", scatter_dimension=0, tiled=True)
    grad_x = input_grad(tokens, gain_row, [summed_part])
    left = jnp.concatenate(normed_blocks, axis=0)
    order = (slot_places[:, None] * rows + jnp.arange(rows, dtype=jnp.int32)[None, :]).reshape(-1)
    joined = [g[:, :head_size] for g in kv_grads] + [g[:, head_size:] for g in kv_grads]
    right = jnp.take(jnp.concatenate(joined, axis=1), order, axis=0)
    summed = lax.psum_scatter(dot_first(left, right), "seq", scatter_dimension=0, tiled=True)
    return (grad_x, grad_queries, summed[:, : w_key.shape[1]], summed[:, w_key.shape[1] :])


def trade(array, distance):
    return lax.ppermute(array, "tp", [(i, i ^ distance) for i in range(lax.axis_size("tp"))])


def shards_paired(tokens, dense, rope_rows, lowest, raw_queries, out_grad, w_key, w_value, reach, once):
    gain_row, q_row, k_row = dense
    cosine, sine = rope_rows
    seq_count = lax.axis_size("seq")
    seq_index = lax.axis_index("seq").astype(jnp.int32)
    place = lax.axis_index("tp").astype(jnp.int32)
    width, cols = w_key.shape
    head_size = q_row.shape[1]
    kv_heads = cols // head_size
    chunk = width // seq_count
    zero = jnp.zeros_like(place)
    slot_places = jnp.stack([place, place ^ 1, place ^ 2, place ^ 3])

    own_slice = jnp.concatenate(
        [lax.dynamic_slice_in_dim(weight, seq_index * chunk, chunk, 0) for weight in (w_key, w_value)], axis=1
    )
    distant = trade(after(tokens, own_slice), 2)

    partner_slice = trade(own_slice, 1)
    info = jnp.stack([zero, place])
    kv_0, keys_0, normed_0 = project(info, [tokens], gain_row, k_row, cosine, sine, w_key, w_value)
    halo_0 = halo_of(kv_0, reach)
    first_slice = after(partner_slice, (normed_0, halo_0))
    spread = [first_slice, swap(first_slice, 1), swap(first_slice, 2)]
    partner_normed_0 = trade(after(normed_0, partner_slice), 1)
    spread += spread_corners(spread)
    pieces = spread_end(spread)
    info = jnp.stack([seq_index, place, place ^ 2])
    far_block = after(distant, [piece for _, _, piece in pieces])
    kv_2, keys_2, normed_2, far_kv, far_keys = project_pair(
        info, normed_0, far_block, gain_row, k_row, cosine, sine, w_key, w_value, pieces
    )
    arrived_kv = trade(far_kv, 1)
    arrived_keys = trade(far_keys, 1)
    halo_2 = halo_of(kv_2, reach)
    arrived_kv = after(arrived_kv, (arrived_keys, partner_normed_0))
    halo_far = halo_of(arrived_kv, reach)
    partner_normed_2 = trade(after(normed_2, arrived_kv), 1)

    blocks = []
    for distance in range(reach, 0, -1):
        outer = halo_far[distance - 1]
        blocks += [(halo_0[distance - 1], 0), (outer, 0), (halo_2[distance - 1], 0), (outer, 1)]
    blocks += [(kv_0, 0), (arrived_kv, 0), (kv_2, 0), (arrived_kv, 1)]
    raw_keys = [(keys_0, 0), (arrived_keys, 0), (keys_2, 0), (arrived_keys, 1)]
    normed = [normed_0, partner_normed_0, normed_2, partner_normed_2]
    weight_info = jnp.concatenate([slot_places, (seq_index & 1)[None]])
    query_parts, kv_grads, arrived = [], [], []
    for head in range(kv_heads):
        outs = attend(head, kv_heads, reach, slot_places, lowest, q_row, cosine, sine, raw_queries, out_grad, blocks)
        query_parts.append(outs[0])
        back = halo_back(outs[2:])
        own = after(outs[1], arrived)
        grads, away = finish(head, slot_places, k_row, cosine, sine, own, back, raw_keys, trading=True)
        kv_grads.append(grads)
        arrived.append(trade(away, 1))
    grad_queries = jnp.concatenate(query_parts, axis=1)

    info = jnp.stack([seq_index, place, place ^ 2])
    away_terms, own_terms = pair_terms(info, kv_grads, arrived, pieces, w_key, w_value, kv_heads)
    other_terms = trade(away_terms, 2)

    def weight_step(step, _):
        parts = []
        for grads in kv_grads:
            send, keep = weight_terms(weight_info + step, grads, normed, chunk)
            keeps, comings = scatter_sum(send, keep)
            parts += [*keeps, *comings]
        return gather_heads(parts, kv_heads)

    empty = jnp.zeros((chunk, cols), jnp.float32)
    grad_wk, grad_wv = lax.fori_loop(0, after(once, away_terms), weight_step, (empty, empty))
    own_terms = after(own_terms, (grad_wk, grad_wv, grad_queries))
    grad_x = input_grad(tokens, gain_row, [own_terms, other_terms])
    return (grad_x, grad_queries, grad_wk, grad_wv)


def shards(tokens, in_gain, raw_queries, w_key, w_value, q_gain, k_gain, doc_lengths, out_grad):
    seq_count = lax.axis_size("seq")
    tp_count = lax.axis_size("tp")
    rows, width = tokens.shape
    shard_rows = rows * tp_count
    reach = (WINDOW - 2) // shard_rows + 1
    first_row = lax.axis_index("seq") * shard_rows
    positions = first_row + jnp.arange(shard_rows, dtype=jnp.int32)
    begins = doc_begin(doc_lengths, positions)
    rope_rows = rope_tables(positions - begins, q_gain.shape[0])
    lowest = jnp.maximum(begins, positions - (WINDOW - 1)) - (first_row - reach * shard_rows)
    dense = (in_gain[None, :], q_gain[None, :], k_gain[None, :])
    chunk = width // seq_count
    paired = (
        tp_count == 1 << 2
        and seq_count == 1 << 3
        and chunk % 16 == 0
        and width % math.lcm(2 * chunk, 128) == 0
    )
    args = (tokens, dense, rope_rows, lowest[None, :], raw_queries, out_grad, w_key, w_value, reach)
    return shards_paired(*args, jnp.minimum(doc_lengths[0], 1)) if paired else shards_general(*args)


def solution(mesh):
    placed = (
        P(("seq", "tp"), None),
        P(),
        P("seq", "tp"),
        P(None, "tp"),
        P(None, "tp"),
        P(),
        P(),
        P(),
        P("seq", "tp"),
    )
    return jax.shard_map(
        shards,
        mesh=mesh,
        in_specs=placed,
        out_specs=(P(("seq", "tp"), None), P("seq", "tp"), P("seq", "tp"), P("seq", "tp")),
        check_vma=False,
    )
```
